32 devices in a mesh: patch: 8 (over z, core), head: 4 (over y, x).
Axes of the slice: x: 2, y: 2, z: 4, core: 2. Of those that a mesh axis runs over, the one named last changes fastest.
Arguments:
- img_qkv: bfloat16 [2048, 9216], P(('patch', 'head')), may hold values from -8 to 8
- txt_qkv: bfloat16 [512, 9216], P('head'), may hold values from -8 to 8
- stale_kv: bfloat16 [2, 2048, 3072], P(None, 'patch', 'head'), may hold values from -8 to 8
- residual: bfloat16 [2048, 3072], P(('patch', 'head')), may hold values from -4 to 4
- gate_scale: float32 [3072], replicated, may hold values from 0.5 to 3
- proj_weight: bfloat16 [3072, 3072], replicated, may hold values from -0.109375 to 0.109375
Outputs:
- image_out: bfloat16 [2048, 3072], P(('patch', 'head'))
- text_attn: bfloat16 [512, 3072], P('head')
The draws below stay inside these ranges and needn't reach their ends.
All inputs are finite; a program needn't handle non-finite values.
Results may differ from the reference program's by a relative error of at most 0.0075.
Values may be sent and summed in bfloat16 or wider, within the bound.
No kernel may reach another device: no remote copies, remote signals or barrier semaphores. Data moves between devices by JAX's collectives and lax.ppermute only.
A program may use at most 192 MiB of HBM per device.

```python
import math
import jax
import jax.numpy as jnp
from jax import lax

H = 24
HD = 128
TXT = 512
D = 3072
GROUP = 256
IMG = 2048
N_PATCH = 8


def draw_rows(key, rows):
    row_width = H * HD
    base = jax.random.fold_in(key, 11)
    entries = jnp.clip(1.6 * jax.random.normal(base, (rows, 3 * row_width), jnp.float32), -8.0, 8.0)
    return entries


def draw_img_qkv(key, part):
    return draw_rows(key, IMG).astype(jnp.bfloat16)


def draw_txt_qkv(key, part):
    return draw_rows(key, TXT).astype(jnp.bfloat16)


def steps_of(own_key, shape, split, low, top_value):
    def one(axis_at, blocks):
        heights = jax.random.uniform(jax.random.fold_in(jax.random.fold_in(own_key, 6), axis_at), (blocks,), jnp.float32, low / len(split), top_value / len(split))
        return jnp.repeat(jnp.exp(heights), shape[axis_at] // blocks).reshape((-1,) + (1,) * (len(shape) - axis_at - 1))

    factor_of = one(*split[0])
    for cut in split[1:]:
        factor_of = factor_of * one(*cut)
    return factor_of


def gaussian(own_key, extent, spread, most, split=(), kind=jnp.bfloat16):
    gain = steps_of(own_key, extent, split, -0.22, 0.18) if split else 1.0
    values = jax.random.normal(own_key, extent, jnp.float32) * spread * gain
    return jnp.minimum(jnp.maximum(values, -most), most).astype(kind)


def setup_inputs(seed: int = 0) -> dict:
    splits = jax.random.split(jax.random.key(seed), 7)
    img_qkv = draw_img_qkv(jax.random.fold_in(splits[6], 71), 0)
    txt_qkv = draw_txt_qkv(jax.random.fold_in(splits[6], 71), 0)
    stale_kv = gaussian(splits[2], (2, IMG, D), 1.6, 8.0, ((1, 8), (2, 4)))
    residual = gaussian(splits[3], (IMG, D), 0.5, 4.0, ((0, 32),))
    gate_scale = jnp.clip(jnp.exp(jax.random.uniform(splits[4], (D,), jnp.float32, math.log(0.5), math.log(3.0))), 0.5, 3.0)
    proj_weight = gaussian(splits[5], (D, D), D ** -0.5, 0.109375)
    return {"img_qkv": img_qkv, "txt_qkv": txt_qkv, "stale_kv": stale_kv, "residual": residual, "gate_scale": gate_scale, "proj_weight": proj_weight}


def attend_head(queries, key_rows, values):
    scores = jnp.dot(queries, key_rows.T, preferred_element_type=jnp.float32) * (1.0 / math.sqrt(HD))
    row_max = lax.optimization_barrier(jnp.max(scores, axis=1, keepdims=True))
    shifted = jnp.exp(scores - row_max)
    row_sum = lax.optimization_barrier(jnp.sum(shifted, axis=1, keepdims=True))
    weights = shifted.astype(jnp.bfloat16)
    mixed_rows = jnp.dot(weights, values, preferred_element_type=jnp.float32)
    return (mixed_rows / row_sum).astype(jnp.bfloat16)

def attend_heads(queries, key_rows, values):
    moved = (jnp.moveaxis(queries, 1, 0), jnp.moveaxis(key_rows, 1, 0), jnp.moveaxis(values, 1, 0))
    result = lax.map(lambda triple: attend_head(triple[0], triple[1], triple[2]), moved)
    return jnp.moveaxis(result, 0, 1)

def reference(img_qkv, txt_qkv, stale_kv, residual, gate_scale, proj_weight):
    img_parts = img_qkv.reshape(IMG, 3, H, HD)
    txt_parts = txt_qkv.reshape(TXT, 3, H, HD)
    stale_keys = stale_kv[0].reshape(IMG, H, HD)
    stale_values = stale_kv[1].reshape(IMG, H, HD)
    text_keys = txt_parts[:, 1]
    text_values = txt_parts[:, 2]

    def one_group(group_index):
        first_row = (group_index * GROUP).astype(jnp.int32)
        fresh_keys = lax.dynamic_slice_in_dim(img_parts[:, 1], first_row, GROUP, 0)
        fresh_values = lax.dynamic_slice_in_dim(img_parts[:, 2], first_row, GROUP, 0)
        group_keys = lax.dynamic_update_slice_in_dim(stale_keys, fresh_keys, first_row, 0)
        group_values = lax.dynamic_update_slice_in_dim(stale_values, fresh_values, first_row, 0)
        queries = lax.dynamic_slice_in_dim(img_parts[:, 0], first_row, GROUP, 0)
        return attend_heads(queries, jnp.concatenate([text_keys, group_keys], axis=0), jnp.concatenate([text_values, group_values], axis=0))
    image_attn = lax.map(one_group, jnp.arange(N_PATCH, dtype=jnp.int32)).reshape(IMG, D)
    text_attn = attend_heads(txt_parts[:, 0], jnp.concatenate([text_keys, stale_keys], axis=0), jnp.concatenate([text_values, stale_values], axis=0)).reshape(TXT, D)
    projected = jnp.dot(image_attn, proj_weight, preferred_element_type=jnp.float32)
    image_out = (residual.astype(jnp.float32) + gate_scale * projected).astype(jnp.bfloat16)
    return (image_out, text_attn)
```

```python
import functools
import math

import jax
import jax.numpy as jnp
from jax import lax
from jax.experimental import pallas as pl
from jax.experimental.pallas import tpu as pltpu
from jax.sharding import PartitionSpec as P

HD = 128
SCALE = math.log2(math.e) / math.sqrt(HD)
VMEM_LIMIT = 40 * 1024 * 1024
TILE = 256


def params(steps=1):
    return pltpu.CompilerParams(
        vmem_limit_bytes=VMEM_LIMIT, dimension_semantics=("arbitrary",) * steps
    )


def dot(first, second, contract):
    return lax.dot_general(
        first, second, ((contract[:1], contract[1:]), ((), ())), preferred_element_type=jnp.float32
    )


def scaled_scores(key_rows, queries):
    return dot(key_rows, queries, (1, 1)) * SCALE


def weigh(scores, values, row_max):
    weights = jnp.exp2(scores - row_max)
    row_sum = jnp.sum(weights, axis=0, keepdims=True)
    return row_sum, dot(values, weights.astype(jnp.bfloat16), (0, 0))


def tiles_of(rows):
    tile = min(TILE, rows)
    return [(first, min(tile, rows - first)) for first in range(0, rows, tile)]


def pack_body(_, *refs):
    sources, packed = refs[:-1], refs[-1]
    for part, source in enumerate(sources):
        width = source.shape[1]
        packed[0, :, part * width : (part + 1) * width] = source[...]


def pack(rows_array, row_block, rows, destinations, column_block, width):
    blocks = rows_array.shape[1] // 3 // width

    def source(part):
        return pl.BlockSpec(
            (rows, width), lambda d, info: (info[0], part * blocks + column_block(d))
        )

    return pl.pallas_call(
        pack_body,
        grid_spec=pltpu.PrefetchScalarGridSpec(
            num_scalar_prefetch=1,
            grid=(destinations,),
            in_specs=[source(0), source(1), source(2)],
            out_specs=pl.BlockSpec((1, rows, 3 * width), lambda d, info: (d, 0, 0)),
        ),
        out_shape=jax.ShapeDtypeStruct((destinations, rows, 3 * width), rows_array.dtype),
        compiler_params=params(),
        name="pack_heads",
    )(row_block, rows_array, rows_array, rows_array)


def first_body(pair, info, *refs):
    q_img, k_img, v_img, q_txt, k_txt, v_txt = refs[:6]
    stale = refs[6 : 6 + pair]
    acc_img, stat_img, acc_txt, stat_txt = refs[6 + pair :]
    core = info[0]
    group_rows = q_img.shape[0] // pair
    text_keys, text_values = k_txt[...], v_txt[...]

    def store(queries, key_rows, values, acc, stat, first, count):
        scores = scaled_scores(key_rows, queries)
        row_max = jnp.max(scores, axis=0, keepdims=True)
        row_sum, mixed = weigh(scores, values, row_max)
        acc[0, :, first : first + count] = mixed
        stat[0, 0:1, first : first + count] = row_max
        stat[0, 1:2, first : first + count] = row_sum

    for group in range(pair):
        key_rows = [text_keys, k_img[group * group_rows : (group + 1) * group_rows, :]]
        values = [text_values, v_img[group * group_rows : (group + 1) * group_rows, :]]
        if pair == 2:
            mine = core == group
            key_rows.append(jnp.where(mine, stale[1][0], stale[0][0]))
            values.append(jnp.where(mine, stale[1][1], stale[0][1]))
        key_rows, values = jnp.concatenate(key_rows, 0), jnp.concatenate(values, 0)
        for first, count in tiles_of(group_rows):
            first = first + group * group_rows
            store(q_img[first : first + count, :], key_rows, values, acc_img, stat_img, first, count)
    key_rows = jnp.concatenate([text_keys] + [block[0] for block in stale], 0)
    values = jnp.concatenate([text_values] + [block[1] for block in stale], 0)
    for first, count in tiles_of(q_txt.shape[0]):
        store(q_txt[first : first + count, :], key_rows, values, acc_txt, stat_txt, first, count)


def column_spec(rows, offset):
    return pl.BlockSpec((rows, HD), lambda h, info: (0, offset + h))


def block_spec(block):
    return pl.BlockSpec((2, block.shape[1], HD), lambda h, info: (0, 0, h))


def state_shapes(heads, rows):
    return [
        jax.ShapeDtypeStruct((heads, HD, rows), jnp.float32),
        jax.ShapeDtypeStruct((heads, 8, rows), jnp.float32),
    ]


def state_specs(rows):
    return [
        pl.BlockSpec((1, HD, rows), lambda h, info: (h, 0, 0)),
        pl.BlockSpec((1, 8, rows), lambda h, info: (h, 0, 0)),
    ]


def attend_cost(queries, keys, heads):
    return pl.CostEstimate(
        flops=4 * queries * keys * heads * HD,
        bytes_accessed=4 * queries * heads * HD + 4 * keys * heads * HD,
        transcendentals=queries * keys * heads,
    )


def attend_first(info, img, txt, stale):
    heads = img.shape[1] // (3 * HD)
    rows, text_rows = img.shape[0], txt.shape[0]
    return pl.pallas_call(
        functools.partial(first_body, len(stale)),
        grid_spec=pltpu.PrefetchScalarGridSpec(
            num_scalar_prefetch=1,
            grid=(heads,),
            in_specs=[column_spec(rows, part * heads) for part in range(3)]
            + [column_spec(text_rows, part * heads) for part in range(3)]
            + [block_spec(block) for block in stale],
            out_specs=state_specs(rows) + state_specs(text_rows),
        ),
        out_shape=state_shapes(heads, rows) + state_shapes(heads, text_rows),
        compiler_params=params(),
        cost_estimate=attend_cost(rows + text_rows, 1024, heads),
        name="attend_own",
    )(info, img, img, img, txt, txt, txt, *stale)


def step_body(sets, per_side, final, info, *refs):
    refs = list(refs)
    sources = [refs[3 * i : 3 * i + 3] for i in range(sets)]
    blocks = refs[3 * sets : 3 * sets + 2 * per_side]
    rest = refs[3 * sets + 2 * per_side :]
    if final:
        outputs, scratch = rest[:sets], rest[sets:]
        states = [scratch[2 * i : 2 * i + 2] for i in range(sets)]
    else:
        states = [rest[2 * i : 2 * i + 2] for i in range(sets)]
    for (_, acc_in, stat_in), (acc, stat) in zip(sources, states):
        acc[...] = acc_in[...]
        stat[...] = stat_in[...]
    for side in range(2):
        mine = blocks[side * per_side : (side + 1) * per_side]

        @pl.when(info[1 + side] == 1)
        def _():
            key_rows = jnp.concatenate([block[0] for block in mine], 0)
            values = jnp.concatenate([block[1] for block in mine], 0)
            for (queries, _, _), (acc, stat) in zip(sources, states):
                for first, count in tiles_of(queries.shape[0]):
                    span = slice(first, first + count)
                    scores = scaled_scores(key_rows, queries[span, :])
                    old_max = stat[0, 0:1, span]
                    row_max = jnp.maximum(old_max, jnp.max(scores, axis=0, keepdims=True))
                    row_sum, mixed = weigh(scores, values, row_max)
                    keep = jnp.exp2(old_max - row_max)
                    acc[0, :, span] = acc[0, :, span] * keep + mixed
                    stat[0, 1:2, span] = stat[0, 1:2, span] * keep + row_sum
                    stat[0, 0:1, span] = row_max

    if final:
        for output, (acc, stat) in zip(outputs, states):
            for first, count in tiles_of(output.shape[0]):
                span = slice(first, first + count)
                output[span, :] = (acc[0, :, span] / stat[0, 1:2, span]).T.astype(output.dtype)


def attend_step(info, sources, left, right, final):
    heads = sources[0][0].shape[1] // (3 * HD)
    operands, in_specs, out_specs, out_shape, scratch = [], [], [], [], []
    for qkv, acc, stat in sources:
        rows = qkv.shape[0]
        operands += [qkv, acc, stat]
        in_specs += [column_spec(rows, 0)] + state_specs(rows)
        if final:
            out_specs.append(column_spec(rows, 0))
            out_shape.append(jax.ShapeDtypeStruct((rows, heads * HD), jnp.bfloat16))
            scratch += [pltpu.VMEM((1, HD, rows), jnp.float32), pltpu.VMEM((1, 8, rows), jnp.float32)]
        else:
            out_specs += state_specs(rows)
            out_shape += state_shapes(heads, rows)
    blocks = list(left) + list(right)
    total = sum(qkv.shape[0] for qkv, _, _ in sources)
    keys = sum(block.shape[1] for block in left)
    return pl.pallas_call(
        functools.partial(step_body, len(sources), len(left), final),
        grid_spec=pltpu.PrefetchScalarGridSpec(
            num_scalar_prefetch=1,
            grid=(heads,),
            in_specs=in_specs + [block_spec(block) for block in blocks],
            out_specs=out_specs,
            scratch_shapes=scratch,
        ),
        out_shape=out_shape,
        compiler_params=params(),
        cost_estimate=attend_cost(total, keys, heads),
        name="attend_last" if final else "attend_arrived",
    )(info, *operands, *blocks)


def project_body(order, x_ref, weight, residual, gate, out, flat):
    @pl.when(pl.program_id(0) == 0)
    def _():
        width = x_ref.shape[2]
        for source, place in enumerate(order):
            flat[:, place * width : (place + 1) * width] = x_ref[source]

    projected = jnp.dot(flat[...], weight[...], preferred_element_type=jnp.float32)
    out[...] = (residual[...].astype(jnp.float32) + gate[...] * projected).astype(out.dtype)


def project(x, order, weight, residual, gate):
    rows, model = residual.shape
    columns = 512 if model % 512 == 0 else HD
    return pl.pallas_call(
        functools.partial(project_body, order),
        grid=(model // columns,),
        in_specs=[
            pl.BlockSpec(x.shape, lambda n: (0, 0, 0)),
            pl.BlockSpec((weight.shape[0], columns), lambda n: (0, n)),
            pl.BlockSpec((rows, columns), lambda n: (0, n)),
            pl.BlockSpec((1, columns), lambda n: (0, n)),
        ],
        out_specs=pl.BlockSpec((rows, columns), lambda n: (0, n)),
        out_shape=jax.ShapeDtypeStruct((rows, model), residual.dtype),
        scratch_shapes=[pltpu.VMEM((rows, weight.shape[0]), x.dtype)],
        compiler_params=params(),
        cost_estimate=pl.CostEstimate(
            flops=2 * rows * model * model, bytes_accessed=2 * model * model, transcendentals=0
        ),
        name="project",
    )(x, weight, residual, gate.reshape(1, model))


def per_device(img_qkv, txt_qkv, stale_kv, residual, gate_scale, proj_weight):
    patches, head_owners = lax.axis_size("patch"), lax.axis_size("head")
    patch, owner = lax.axis_index("patch"), lax.axis_index("head")
    model = img_qkv.shape[1] // 3
    owned_heads = stale_kv.shape[2] // HD
    pair = 2 if patches % 2 == 0 and owned_heads % 2 == 0 else 1
    planes = patches // pair
    plane, core = patch // pair, patch % pair
    width = stale_kv.shape[2] // pair
    img_rows = img_qkv.shape[0]
    text_rows = txt_qkv.shape[0] // pair
    destinations = pair * head_owners
    order = [(d % head_owners) * pair + d // head_owners for d in range(destinations)]

    def column_block(d):
        return (d % head_owners) * pair + d // head_owners

    groups = [[g * destinations + d for d in range(destinations)] for g in range(planes)]

    def exchange(x):
        return lax.all_to_all(
            x, ("patch", "head"), split_axis=0, concat_axis=0, axis_index_groups=groups, tiled=True
        )

    swap_pairs = [(p, p + 1 - 2 * (p % 2)) for p in range(patches)]
    mine = lax.dynamic_slice_in_dim(stale_kv, core * width, width, 2)
    stale = [mine]
    if pair == 2:
        theirs = lax.dynamic_slice_in_dim(stale_kv, (1 - core) * width, width, 2)
        stale.append(lax.ppermute(theirs, "patch", swap_pairs))

    zero = jnp.zeros((), jnp.int32)
    img = exchange(
        pack(img_qkv, zero.reshape(1), img_rows, destinations, column_block, width)
    ).reshape(destinations * img_rows, 3 * width)
    txt = exchange(
        pack(txt_qkv, core.astype(jnp.int32).reshape(1), text_rows, destinations, column_block, width)
    ).reshape(destinations * text_rows, 3 * width)

    info = jnp.stack([core, zero, zero]).astype(jnp.int32)
    state = attend_first(info, img, txt, stale)
    from_left, from_right = stale, stale
    for step in range(1, planes):
        right_pairs = [(p, p + pair) for p in range((step - 1) * pair, patches - pair)]
        left_pairs = [(q, p) for p, q in right_pairs]
        left_pairs = [(p + pair, p) for p in range(0, patches - step * pair)]
        from_left = [lax.ppermute(block, "patch", right_pairs) for block in from_left]
        from_right = [lax.ppermute(block, "patch", left_pairs) for block in from_right]
        info = jnp.stack([core, plane >= step, plane + step < planes]).astype(jnp.int32)
        img_source = (img, state[0], state[1])
        txt_source = (txt, state[2], state[3])
        if step < planes - 1:
            state = attend_step(info, [img_source, txt_source], from_left, from_right, False)
        else:
            (image_attn,) = attend_step(info, [img_source], from_left, from_right, True)
            (text_attn,) = attend_step(info, [txt_source], from_left, from_right, True)

    image_back = exchange(image_attn.reshape(destinations, img_rows, width))
    image_out = project(image_back, order, proj_weight, residual, gate_scale)

    text_back = exchange(text_attn.reshape(destinations, text_rows, width))
    text_out = (
        text_back.reshape(pair, head_owners, text_rows, width)
        .transpose(2, 1, 0, 3)
        .reshape(text_rows, model)
    )
    if pair == 2:
        other = lax.ppermute(text_out, "patch", swap_pairs)
        lower = core == 0
        text_out = jnp.concatenate(
            [jnp.where(lower, text_out, other), jnp.where(lower, other, text_out)], 0
        )
    return (image_out, text_out)


def solution(mesh):
    return jax.shard_map(
        per_device,
        mesh=mesh,
        in_specs=(
            P(("patch", "head"), None),
            P("head", None),
            P(None, "patch", "head"),
            P(("patch", "head"), None),
            P(),
            P(),
        ),
        out_specs=(P(("patch", "head"), None), P("head", None)),
        check_vma=False,
    )
```

```python
import functools
import math

import jax
import jax.numpy as jnp
from jax import lax
from jax.experimental import pallas as pl
from jax.experimental.pallas import tpu as pltpu
from jax.sharding import PartitionSpec as P

HD = 128
SCALE = math.log2(math.e) / math.sqrt(HD)
VMEM_LIMIT = 24 * 1024 * 1024
TILE = 256
LARGE = 2.0**60


def params():
    return pltpu.CompilerParams(
        vmem_limit_bytes=VMEM_LIMIT, dimension_semantics=("arbitrary",)
    )


def pack_body(info, *refs):
    sources, packed = refs[:6], refs[-1]
    first = 0
    for group in (sources[:3], sources[3:]):
        rows, width = group[0].shape
        for part, source in enumerate(group):
            packed[0, first : first + rows, part * width : (part + 1) * width] = source[...]
        first += rows


def pack(core, img_qkv, txt_qkv, text_rows, destinations, column_block, width, after):
    img_rows = img_qkv.shape[0]
    blocks = img_qkv.shape[1] // 3 // width

    def source(rows, part, by_core):
        def place(d, info):
            return (info[0] if by_core else 0, part * blocks + column_block(d))

        return pl.BlockSpec((rows, width), place)

    return pl.pallas_call(
        pack_body,
        grid_spec=pltpu.PrefetchScalarGridSpec(
            num_scalar_prefetch=1,
            grid=(destinations,),
            in_specs=[source(img_rows, part, False) for part in range(3)]
            + [source(text_rows, part, True) for part in range(3)]
            + [pl.BlockSpec(memory_space=pl.ANY)] * len(after),
            out_specs=pl.BlockSpec(
                (1, img_rows + text_rows, 3 * width), lambda d, info: (d, 0, 0)
            ),
        ),
        out_shape=jax.ShapeDtypeStruct(
            (destinations, img_rows + text_rows, 3 * width), img_qkv.dtype
        ),
        compiler_params=params(),
        name="pack_heads",
    )(core, img_qkv, img_qkv, img_qkv, txt_qkv, txt_qkv, txt_qkv, *after)


def dot(first, second, contract):
    return lax.dot_general(
        first, second, ((contract[:1], contract[1:]), ((), ())), preferred_element_type=jnp.float32
    )


def with_ones(block):
    return jnp.concatenate([block, jnp.ones_like(block)], axis=1)


def reference_columns(row_max):
    reference = row_max.astype(jnp.bfloat16).astype(jnp.float32)
    return jnp.broadcast_to(reference * (-1.0 / HD), (row_max.shape[0], HD)).astype(jnp.bfloat16)


def weighted(queries, key_rows, values):
    weights = jnp.exp2(dot(queries, key_rows, (1, 1)) * SCALE).astype(jnp.bfloat16)
    return dot(weights, values, (1, 0))


def tiles_of(rows):
    tile = min(TILE, rows)
    return [slice(first, min(first + tile, rows)) for first in range(0, rows, tile)]


def split_rows(block, img_rows):
    return (
        block[:, :img_rows, :].reshape(-1, HD),
        block[:, img_rows:, :].reshape(-1, HD),
    )


def until_small(flag, total, attempt):
    flag[0] = 1

    @pl.loop(0, 2)
    def _(turn):
        @pl.when(flag[0] == 1)
        def _():
            attempt(turn)
            flag[0] = jnp.where(jnp.max(total[0, :, HD:]) > LARGE, 1, 0).astype(jnp.int32)


def most_body(pair, img_rows, sides, info, *refs):
    q_ref, k_ref, v_ref = refs[:3]
    stale = refs[3 : 3 + pair]
    arrived = refs[3 + pair : 3 + pair + sides * pair]
    aug, total, flag = refs[3 + pair + sides * pair :]
    core = info[0]
    k_img, k_txt = split_rows(k_ref[...], img_rows)
    v_img, v_txt = split_rows(v_ref[...], img_rows)
    q_img, q_txt = split_rows(q_ref[...], img_rows)
    fresh_rows = q_img.shape[0]
    group_rows = fresh_rows // pair
    rows = fresh_rows + q_txt.shape[0]

    def queries_at(span):
        if span.stop <= fresh_rows:
            return q_img[span, :]
        return q_txt[span.start - fresh_rows : span.stop - fresh_rows, :]

    def own_sets():
        sets = []
        for group in range(pair):
            span = slice(group * group_rows, (group + 1) * group_rows)
            key_rows, values = [k_txt, k_img[span, :]], [v_txt, v_img[span, :]]
            if pair == 2:
                mine = core == group
                key_rows.append(jnp.where(mine, stale[1][0], stale[0][0]))
                values.append(jnp.where(mine, stale[1][1], stale[0][1]))
            sets.append((span, key_rows, values))
        sets.append(
            (
                slice(fresh_rows, rows),
                [k_txt] + [block[0] for block in stale],
                [v_txt] + [block[1] for block in stale],
            )
        )
        for span, key_rows, values in sets:
            key_rows, values = jnp.concatenate(key_rows, 0), jnp.concatenate(values, 0)
            spans = [
                slice(span.start + t.start, span.start + t.stop)
                for t in tiles_of(span.stop - span.start)
            ]
            yield spans, key_rows, values

    def each_arrived(act):
        for side in range(sides):
            blocks = arrived[side * pair : (side + 1) * pair]

            @pl.when(info[1 + side] == 1)
            def _():
                key_rows = jnp.concatenate([block[0] for block in blocks], 0)
                values = jnp.concatenate([block[1] for block in blocks], 0)
                for first in range(0, rows, fresh_rows):
                    for tile in tiles_of(min(fresh_rows, rows - first)):
                        act(slice(first + tile.start, first + tile.stop), key_rows, values)

    def largest(span, key_rows):
        return jnp.max(dot(queries_at(span), key_rows, (1, 1)), axis=1, keepdims=True)

    def attempt(turn):
        @pl.when(turn == 0)
        def _():
            for spans, key_rows, _ in own_sets():
                for span in spans:
                    aug[0, span, :] = reference_columns(
                        largest(span, key_rows[: min(256, key_rows.shape[0]), :])
                    )

        @pl.when(turn == 1)
        def _():
            def raise_to(span, key_rows, _):
                total[0, span, :] = jnp.maximum(
                    total[0, span, :], jnp.broadcast_to(largest(span, key_rows), total[0, span, :].shape)
                )

            for spans, key_rows, _ in own_sets():
                for span in spans:
                    total[0, span, :] = jnp.broadcast_to(
                        largest(span, key_rows), total[0, span, :].shape
                    )
            each_arrived(raise_to)
            for spans, _, _ in own_sets():
                for span in spans:
                    aug[0, span, :] = reference_columns(total[0, span, :1])

        def queries_of(span):
            return jnp.concatenate([queries_at(span), aug[0, span, :]], axis=1)

        def add(span, key_rows, values):
            total[0, span, :] += weighted(queries_of(span), with_ones(key_rows), with_ones(values))

        for spans, key_rows, values in own_sets():
            key_rows, values = with_ones(key_rows), with_ones(values)
            for span in spans:
                total[0, span, :] = weighted(queries_of(span), key_rows, values)
        each_arrived(add)

    until_small(flag, total, attempt)


def column_spec(array, offset):
    return pl.BlockSpec(array.shape[:2] + (HD,), lambda h, info: (0, 0, offset + h))


def head_spec(shape):
    return pl.BlockSpec((1,) + shape[1:], lambda h, info: (h, 0, 0))


def attend_cost(queries, keys, heads):
    return pl.CostEstimate(
        flops=4 * queries * keys * heads * HD,
        bytes_accessed=4 * queries * heads * HD + 4 * keys * heads * HD,
        transcendentals=queries * keys * heads,
    )


def attend_most(info, qkv, img_rows, stale, arrived):
    heads = qkv.shape[2] // (3 * HD)
    rows = qkv.shape[0] * qkv.shape[1]
    blocks = list(stale) + [block for side in arrived for block in side]
    shapes = [
        jax.ShapeDtypeStruct((heads, rows, HD), jnp.bfloat16),
        jax.ShapeDtypeStruct((heads, rows, 2 * HD), jnp.float32),
    ]
    keys = sum(block.shape[1] for block in blocks) // 2 + rows // 2
    return pl.pallas_call(
        functools.partial(most_body, len(stale), img_rows, len(arrived)),
        grid_spec=pltpu.PrefetchScalarGridSpec(
            num_scalar_prefetch=1,
            grid=(heads,),
            in_specs=[column_spec(qkv, part * heads) for part in range(3)]
            + [column_spec(block, 0) for block in blocks],
            out_specs=[head_spec(shape.shape) for shape in shapes],
            scratch_shapes=[pltpu.SMEM((1,), jnp.int32)],
        ),
        out_shape=shapes,
        compiler_params=params(),
        cost_estimate=attend_cost(rows, keys, heads),
        name="attend_most",
    )(info, qkv, qkv, qkv, *blocks)


def last_body(pair, img_rows, sides, info, *refs):
    q_ref, aug_ref, total_ref = refs[:3]
    arrived = refs[3 : 3 + sides * pair]
    out, total, shift, flag = refs[3 + sides * pair :]
    q_img, q_txt = split_rows(q_ref[...], img_rows)
    fresh_rows = q_img.shape[0]
    rows = total.shape[1]

    def queries_at(span):
        if span.stop <= fresh_rows:
            queries = q_img[span, :]
        else:
            queries = q_txt[span.start - fresh_rows : span.stop - fresh_rows, :]
        return jnp.concatenate([queries, aug_ref[0, span, :]], axis=1)

    def each_arrived(act):
        for side in range(sides):
            blocks = arrived[side * pair : (side + 1) * pair]

            @pl.when(info[1 + side] == 1)
            def _():
                key_rows = with_ones(jnp.concatenate([block[0] for block in blocks], 0))
                values = with_ones(jnp.concatenate([block[1] for block in blocks], 0))
                for first, last in ((0, fresh_rows), (fresh_rows, rows)):
                    for tile in tiles_of(last - first):
                        act(slice(first + tile.start, first + tile.stop), key_rows, values)

    def add(span, key_rows, values):
        total[0, span, :] += weighted(queries_at(span), key_rows, values)

    def raise_to(span, key_rows, _):
        above = jnp.max(dot(queries_at(span), key_rows, (1, 1)), axis=1, keepdims=True)
        shift[span, :] = jnp.maximum(shift[span, :], jnp.broadcast_to(above, shift[span, :].shape))

    def add_shifted(span, key_rows, values):
        scores = dot(queries_at(span), key_rows, (1, 1)) - shift[span, :1]
        total[0, span, :] += dot(jnp.exp2(scores * SCALE).astype(jnp.bfloat16), values, (1, 0))

    def attempt(turn):
        @pl.when(turn == 0)
        def _():
            total[...] = total_ref[...]
            each_arrived(add)

        @pl.when(turn == 1)
        def _():
            shift[...] = jnp.zeros_like(shift)
            each_arrived(raise_to)
            keep = jnp.exp2(shift[...] * -SCALE)
            total[0] = total_ref[0] * jnp.concatenate([keep, keep], axis=1)
            each_arrived(add_shifted)

    until_small(flag, total, attempt)
    attended = (total[0, :, :HD] / total[0, :, HD:]).astype(out.dtype)
    destinations = out.shape[0]
    out[:, :img_rows, :] = attended[:fresh_rows].reshape(destinations, img_rows, HD)
    out[:, img_rows:, :] = attended[fresh_rows:].reshape(destinations, -1, HD)


def attend_last(info, qkv, img_rows, state, arrived):
    heads = qkv.shape[2] // (3 * HD)
    rows = qkv.shape[0] * qkv.shape[1]
    blocks = [block for side in arrived for block in side]
    return pl.pallas_call(
        functools.partial(last_body, len(arrived[0]), img_rows, len(arrived)),
        grid_spec=pltpu.PrefetchScalarGridSpec(
            num_scalar_prefetch=1,
            grid=(heads,),
            in_specs=[column_spec(qkv, 0)]
            + [head_spec(part.shape) for part in state]
            + [column_spec(block, 0) for block in blocks],
            out_specs=pl.BlockSpec(qkv.shape[:2] + (HD,), lambda h, info: (0, 0, h)),
            scratch_shapes=[
                pltpu.VMEM((1, rows, 2 * HD), jnp.float32),
                pltpu.VMEM((rows, HD), jnp.float32),
                pltpu.SMEM((1,), jnp.int32),
            ],
        ),
        out_shape=jax.ShapeDtypeStruct(qkv.shape[:2] + (heads * HD,), qkv.dtype),
        compiler_params=params(),
        cost_estimate=attend_cost(rows, blocks[0].shape[1] * len(arrived[0]), heads),
        name="attend_last",
    )(info, qkv, *state, *blocks)


def project_body(order, x_ref, weight, residual, gate, out, flat):
    @pl.when(pl.program_id(0) == 0)
    def _():
        rows, width = flat.shape[0], x_ref.shape[2]
        for source, place in enumerate(order):
            flat[:, place * width : (place + 1) * width] = x_ref[source, :rows, :]

    projected = jnp.dot(flat[...], weight[...], preferred_element_type=jnp.float32)
    out[...] = (residual[...].astype(jnp.float32) + gate[...] * projected).astype(out.dtype)


def project(x, order, weight, residual, gate):
    rows, model = residual.shape
    columns = 512 if model % 512 == 0 else HD
    return pl.pallas_call(
        functools.partial(project_body, order),
        grid=(model // columns,),
        in_specs=[
            pl.BlockSpec(x.shape, lambda n: (0, 0, 0)),
            pl.BlockSpec((weight.shape[0], columns), lambda n: (0, n)),
            pl.BlockSpec((rows, columns), lambda n: (0, n)),
            pl.BlockSpec((1, columns), lambda n: (0, n)),
        ],
        out_specs=pl.BlockSpec((rows, columns), lambda n: (0, n)),
        out_shape=jax.ShapeDtypeStruct((rows, model), residual.dtype),
        scratch_shapes=[pltpu.VMEM((rows, weight.shape[0]), x.dtype)],
        compiler_params=params(),
        cost_estimate=pl.CostEstimate(
            flops=2 * rows * model * model, bytes_accessed=2 * model * model, transcendentals=0
        ),
        name="project",
    )(x, weight, residual, gate.reshape(1, model))


def unpack_body(order, first, x_ref, out):
    width = x_ref.shape[2]
    for source, place in enumerate(order):
        out[:, place * width : (place + 1) * width] = x_ref[source, first:, :]


def unpack_text(x, order, first):
    model = x.shape[0] * x.shape[2]
    return pl.pallas_call(
        functools.partial(unpack_body, order, first),
        grid=(1,),
        in_specs=[pl.BlockSpec(x.shape, lambda n: (0, 0, 0))],
        out_specs=pl.BlockSpec((x.shape[1] - first, model), lambda n: (0, 0)),
        out_shape=jax.ShapeDtypeStruct((x.shape[1] - first, model), x.dtype),
        compiler_params=params(),
        name="unpack_text",
    )(x)


def per_device(img_qkv, txt_qkv, stale_kv, residual, gate_scale, proj_weight):
    patches, head_owners = lax.axis_size("patch"), lax.axis_size("head")
    patch = lax.axis_index("patch")
    owned_heads = stale_kv.shape[2] // HD
    pair = 2 if patches % 2 == 0 and owned_heads % 2 == 0 else 1
    planes = patches // pair
    plane, core = patch // pair, patch % pair
    width = stale_kv.shape[2] // pair
    img_rows = img_qkv.shape[0]
    text_rows = txt_qkv.shape[0] // pair
    destinations = pair * head_owners

    def column_block(d):
        return (d % head_owners) * pair + d // head_owners

    order = [column_block(d) for d in range(destinations)]
    groups = [[g * destinations + d for d in range(destinations)] for g in range(planes)]

    def exchange(x):
        return lax.all_to_all(
            x, ("patch", "head"), split_axis=0, concat_axis=0, axis_index_groups=groups, tiled=True
        )

    swap_pairs = [(p, p + 1 - 2 * (p % 2)) for p in range(patches)]
    stale = [lax.dynamic_slice_in_dim(stale_kv, core * width, width, 2)]
    if pair == 2:
        theirs = lax.dynamic_slice_in_dim(stale_kv, (1 - core) * width, width, 2)
        stale.append(lax.ppermute(theirs, "patch", swap_pairs))

    core_only = core.astype(jnp.int32).reshape(1)
    qkv = exchange(
        pack(core_only, img_qkv, txt_qkv, text_rows, destinations, column_block, width, stale[1:])
    )

    arrived, valid = [], []
    from_left, from_right = stale, stale
    for step in range(1, planes):
        right_pairs = [(p, p + pair) for p in range((step - 1) * pair, patches - pair)]
        left_pairs = [(p + pair, p) for p in range(0, patches - step * pair)]
        from_left = [lax.ppermute(block, "patch", right_pairs) for block in from_left]
        from_right = [lax.ppermute(block, "patch", left_pairs) for block in from_right]
        arrived += [from_left, from_right]
        valid += [plane >= step, plane + step < planes]
    early = max(0, len(arrived) - 2)
    info = jnp.stack([core] + valid[:early]).astype(jnp.int32)
    last_info = jnp.stack([core] + valid[early:]).astype(jnp.int32)
    state = attend_most(info, qkv, img_rows, stale, arrived[:early])
    attended = attend_last(last_info, qkv, img_rows, state, arrived[early:])

    back = exchange(attended)
    text_out = unpack_text(back, order, img_rows)
    if pair == 2:
        other = lax.ppermute(text_out, "patch", swap_pairs)
        lower = core == 0
        text_out = jnp.concatenate(
            [jnp.where(lower, text_out, other), jnp.where(lower, other, text_out)], 0
        )
    image_out = project(back, order, proj_weight, residual, gate_scale)
    return (image_out, text_out)


def solution(mesh):
    return jax.shard_map(
        per_device,
        mesh=mesh,
        in_specs=(
            P(("patch", "head"), None),
            P("head", None),
            P(None, "patch", "head"),
            P(("patch", "head"), None),
            P(),
            P(),
        ),
        out_specs=(P(("patch", "head"), None), P("head", None)),
        check_vma=False,
    )
```

```python
import functools
import math

import jax
import jax.numpy as jnp
from jax import lax
from jax.experimental import pallas as pl
from jax.experimental.pallas import tpu as pltpu
from jax.sharding import PartitionSpec as P

HD = 128
SCALE = math.log2(math.e) / math.sqrt(HD)
VMEM_LIMIT = 24 * 1024 * 1024
TILE = 256
LARGE = 2.0**60


def params():
    return pltpu.CompilerParams(
        vmem_limit_bytes=VMEM_LIMIT, dimension_semantics=("arbitrary",)
    )


def pack_body(info, *refs):
    sources, packed = refs[:6], refs[-1]
    first = 0
    for group in (sources[:3], sources[3:]):
        rows, width = group[0].shape
        for part, source in enumerate(group):
            packed[0, first : first + rows, part * width : (part + 1) * width] = source[...]
        first += rows


def pack(core, img_qkv, txt_qkv, text_rows, destinations, column_block, width, after):
    img_rows = img_qkv.shape[0]
    blocks = img_qkv.shape[1] // 3 // width

    def source(rows, part, by_core):
        def place(d, info):
            return (info[0] if by_core else 0, part * blocks + column_block(d))

        return pl.BlockSpec((rows, width), place)

    return pl.pallas_call(
        pack_body,
        grid_spec=pltpu.PrefetchScalarGridSpec(
            num_scalar_prefetch=1,
            grid=(destinations,),
            in_specs=[source(img_rows, part, False) for part in range(3)]
            + [source(text_rows, part, True) for part in range(3)]
            + [pl.BlockSpec(memory_space=pl.ANY)] * len(after),
            out_specs=pl.BlockSpec(
                (1, img_rows + text_rows, 3 * width), lambda d, info: (d, 0, 0)
            ),
        ),
        out_shape=jax.ShapeDtypeStruct(
            (destinations, img_rows + text_rows, 3 * width), img_qkv.dtype
        ),
        compiler_params=params(),
        name="pack_heads",
    )(core, img_qkv, img_qkv, img_qkv, txt_qkv, txt_qkv, txt_qkv, *after)


def dot(first, second, contract):
    return lax.dot_general(
        first, second, ((contract[:1], contract[1:]), ((), ())), preferred_element_type=jnp.float32
    )


def with_ones(block):
    return jnp.concatenate([block, jnp.ones_like(block)], axis=1)


def reference_columns(row_max):
    reference = row_max.astype(jnp.bfloat16).astype(jnp.float32)
    return jnp.broadcast_to(reference * (-1.0 / HD), (row_max.shape[0], HD)).astype(jnp.bfloat16)


def weighted(queries, key_rows, values):
    weights = jnp.exp2(dot(queries, key_rows, (1, 1)) * SCALE).astype(jnp.bfloat16)
    return dot(weights, values, (1, 0))


def tiles_of(rows):
    tile = min(TILE, rows)
    return [slice(first, min(first + tile, rows)) for first in range(0, rows, tile)]


def split_rows(block, img_rows):
    return (
        block[:, :img_rows, :].reshape(-1, HD),
        block[:, img_rows:, :].reshape(-1, HD),
    )


def until_small(flag, total, attempt):
    flag[0] = 1

    @pl.loop(0, 2)
    def _(turn):
        @pl.when(flag[0] == 1)
        def _():
            attempt(turn)
            flag[0] = jnp.where(jnp.max(total[:, HD:]) > LARGE, 1, 0).astype(jnp.int32)


def head_body(pair, img_rows, others, has_earlier, info, *refs):
    q_ref, k_ref, v_ref = refs[:3]
    stale = refs[3 : 3 + pair]
    arrived = refs[3 + pair : 3 + pair + others]
    out, aug, total, flag = refs[3 + pair + others + has_earlier :]
    core = info[0]
    k_img, k_txt = split_rows(k_ref[...], img_rows)
    v_img, v_txt = split_rows(v_ref[...], img_rows)
    q_img, q_txt = split_rows(q_ref[...], img_rows)
    fresh_rows = q_img.shape[0]
    group_rows = fresh_rows // pair
    rows = fresh_rows + q_txt.shape[0]

    def queries_at(span):
        if span.stop <= fresh_rows:
            return q_img[span, :]
        return q_txt[span.start - fresh_rows : span.stop - fresh_rows, :]

    def key_sets():
        shared = [(k_txt, v_txt)] + [(block[0, 0], block[0, 1]) for block in arrived]
        for group in range(pair):
            span = slice(group * group_rows, (group + 1) * group_rows)
            own = [(k_img[span, :], v_img[span, :])]
            if pair == 2:
                mine = core == group
                own.append(
                    (
                        jnp.where(mine, stale[1][0], stale[0][0]),
                        jnp.where(mine, stale[1][1], stale[0][1]),
                    )
                )
            yield span, own, shared
        yield slice(fresh_rows, rows), [(block[0], block[1]) for block in stale], shared

    def pieces_of(own, shared):
        joined = (
            jnp.concatenate([key_rows for key_rows, _ in own], 0),
            jnp.concatenate([values for _, values in own], 0),
        )
        return shared[:1] + [joined] + shared[1:]

    def spans_of(span):
        return [
            slice(span.start + tile.start, span.start + tile.stop)
            for tile in tiles_of(span.stop - span.start)
        ]

    def largest(span, key_rows):
        return jnp.max(dot(queries_at(span), key_rows, (1, 1)), axis=1, keepdims=True)

    def attempt(turn):
        @pl.when(turn == 0)
        def _():
            for span, _, shared in key_sets():
                for tile in spans_of(span):
                    key_rows = shared[0][0]
                    aug[tile, :] = reference_columns(
                        largest(tile, key_rows[: min(256, key_rows.shape[0]), :])
                    )

        @pl.when(turn == 1)
        def _():
            for span, own, shared in key_sets():
                for tile in spans_of(span):
                    row_max = None
                    for key_rows, _ in pieces_of(own, shared):
                        piece_max = largest(tile, key_rows)
                        row_max = piece_max if row_max is None else jnp.maximum(row_max, piece_max)
                    aug[tile, :] = reference_columns(row_max)

        for span, own, shared in key_sets():
            pieces = [(with_ones(k), with_ones(v)) for k, v in pieces_of(own, shared)]
            for tile in spans_of(span):
                queries = jnp.concatenate([queries_at(tile), aug[tile, :]], axis=1)
                summed = None
                for key_rows, values in pieces:
                    piece = weighted(queries, key_rows, values)
                    summed = piece if summed is None else summed + piece
                total[tile, :] = summed

    until_small(flag, total, attempt)
    attended = (total[:, :HD] / total[:, HD:]).astype(out.dtype)
    destinations = out.shape[0]
    out[:, :img_rows, :] = attended[:fresh_rows].reshape(destinations, img_rows, HD)
    out[:, img_rows:, :] = attended[fresh_rows:].reshape(destinations, -1, HD)


def attend_cost(queries, keys, heads):
    return pl.CostEstimate(
        flops=4 * queries * keys * heads * HD,
        bytes_accessed=4 * queries * heads * HD + 4 * keys * heads * HD,
        transcendentals=queries * keys * heads,
    )


def attend_head(info, qkv, img_rows, stale, gathered, head, place, places, earlier=None):
    heads = qkv.shape[2] // (3 * HD)
    others = gathered.shape[0] - 1
    rows = qkv.shape[0] * qkv.shape[1]

    def columns(array, block):
        return pl.BlockSpec(array.shape[:2] + (HD,), lambda n, info: (0, 0, block))

    def other(index):
        return pl.BlockSpec(
            (1,) + gathered.shape[1:], lambda n, info: (info[1 + index], 0, 0, 0)
        )

    operands = [qkv] * 3 + list(stale) + [gathered] * others
    in_specs = [columns(qkv, part * heads + head) for part in range(3)]
    in_specs += [columns(block, head) for block in stale]
    in_specs += [other(index) for index in range(others)]
    aliases = {}
    if earlier is not None:
        aliases = {1 + len(operands): 0}
        operands.append(earlier)
        in_specs.append(pl.BlockSpec(memory_space=pl.ANY))
    keys = others * gathered.shape[2] + 2 * rows // 2
    return pl.pallas_call(
        functools.partial(head_body, len(stale), img_rows, others, int(earlier is not None)),
        grid_spec=pltpu.PrefetchScalarGridSpec(
            num_scalar_prefetch=1,
            grid=(1,),
            in_specs=in_specs,
            out_specs=pl.BlockSpec(qkv.shape[:2] + (HD,), lambda n, info: (0, 0, place)),
            scratch_shapes=[
                pltpu.VMEM((rows, HD), jnp.bfloat16),
                pltpu.VMEM((rows, 2 * HD), jnp.float32),
                pltpu.SMEM((1,), jnp.int32),
            ],
        ),
        out_shape=jax.ShapeDtypeStruct(qkv.shape[:2] + (places * HD,), qkv.dtype),
        input_output_aliases=aliases,
        compiler_params=params(),
        cost_estimate=attend_cost(rows, keys, 1),
        name="attend_head",
    )(info, *operands)


def project_body(order, last, x_ref, weight, *refs):
    if last:
        residual, gate, earlier, out, flat = refs
    else:
        out, flat = refs

    @pl.when(pl.program_id(0) == 0)
    def _():
        rows, width = flat.shape[0], x_ref.shape[2]
        for source, place in enumerate(order):
            flat[:, place * width : (place + 1) * width] = x_ref[source, :rows, :]

    columns = weight.shape[3]
    block = weight[...].reshape(flat.shape[1], columns)
    projected = jnp.dot(flat[...], block, preferred_element_type=jnp.float32)
    if last:
        projected = earlier[...] + projected
        projected = residual[...].astype(jnp.float32) + gate[...] * projected
    out[...] = projected.astype(out.dtype)


def project(x, order, weight, first_head, rows, final=None):
    model = weight.shape[3]
    heads = x.shape[2] // HD
    columns = 512 if model % 512 == 0 else HD
    row_spec = pl.BlockSpec((rows, columns), lambda n: (0, n))
    operands, in_specs = [x, weight], [
        pl.BlockSpec(x.shape, lambda n: (0, 0, 0)),
        pl.BlockSpec(
            (weight.shape[0], heads, HD, columns), lambda n: (0, first_head // heads, 0, n)
        ),
    ]
    if final is not None:
        residual, gate, earlier = final
        operands += [residual, gate.reshape(1, model), earlier]
        in_specs += [row_spec, pl.BlockSpec((1, columns), lambda n: (0, n)), row_spec]
    depth = x.shape[0] * x.shape[2]
    return pl.pallas_call(
        functools.partial(project_body, order, final is not None),
        grid=(model // columns,),
        in_specs=in_specs,
        out_specs=row_spec,
        out_shape=jax.ShapeDtypeStruct(
            (rows, model), jnp.float32 if final is None else residual.dtype
        ),
        scratch_shapes=[pltpu.VMEM((rows, depth), x.dtype)],
        compiler_params=params(),
        cost_estimate=pl.CostEstimate(
            flops=2 * rows * model * depth, bytes_accessed=2 * model * depth, transcendentals=0
        ),
        name="project_last" if final is not None else "project_early",
    )(*operands)


def unpack_body(order, first, heads, *refs):
    sources, out = refs[:-1], refs[-1]
    for source, place in enumerate(order):
        at = place * heads * HD
        for x_ref in sources:
            width = x_ref.shape[2]
            out[:, at : at + width] = x_ref[source, first:, :]
            at += width


def unpack_text(parts, order, first):
    heads = sum(x.shape[2] for x in parts) // HD
    rows, model = parts[0].shape[1] - first, parts[0].shape[0] * heads * HD
    return pl.pallas_call(
        functools.partial(unpack_body, order, first, heads),
        grid=(1,),
        in_specs=[pl.BlockSpec(x.shape, lambda n: (0, 0, 0)) for x in parts],
        out_specs=pl.BlockSpec((rows, model), lambda n: (0, 0)),
        out_shape=jax.ShapeDtypeStruct((rows, model), parts[0].dtype),
        compiler_params=params(),
        name="unpack_text",
    )(*parts)


def per_device(img_qkv, txt_qkv, stale_kv, residual, gate_scale, proj_weight):
    patches, head_owners = lax.axis_size("patch"), lax.axis_size("head")
    patch = lax.axis_index("patch")
    owned_heads = stale_kv.shape[2] // HD
    pair = 2 if patches % 2 == 0 and owned_heads % 2 == 0 else 1
    planes = patches // pair
    plane, core = patch // pair, patch % pair
    width = stale_kv.shape[2] // pair
    heads = width // HD
    img_rows, model = residual.shape
    text_rows = txt_qkv.shape[0] // pair
    destinations = pair * head_owners

    def column_block(d):
        return (d % head_owners) * pair + d // head_owners

    order = [column_block(d) for d in range(destinations)]
    groups = [[g * destinations + d for d in range(destinations)] for g in range(planes)]
    columns = [[z * pair + c for z in range(planes)] for c in range(pair)]

    def exchange(x):
        return lax.all_to_all(
            x, ("patch", "head"), split_axis=0, concat_axis=0, axis_index_groups=groups, tiled=True
        )

    swap_pairs = [(p, p + 1 - 2 * (p % 2)) for p in range(patches)]
    stale = [lax.dynamic_slice_in_dim(stale_kv, core * width, width, 2)]
    if pair == 2:
        theirs = lax.dynamic_slice_in_dim(stale_kv, (1 - core) * width, width, 2)
        stale.append(lax.ppermute(theirs, "patch", swap_pairs))

    gathered = []
    for head in range(heads):
        columns_of = [block[:, :, head * HD : (head + 1) * HD] for block in stale]
        gathered.append(
            lax.all_gather(
                jnp.concatenate(columns_of, axis=1), "patch", axis=0, axis_index_groups=columns
            )
        )

    core_only = core.astype(jnp.int32).reshape(1)
    qkv = exchange(
        pack(core_only, img_qkv, txt_qkv, text_rows, destinations, column_block, width, stale[1:])
    )

    info = jnp.stack([core] + [(plane + step) % planes for step in range(1, planes)])
    info = info.astype(jnp.int32)
    early = None
    for head in range(heads - 1):
        early = attend_head(
            info, qkv, img_rows, stale, gathered[head], head, head, heads - 1, early
        )
    weight = proj_weight.reshape(destinations, heads, HD, model)
    early = exchange(early)
    late = exchange(attend_head(info, qkv, img_rows, stale, gathered[-1], heads - 1, 0, 1))

    text_out = unpack_text([early, late], order, img_rows)
    if pair == 2:
        other = lax.ppermute(text_out, "patch", swap_pairs)
        lower = core == 0
        text_out = jnp.concatenate(
            [jnp.where(lower, text_out, other), jnp.where(lower, other, text_out)], 0
        )
    partial = project(early, order, weight, 0, img_rows)
    image_out = project(
        late, order, weight, heads - 1, img_rows, (residual, gate_scale, partial)
    )
    return (image_out, text_out)


def solution(mesh):
    return jax.shard_map(
        per_device,
        mesh=mesh,
        in_specs=(
            P(("patch", "head"), None),
            P("head", None),
            P(None, "patch", "head"),
            P(("patch", "head"), None),
            P(),
            P(),
        ),
        out_specs=(P(("patch", "head"), None), P("head", None)),
        check_vma=False,
    )
```

```python
import functools
import math

import jax
import jax.numpy as jnp
from jax import lax
from jax.experimental import pallas as pl
from jax.experimental.pallas import tpu as pltpu
from jax.sharding import PartitionSpec as P

HD = 128
SCALE = math.log2(math.e) / math.sqrt(HD)
VMEM_LIMIT = 24 * 1024 * 1024
WIDE_LIMIT = 48 * 1024 * 1024
TILE = 256
LARGE = 2.0**60


def params():
    return pltpu.CompilerParams(
        vmem_limit_bytes=VMEM_LIMIT, dimension_semantics=("arbitrary",)
    )


def pack_body(info, *refs):
    sources, packed = refs[:6], refs[-1]
    first = 0
    for group in (sources[:3], sources[3:]):
        rows, width = group[0].shape
        for part, source in enumerate(group):
            packed[0, first : first + rows, part * width : (part + 1) * width] = source[...]
        first += rows


def pack(core, img_qkv, txt_qkv, text_rows, destinations, column_block, width, after):
    img_rows = img_qkv.shape[0]
    blocks = img_qkv.shape[1] // 3 // width

    def source(rows, part, by_core):
        def place(d, info):
            return (info[0] if by_core else 0, part * blocks + column_block(d))

        return pl.BlockSpec((rows, width), place)

    return pl.pallas_call(
        pack_body,
        grid_spec=pltpu.PrefetchScalarGridSpec(
            num_scalar_prefetch=1,
            grid=(destinations,),
            in_specs=[source(img_rows, part, False) for part in range(3)]
            + [source(text_rows, part, True) for part in range(3)]
            + [pl.BlockSpec(memory_space=pl.ANY)] * len(after),
            out_specs=pl.BlockSpec(
                (1, img_rows + text_rows, 3 * width), lambda d, info: (d, 0, 0)
            ),
        ),
        out_shape=jax.ShapeDtypeStruct(
            (destinations, img_rows + text_rows, 3 * width), img_qkv.dtype
        ),
        compiler_params=params(),
        name="pack_heads",
    )(core, img_qkv, img_qkv, img_qkv, txt_qkv, txt_qkv, txt_qkv, *after)


def dot(first, second, contract):
    return lax.dot_general(
        first, second, ((contract[:1], contract[1:]), ((), ())), preferred_element_type=jnp.float32
    )


def with_ones(block):
    return jnp.concatenate([block, jnp.ones_like(block)], axis=1)


def reference_columns(row_max):
    reference = row_max.astype(jnp.bfloat16).astype(jnp.float32)
    return jnp.broadcast_to(reference * (-1.0 / HD), (row_max.shape[0], HD)).astype(jnp.bfloat16)


def weighted(queries, key_rows, values):
    weights = jnp.exp2(dot(queries, key_rows, (1, 1)) * SCALE).astype(jnp.bfloat16)
    return dot(weights, values, (1, 0))


def tiles_of(rows):
    tile = min(TILE, rows)
    return [slice(first, min(first + tile, rows)) for first in range(0, rows, tile)]


def split_rows(block, img_rows):
    return (
        block[:, :img_rows, :].reshape(-1, HD),
        block[:, img_rows:, :].reshape(-1, HD),
    )


def until_small(flag, total, attempt):
    flag[0] = 1

    @pl.loop(0, 2)
    def _(turn):
        @pl.when(flag[0] == 1)
        def _():
            attempt(turn)
            flag[0] = jnp.where(jnp.max(total[:, HD:]) > LARGE, 1, 0).astype(jnp.int32)


def head_body(pair, img_rows, others, has_earlier, info, *refs):
    q_ref, k_ref, v_ref = refs[:3]
    stale = refs[3 : 3 + pair]
    candidates = refs[3 + pair : 3 + pair + 2 * others]
    out, arrived, aug, total, flag = refs[3 + pair + 2 * others + has_earlier :]
    for index in range(others):
        from_left = info[1 + index] == 1
        arrived[index] = jnp.where(
            from_left, candidates[2 * index][...], candidates[2 * index + 1][...]
        )
    core = info[0]
    k_img, k_txt = split_rows(k_ref[...], img_rows)
    v_img, v_txt = split_rows(v_ref[...], img_rows)
    q_img, q_txt = split_rows(q_ref[...], img_rows)
    fresh_rows = q_img.shape[0]
    group_rows = fresh_rows // pair
    rows = fresh_rows + q_txt.shape[0]

    def queries_at(span):
        if span.stop <= fresh_rows:
            return q_img[span, :]
        return q_txt[span.start - fresh_rows : span.stop - fresh_rows, :]

    def key_sets():
        shared = [(k_txt, v_txt)] + [(arrived[i, 0], arrived[i, 1]) for i in range(others)]
        for group in range(pair):
            span = slice(group * group_rows, (group + 1) * group_rows)
            own = [(k_img[span, :], v_img[span, :])]
            if pair == 2:
                mine = core == group
                own.append(
                    (
                        jnp.where(mine, stale[1][0], stale[0][0]),
                        jnp.where(mine, stale[1][1], stale[0][1]),
                    )
                )
            yield span, own, shared
        yield slice(fresh_rows, rows), [(block[0], block[1]) for block in stale], shared

    def pieces_of(own, shared):
        joined = (
            jnp.concatenate([key_rows for key_rows, _ in own], 0),
            jnp.concatenate([values for _, values in own], 0),
        )
        return shared[:1] + [joined] + shared[1:]

    def spans_of(span):
        return [
            slice(span.start + tile.start, span.start + tile.stop)
            for tile in tiles_of(span.stop - span.start)
        ]

    def largest(span, key_rows):
        return jnp.max(dot(queries_at(span), key_rows, (1, 1)), axis=1, keepdims=True)

    def attempt(turn):
        @pl.when(turn == 0)
        def _():
            for span, _, shared in key_sets():
                for tile in spans_of(span):
                    key_rows = shared[0][0]
                    aug[tile, :] = reference_columns(
                        largest(tile, key_rows[: min(256, key_rows.shape[0]), :])
                    )

        @pl.when(turn == 1)
        def _():
            for span, own, shared in key_sets():
                for tile in spans_of(span):
                    row_max = None
                    for key_rows, _ in pieces_of(own, shared):
                        piece_max = largest(tile, key_rows)
                        row_max = piece_max if row_max is None else jnp.maximum(row_max, piece_max)
                    aug[tile, :] = reference_columns(row_max)

        for span, own, shared in key_sets():
            pieces = [(with_ones(k), with_ones(v)) for k, v in pieces_of(own, shared)]
            for tile in spans_of(span):
                queries = jnp.concatenate([queries_at(tile), aug[tile, :]], axis=1)
                summed = None
                for key_rows, values in pieces:
                    piece = weighted(queries, key_rows, values)
                    summed = piece if summed is None else summed + piece
                total[tile, :] = summed

    until_small(flag, total, attempt)
    attended = (total[:, :HD] / total[:, HD:]).astype(out.dtype)
    destinations = out.shape[0]
    out[:, :img_rows, :] = attended[:fresh_rows].reshape(destinations, img_rows, HD)
    out[:, img_rows:, :] = attended[fresh_rows:].reshape(destinations, -1, HD)


def attend_cost(queries, keys, heads):
    return pl.CostEstimate(
        flops=4 * queries * keys * heads * HD,
        bytes_accessed=4 * queries * heads * HD + 4 * keys * heads * HD,
        transcendentals=queries * keys * heads,
    )


def attend_head(info, qkv, img_rows, stale, arrived, head, place, places, earlier=None):
    heads = qkv.shape[2] // (3 * HD)
    others = len(arrived)
    block_shape = arrived[0][0].shape
    rows = qkv.shape[0] * qkv.shape[1]

    def spec(shape, block):
        return pl.BlockSpec(
            shape, lambda n, info: (0, 0, block), pipeline_mode=pl.Buffered(buffer_count=1)
        )

    def columns(array, block):
        return spec(array.shape[:2] + (HD,), block)

    operands = [qkv] * 3 + list(stale) + [block for either in arrived for block in either]
    in_specs = [columns(qkv, part * heads + head) for part in range(3)]
    in_specs += [columns(block, head) for block in stale]
    in_specs += [spec(block_shape, 0)] * (2 * others)
    aliases = {}
    if earlier is not None:
        aliases = {1 + len(operands): 0}
        operands.append(earlier)
        in_specs.append(pl.BlockSpec(memory_space=pl.ANY))
    keys = others * block_shape[1] + rows
    return pl.pallas_call(
        functools.partial(head_body, len(stale), img_rows, others, int(earlier is not None)),
        grid_spec=pltpu.PrefetchScalarGridSpec(
            num_scalar_prefetch=1,
            grid=(1,),
            in_specs=in_specs,
            out_specs=pl.BlockSpec(qkv.shape[:2] + (HD,), lambda n, info: (0, 0, place)),
            scratch_shapes=[
                pltpu.VMEM((others,) + block_shape, qkv.dtype),
                pltpu.VMEM((rows, HD), jnp.bfloat16),
                pltpu.VMEM((rows, 2 * HD), jnp.float32),
                pltpu.SMEM((1,), jnp.int32),
            ],
        ),
        out_shape=jax.ShapeDtypeStruct(qkv.shape[:2] + (places * HD,), qkv.dtype),
        input_output_aliases=aliases,
        compiler_params=params(),
        cost_estimate=attend_cost(rows, keys, 1),
        name="attend_head",
    )(info, *operands)


def project_body(order, first_head, heads, group, last, *refs):
    if last:
        x_ref, weight, residual, gate, earlier, out, flat, held, total, sems = refs
    else:
        x_ref, weight, out, flat, held, total, sems = refs
    chunks = weight.shape[0] // group
    copies = [
        pltpu.make_async_copy(
            weight.at[pl.ds(chunk * group, group), pl.ds(first_head, heads)],
            held.at[pl.ds(chunk * group, group)],
            sems.at[chunk],
        )
        for chunk in range(chunks)
    ]
    for copy in copies:
        copy.start()
    rows, width = flat.shape[0], x_ref.shape[2]
    for source, place in enumerate(order):
        flat[:, place * width : (place + 1) * width] = x_ref[source, :rows, :]
    depth = group * width
    for chunk, copy in enumerate(copies):
        copy.wait()
        block = held[chunk * group : (chunk + 1) * group].reshape(depth, held.shape[3])
        part = jnp.dot(
            flat[:, chunk * depth : (chunk + 1) * depth], block, preferred_element_type=jnp.float32
        )
        if chunk == 0:
            total[...] = part
        else:
            total[...] += part
    if last:
        projected = earlier[...] + total[...]
        out[...] = (residual[...].astype(jnp.float32) + gate[...] * projected).astype(out.dtype)
    else:
        out[...] = total[...]


def project(x, order, weight, first_head, rows, final=None):
    destinations, model = weight.shape[0], weight.shape[3]
    heads = x.shape[2] // HD
    group = 2 if heads % 2 and destinations % 2 == 0 else 1
    operands = [x, weight]
    in_specs = [pl.BlockSpec(memory_space=pltpu.VMEM), pl.BlockSpec(memory_space=pl.ANY)]
    if final is not None:
        residual, gate, earlier = final
        operands += [residual, gate.reshape(1, model), earlier]
        in_specs += [pl.BlockSpec(memory_space=pltpu.VMEM)] * 3
    depth = x.shape[0] * x.shape[2]
    return pl.pallas_call(
        functools.partial(project_body, order, first_head, heads, group, final is not None),
        in_specs=in_specs,
        out_specs=pl.BlockSpec(memory_space=pltpu.VMEM),
        out_shape=jax.ShapeDtypeStruct(
            (rows, model), jnp.float32 if final is None else residual.dtype
        ),
        scratch_shapes=[
            pltpu.VMEM((rows, depth), x.dtype),
            pltpu.VMEM((destinations, heads, HD, model), weight.dtype),
            pltpu.VMEM((rows, model), jnp.float32),
            pltpu.SemaphoreType.DMA((destinations // group,)),
        ],
        compiler_params=pltpu.CompilerParams(vmem_limit_bytes=WIDE_LIMIT),
        cost_estimate=pl.CostEstimate(
            flops=2 * rows * model * depth, bytes_accessed=2 * model * depth, transcendentals=0
        ),
        name="project_last" if final is not None else "project_early",
    )(*operands)


def unpack_body(order, first, heads, *refs):
    sources, out = refs[:-1], refs[-1]
    for source, place in enumerate(order):
        at = place * heads * HD
        for x_ref in sources:
            width = x_ref.shape[2]
            out[:, at : at + width] = x_ref[source, first:, :]
            at += width


def unpack_text(parts, order, first):
    heads = sum(x.shape[2] for x in parts) // HD
    rows, model = parts[0].shape[1] - first, parts[0].shape[0] * heads * HD
    return pl.pallas_call(
        functools.partial(unpack_body, order, first, heads),
        grid=(1,),
        in_specs=[pl.BlockSpec(x.shape, lambda n: (0, 0, 0)) for x in parts],
        out_specs=pl.BlockSpec((rows, model), lambda n: (0, 0)),
        out_shape=jax.ShapeDtypeStruct((rows, model), parts[0].dtype),
        compiler_params=params(),
        name="unpack_text",
    )(*parts)


def per_device(img_qkv, txt_qkv, stale_kv, residual, gate_scale, proj_weight):
    patches, head_owners = lax.axis_size("patch"), lax.axis_size("head")
    patch = lax.axis_index("patch")
    owned_heads = stale_kv.shape[2] // HD
    pair = 2 if patches % 2 == 0 and owned_heads % 2 == 0 else 1
    planes = patches // pair
    plane, core = patch // pair, patch % pair
    width = stale_kv.shape[2] // pair
    heads = width // HD
    img_rows, model = residual.shape
    text_rows = txt_qkv.shape[0] // pair
    destinations = pair * head_owners

    def column_block(d):
        return (d % head_owners) * pair + d // head_owners

    order = [column_block(d) for d in range(destinations)]
    groups = [[g * destinations + d for d in range(destinations)] for g in range(planes)]
    def exchange(x):
        return lax.all_to_all(
            x, ("patch", "head"), split_axis=0, concat_axis=0, axis_index_groups=groups, tiled=True
        )

    swap_pairs = [(p, p + 1 - 2 * (p % 2)) for p in range(patches)]
    stale = [lax.dynamic_slice_in_dim(stale_kv, core * width, width, 2)]
    if pair == 2:
        theirs = lax.dynamic_slice_in_dim(stale_kv, (1 - core) * width, width, 2)
        stale.append(lax.ppermute(theirs, "patch", swap_pairs))

    arrived = []
    for head in range(heads):
        columns_of = [block[:, :, head * HD : (head + 1) * HD] for block in stale]
        from_left = from_right = jnp.concatenate(columns_of, axis=1)
        left, right = [], []
        for step in range(1, planes):
            right_pairs = [(p, p + pair) for p in range((step - 1) * pair, patches - pair)]
            left_pairs = [(p + pair, p) for p in range(0, patches - step * pair)]
            from_left = lax.ppermute(from_left, "patch", right_pairs)
            from_right = lax.ppermute(from_right, "patch", left_pairs)
            left.append(from_left)
            right.append(from_right)
        arrived.append(list(zip(left, reversed(right))))

    core_only = core.astype(jnp.int32).reshape(1)
    qkv = exchange(
        pack(core_only, img_qkv, txt_qkv, text_rows, destinations, column_block, width, stale[1:])
    )

    info = jnp.stack([core] + [plane >= step for step in range(1, planes)])
    info = info.astype(jnp.int32)
    early = None
    for head in range(heads - 1):
        early = attend_head(
            info, qkv, img_rows, stale, arrived[head], head, head, heads - 1, early
        )
    weight = proj_weight.reshape(destinations, heads, HD, model)
    early = exchange(early)
    late = exchange(attend_head(info, qkv, img_rows, stale, arrived[-1], heads - 1, 0, 1))

    text_out = unpack_text([early, late], order, img_rows)
    if pair == 2:
        other = lax.ppermute(text_out, "patch", swap_pairs)
        lower = core == 0
        text_out = jnp.concatenate(
            [jnp.where(lower, text_out, other), jnp.where(lower, other, text_out)], 0
        )
    partial = project(early, order, weight, 0, img_rows)
    image_out = project(
        late, order, weight, heads - 1, img_rows, (residual, gate_scale, partial)
    )
    return (image_out, text_out)


def solution(mesh):
    return jax.shard_map(
        per_device,
        mesh=mesh,
        in_specs=(
            P(("patch", "head"), None),
            P("head", None),
            P(None, "patch", "head"),
            P(("patch", "head"), None),
            P(),
            P(),
        ),
        out_specs=(P(("patch", "head"), None), P("head", None)),
        check_vma=False,
    )
```

```python
import functools
import math

import jax
import jax.numpy as jnp
from jax import lax
from jax.experimental import pallas as pl
from jax.experimental.pallas import tpu as pltpu
from jax.sharding import PartitionSpec as P

HD = 128
SCALE = math.log2(math.e) / math.sqrt(HD)
VMEM_LIMIT = 16 * 1024 * 1024
WIDE_LIMIT = 48 * 1024 * 1024
TILE = 256
LARGE = 2.0**60


def params():
    return pltpu.CompilerParams(
        vmem_limit_bytes=VMEM_LIMIT, dimension_semantics=("arbitrary",)
    )


def pack_body(text_rows, places, width, core, img, txt, packed, sem):
    img_rows, model = img.shape[0], img.shape[1] // 3
    first = pl.multiple_of(core[0] * text_rows, text_rows)
    copies = []
    for destination, place in enumerate(places):
        for part in range(3):
            source = pl.ds(part * model + place * width, width)
            target = pl.ds(part * width, width)
            copies.append((img.at[:, source], packed.at[destination, pl.ds(0, img_rows), target]))
            copies.append(
                (
                    txt.at[pl.ds(first, text_rows), source],
                    packed.at[destination, pl.ds(img_rows, text_rows), target],
                )
            )
    copies = [
        pltpu.make_async_copy(source, target, sem.at[index])
        for index, (source, target) in enumerate(copies)
    ]
    for copy in copies:
        copy.start()
    for copy in copies:
        copy.wait()


def pack(core, img_qkv, txt_qkv, text_rows, places, width):
    rows = img_qkv.shape[0] + text_rows
    anywhere = pl.BlockSpec(memory_space=pl.ANY)
    return pl.pallas_call(
        functools.partial(pack_body, text_rows, places, width),
        in_specs=[pl.BlockSpec(memory_space=pltpu.SMEM), anywhere, anywhere],
        out_specs=anywhere,
        out_shape=jax.ShapeDtypeStruct((len(places), rows, 3 * width), img_qkv.dtype),
        scratch_shapes=[pltpu.SemaphoreType.DMA((6 * len(places),))],
        compiler_params=pltpu.CompilerParams(vmem_limit_bytes=WIDE_LIMIT),
        name="pack_heads",
    )(core, img_qkv, txt_qkv)


def dot(first, second, contract):
    return lax.dot_general(
        first, second, ((contract[:1], contract[1:]), ((), ())), preferred_element_type=jnp.float32
    )


def with_ones(block):
    return jnp.concatenate([block, jnp.ones_like(block)], axis=1)


def reference_columns(row_max):
    reference = row_max.astype(jnp.bfloat16).astype(jnp.float32)
    return jnp.broadcast_to(reference * (-1.0 / HD), (row_max.shape[0], HD)).astype(jnp.bfloat16)


def weighted(queries, key_rows, values):
    weights = jnp.exp2(dot(queries, key_rows, (1, 1)) * SCALE).astype(jnp.bfloat16)
    return dot(weights, values, (1, 0))


def tiles_of(rows):
    tile = min(TILE, rows)
    return [slice(first, min(first + tile, rows)) for first in range(0, rows, tile)]


def split_rows(block, img_rows):
    return (
        block[:, :img_rows, :].reshape(-1, HD),
        block[:, img_rows:, :].reshape(-1, HD),
    )


def until_small(flag, total, attempt):
    flag[0] = 1

    @pl.loop(0, 2)
    def _(turn):
        @pl.when(flag[0] == 1)
        def _():
            attempt(turn)
            flag[0] = jnp.where(jnp.max(total[:, HD:]) > LARGE, 1, 0).astype(jnp.int32)


def head_body(pair, img_rows, others, untouched, info, *refs):
    q_ref, k_ref, v_ref = refs[:3]
    stale = refs[3 : 3 + pair]
    candidates = refs[3 + pair : 3 + pair + 2 * others]
    out = refs[3 + pair + 2 * others + untouched]
    arrived, aug, total, flag = refs[-4:]
    for index in range(others):
        from_left = info[1 + index] == 1
        arrived[index] = jnp.where(
            from_left, candidates[2 * index][...], candidates[2 * index + 1][...]
        )
    core = info[0]
    k_img, k_txt = split_rows(k_ref[...], img_rows)
    v_img, v_txt = split_rows(v_ref[...], img_rows)
    q_img, q_txt = split_rows(q_ref[...], img_rows)
    fresh_rows = q_img.shape[0]
    group_rows = fresh_rows // pair
    rows = fresh_rows + q_txt.shape[0]

    def queries_at(span):
        if span.stop <= fresh_rows:
            return q_img[span, :]
        return q_txt[span.start - fresh_rows : span.stop - fresh_rows, :]

    def key_sets():
        shared = [(k_txt, v_txt)] + [(arrived[i, 0], arrived[i, 1]) for i in range(others)]
        for group in range(pair):
            span = slice(group * group_rows, (group + 1) * group_rows)
            own = [(k_img[span, :], v_img[span, :])]
            if pair == 2:
                mine = core == group
                own.append(
                    (
                        jnp.where(mine, stale[1][0], stale[0][0]),
                        jnp.where(mine, stale[1][1], stale[0][1]),
                    )
                )
            yield span, own, shared
        yield slice(fresh_rows, rows), [(block[0], block[1]) for block in stale], shared

    def pieces_of(own, shared):
        joined = (
            jnp.concatenate([key_rows for key_rows, _ in own], 0),
            jnp.concatenate([values for _, values in own], 0),
        )
        return shared[:1] + [joined] + shared[1:]

    def spans_of(span):
        return [
            slice(span.start + tile.start, span.start + tile.stop)
            for tile in tiles_of(span.stop - span.start)
        ]

    def largest(span, key_rows):
        return jnp.max(dot(queries_at(span), key_rows, (1, 1)), axis=1, keepdims=True)

    def attempt(turn):
        @pl.when(turn == 0)
        def _():
            for span, _, shared in key_sets():
                for tile in spans_of(span):
                    key_rows = shared[0][0]
                    aug[tile, :] = reference_columns(
                        largest(tile, key_rows[: min(256, key_rows.shape[0]), :])
                    )

        @pl.when(turn == 1)
        def _():
            for span, own, shared in key_sets():
                for tile in spans_of(span):
                    row_max = None
                    for key_rows, _ in pieces_of(own, shared):
                        piece_max = largest(tile, key_rows)
                        row_max = piece_max if row_max is None else jnp.maximum(row_max, piece_max)
                    aug[tile, :] = reference_columns(row_max)

        for span, own, shared in key_sets():
            pieces = [(with_ones(k), with_ones(v)) for k, v in pieces_of(own, shared)]
            for tile in spans_of(span):
                queries = jnp.concatenate([queries_at(tile), aug[tile, :]], axis=1)
                summed = None
                for key_rows, values in pieces:
                    piece = weighted(queries, key_rows, values)
                    summed = piece if summed is None else summed + piece
                total[tile, :] = summed

    until_small(flag, total, attempt)
    attended = (total[:, :HD] / total[:, HD:]).astype(out.dtype)
    destinations = out.shape[0]
    out[:, :img_rows, :] = attended[:fresh_rows].reshape(destinations, img_rows, HD)
    out[:, img_rows:, :] = attended[fresh_rows:].reshape(destinations, -1, HD)


def attend_cost(queries, keys, heads):
    return pl.CostEstimate(
        flops=4 * queries * keys * heads * HD,
        bytes_accessed=4 * queries * heads * HD + 4 * keys * heads * HD,
        transcendentals=queries * keys * heads,
    )


def attend_head(info, qkv, img_rows, stale, arrived, head, place, places, earlier=None, passing=()):
    heads = qkv.shape[2] // (3 * HD)
    others = len(arrived)
    block_shape = arrived[0][0].shape
    rows = qkv.shape[0] * qkv.shape[1]

    def spec(shape, block):
        return pl.BlockSpec(
            shape, lambda n, info: (0, 0, block), pipeline_mode=pl.Buffered(buffer_count=1)
        )

    def columns(array, block):
        return spec(array.shape[:2] + (HD,), block)

    operands = [qkv] * 3 + list(stale) + [block for either in arrived for block in either]
    in_specs = [columns(qkv, part * heads + head) for part in range(3)]
    in_specs += [columns(block, head) for block in stale]
    in_specs += [spec(block_shape, 0)] * (2 * others)
    aliases = {}
    if earlier is not None:
        aliases = {1 + len(operands): 0}
        operands.append(earlier)
    for index, array in enumerate(passing):
        aliases[1 + len(operands)] = 1 + index
        operands.append(array)
    untouched = len(operands) - len(in_specs)
    anywhere = pl.BlockSpec(memory_space=pl.ANY)
    in_specs += [anywhere] * untouched
    keys = others * block_shape[1] + rows
    return pl.pallas_call(
        functools.partial(head_body, len(stale), img_rows, others, untouched),
        grid_spec=pltpu.PrefetchScalarGridSpec(
            num_scalar_prefetch=1,
            grid=(1,),
            in_specs=in_specs,
            out_specs=[pl.BlockSpec(qkv.shape[:2] + (HD,), lambda n, info: (0, 0, place))]
            + [anywhere] * len(passing),
            scratch_shapes=[
                pltpu.VMEM((others,) + block_shape, qkv.dtype),
                pltpu.VMEM((rows, HD), jnp.bfloat16),
                pltpu.VMEM((rows, 2 * HD), jnp.float32),
                pltpu.SMEM((1,), jnp.int32),
            ],
        ),
        out_shape=[jax.ShapeDtypeStruct(qkv.shape[:2] + (places * HD,), qkv.dtype)]
        + [jax.ShapeDtypeStruct(array.shape, array.dtype) for array in passing],
        input_output_aliases=aliases,
        compiler_params=params(),
        cost_estimate=attend_cost(rows, keys, 1),
        name="attend_head",
    )(info, *operands)


def most_body(pair, img_rows, sides, info, *refs):
    q_ref, k_ref, v_ref = refs[:3]
    stale = refs[3 : 3 + pair]
    arrived = refs[3 + pair : 3 + pair + sides]
    aug_out, total_out, flag = refs[4 + pair + sides :]
    aug, total = aug_out.at[0], total_out.at[0]
    core = info[0]
    k_img, k_txt = split_rows(k_ref[...], img_rows)
    v_img, v_txt = split_rows(v_ref[...], img_rows)
    q_img, q_txt = split_rows(q_ref[...], img_rows)
    fresh_rows = q_img.shape[0]
    group_rows = fresh_rows // pair
    rows = fresh_rows + q_txt.shape[0]

    def queries_at(span):
        if span.stop <= fresh_rows:
            return q_img[span, :]
        return q_txt[span.start - fresh_rows : span.stop - fresh_rows, :]

    def own_sets():
        sets = []
        for group in range(pair):
            span = slice(group * group_rows, (group + 1) * group_rows)
            key_rows, values = [k_txt, k_img[span, :]], [v_txt, v_img[span, :]]
            if pair == 2:
                mine = core == group
                key_rows.append(jnp.where(mine, stale[1][0], stale[0][0]))
                values.append(jnp.where(mine, stale[1][1], stale[0][1]))
            sets.append((span, key_rows, values))
        sets.append(
            (
                slice(fresh_rows, rows),
                [k_txt] + [block[0] for block in stale],
                [v_txt] + [block[1] for block in stale],
            )
        )
        for span, key_rows, values in sets:
            key_rows, values = jnp.concatenate(key_rows, 0), jnp.concatenate(values, 0)
            spans = [
                slice(span.start + t.start, span.start + t.stop)
                for t in tiles_of(span.stop - span.start)
            ]
            yield spans, key_rows, values

    def each_arrived(act):
        for side in range(sides):
            block = arrived[side]

            @pl.when(info[1 + side] == 1)
            def _():
                key_rows, values = block[0], block[1]
                for first in range(0, rows, fresh_rows):
                    for tile in tiles_of(min(fresh_rows, rows - first)):
                        act(slice(first + tile.start, first + tile.stop), key_rows, values)

    def largest(span, key_rows):
        return jnp.max(dot(queries_at(span), key_rows, (1, 1)), axis=1, keepdims=True)

    def attempt(turn):
        @pl.when(turn == 0)
        def _():
            for spans, key_rows, _ in own_sets():
                for span in spans:
                    aug[span, :] = reference_columns(
                        largest(span, key_rows[: min(256, key_rows.shape[0]), :])
                    )

        @pl.when(turn == 1)
        def _():
            def raise_to(span, key_rows, _):
                total[span, :] = jnp.maximum(
                    total[span, :], jnp.broadcast_to(largest(span, key_rows), total[span, :].shape)
                )

            for spans, key_rows, _ in own_sets():
                for span in spans:
                    total[span, :] = jnp.broadcast_to(
                        largest(span, key_rows), total[span, :].shape
                    )
            each_arrived(raise_to)
            for spans, _, _ in own_sets():
                for span in spans:
                    aug[span, :] = reference_columns(total[span, :1])

        def queries_of(span):
            return jnp.concatenate([queries_at(span), aug[span, :]], axis=1)

        def add(span, key_rows, values):
            total[span, :] += weighted(queries_of(span), with_ones(key_rows), with_ones(values))

        for spans, key_rows, values in own_sets():
            key_rows, values = with_ones(key_rows), with_ones(values)
            for span in spans:
                total[span, :] = weighted(queries_of(span), key_rows, values)
        each_arrived(add)

    until_small(flag, total, attempt)


def one_spec(shape, block=0):
    return pl.BlockSpec(
        shape, lambda n, info: (0, 0, block), pipeline_mode=pl.Buffered(buffer_count=1)
    )


def attend_most(info, qkv, img_rows, stale, arrived, head, after):
    heads = qkv.shape[2] // (3 * HD)
    rows = qkv.shape[0] * qkv.shape[1]
    shapes = [
        jax.ShapeDtypeStruct((1, rows, HD), jnp.bfloat16),
        jax.ShapeDtypeStruct((1, rows, 2 * HD), jnp.float32),
    ]
    in_specs = [one_spec(qkv.shape[:2] + (HD,), part * heads + head) for part in range(3)]
    in_specs += [one_spec(block.shape[:2] + (HD,), head) for block in stale]
    in_specs += [one_spec(block.shape) for block in arrived]
    in_specs += [pl.BlockSpec(memory_space=pl.ANY)]
    keys = sum(block.shape[1] for block in arrived) // 2 + rows
    return pl.pallas_call(
        functools.partial(most_body, len(stale), img_rows, len(arrived)),
        grid_spec=pltpu.PrefetchScalarGridSpec(
            num_scalar_prefetch=1,
            grid=(1,),
            in_specs=in_specs,
            out_specs=[one_spec(shape.shape) for shape in shapes],
            scratch_shapes=[pltpu.SMEM((1,), jnp.int32)],
        ),
        out_shape=shapes,
        compiler_params=params(),
        cost_estimate=attend_cost(rows, keys, 1),
        name="attend_most",
    )(info, *[qkv] * 3, *stale, *arrived, after)


def last_body(img_rows, sides, info, *refs):
    q_ref, aug_ref, total_ref = refs[:3]
    arrived = refs[3 : 3 + sides]
    out, total, shift, flag = refs[3 + sides :]
    q_img, q_txt = split_rows(q_ref[...], img_rows)
    fresh_rows = q_img.shape[0]
    rows = total.shape[0]

    def queries_at(span):
        if span.stop <= fresh_rows:
            queries = q_img[span, :]
        else:
            queries = q_txt[span.start - fresh_rows : span.stop - fresh_rows, :]
        return jnp.concatenate([queries, aug_ref[0, span, :]], axis=1)

    def each_arrived(act):
        for side in range(sides):
            block = arrived[side]

            @pl.when(info[1 + side] == 1)
            def _():
                key_rows, values = with_ones(block[0]), with_ones(block[1])
                for first, last in ((0, fresh_rows), (fresh_rows, rows)):
                    for tile in tiles_of(last - first):
                        act(slice(first + tile.start, first + tile.stop), key_rows, values)

    def add(span, key_rows, values):
        total[span, :] += weighted(queries_at(span), key_rows, values)

    def raise_to(span, key_rows, _):
        above = jnp.max(dot(queries_at(span), key_rows, (1, 1)), axis=1, keepdims=True)
        shift[span, :] = jnp.maximum(shift[span, :], jnp.broadcast_to(above, shift[span, :].shape))

    def add_shifted(span, key_rows, values):
        scores = dot(queries_at(span), key_rows, (1, 1)) - shift[span, :1]
        total[span, :] += dot(jnp.exp2(scores * SCALE).astype(jnp.bfloat16), values, (1, 0))

    def attempt(turn):
        @pl.when(turn == 0)
        def _():
            total[...] = total_ref[0]
            each_arrived(add)

        @pl.when(turn == 1)
        def _():
            shift[...] = jnp.zeros_like(shift)
            each_arrived(raise_to)
            keep = jnp.exp2(shift[...] * -SCALE)
            total[...] = total_ref[0] * jnp.concatenate([keep, keep], axis=1)
            each_arrived(add_shifted)

    until_small(flag, total, attempt)
    attended = (total[:, :HD] / total[:, HD:]).astype(out.dtype)
    destinations = out.shape[0]
    out[:, :img_rows, :] = attended[:fresh_rows].reshape(destinations, img_rows, HD)
    out[:, img_rows:, :] = attended[fresh_rows:].reshape(destinations, -1, HD)


def attend_last(info, qkv, img_rows, state, arrived, head):
    rows = qkv.shape[0] * qkv.shape[1]
    return pl.pallas_call(
        functools.partial(last_body, img_rows, len(arrived)),
        grid_spec=pltpu.PrefetchScalarGridSpec(
            num_scalar_prefetch=1,
            grid=(1,),
            in_specs=[one_spec(qkv.shape[:2] + (HD,), head)]
            + [one_spec(part.shape) for part in state]
            + [one_spec(block.shape) for block in arrived],
            out_specs=one_spec(qkv.shape[:2] + (HD,)),
            scratch_shapes=[
                pltpu.VMEM((rows, 2 * HD), jnp.float32),
                pltpu.VMEM((rows, HD), jnp.float32),
                pltpu.SMEM((1,), jnp.int32),
            ],
        ),
        out_shape=jax.ShapeDtypeStruct(qkv.shape[:2] + (HD,), qkv.dtype),
        compiler_params=params(),
        cost_estimate=attend_cost(rows, arrived[0].shape[1], 1),
        name="attend_last",
    )(info, qkv, *state, *arrived)


def project_body(order, first_head, heads, group, last, *refs):
    if last:
        x_ref, weight, residual, gate, earlier, out, flat, held, total, sems = refs
    else:
        x_ref, weight, out, flat, held, total, sems = refs
    chunks = weight.shape[0] // group
    copies = [
        pltpu.make_async_copy(
            weight.at[pl.ds(chunk * group, group), pl.ds(first_head, heads)],
            held.at[pl.ds(chunk * group, group)],
            sems.at[chunk],
        )
        for chunk in range(chunks)
    ]
    for copy in copies:
        copy.start()
    rows, width = flat.shape[0], x_ref.shape[2]
    for source, place in enumerate(order):
        flat[:, place * width : (place + 1) * width] = x_ref[source, :rows, :]
    depth = group * width
    for chunk, copy in enumerate(copies):
        copy.wait()
        block = held[chunk * group : (chunk + 1) * group].reshape(depth, held.shape[3])
        part = jnp.dot(
            flat[:, chunk * depth : (chunk + 1) * depth], block, preferred_element_type=jnp.float32
        )
        if chunk == 0:
            total[...] = part
        else:
            total[...] += part
    if last:
        projected = earlier[...] + total[...]
        out[...] = (residual[...].astype(jnp.float32) + gate[...] * projected).astype(out.dtype)
    else:
        out[...] = total[...]


def project(x, order, weight, first_head, rows, final=None):
    destinations, model = weight.shape[0], weight.shape[3]
    heads = x.shape[2] // HD
    group = 2 if heads % 2 and destinations % 2 == 0 else 1
    operands = [x, weight]
    in_specs = [pl.BlockSpec(memory_space=pltpu.VMEM), pl.BlockSpec(memory_space=pl.ANY)]
    if final is not None:
        residual, gate, earlier = final
        operands += [residual, gate.reshape(1, model), earlier]
        in_specs += [pl.BlockSpec(memory_space=pltpu.VMEM)] * 3
    depth = x.shape[0] * x.shape[2]
    return pl.pallas_call(
        functools.partial(project_body, order, first_head, heads, group, final is not None),
        in_specs=in_specs,
        out_specs=pl.BlockSpec(memory_space=pltpu.VMEM),
        out_shape=jax.ShapeDtypeStruct(
            (rows, model), jnp.float32 if final is None else residual.dtype
        ),
        scratch_shapes=[
            pltpu.VMEM((rows, depth), x.dtype),
            pltpu.VMEM((destinations, heads, HD, model), weight.dtype),
            pltpu.VMEM((rows, model), jnp.float32),
            pltpu.SemaphoreType.DMA((destinations // group,)),
        ],
        compiler_params=pltpu.CompilerParams(vmem_limit_bytes=WIDE_LIMIT),
        cost_estimate=pl.CostEstimate(
            flops=2 * rows * model * depth, bytes_accessed=2 * model * depth, transcendentals=0
        ),
        name="project_last" if final is not None else "project_early",
    )(*operands)


def unpack_body(order, first, heads, *refs):
    sources, out = refs[:-1], refs[-1]
    for source, place in enumerate(order):
        at = place * heads * HD
        for x_ref in sources:
            width = x_ref.shape[2]
            out[:, at : at + width] = x_ref[source, first:, :]
            at += width


def unpack_text(parts, order, first):
    heads = sum(x.shape[2] for x in parts) // HD
    rows, model = parts[0].shape[1] - first, parts[0].shape[0] * heads * HD
    return pl.pallas_call(
        functools.partial(unpack_body, order, first, heads),
        grid=(1,),
        in_specs=[pl.BlockSpec(x.shape, lambda n: (0, 0, 0)) for x in parts],
        out_specs=pl.BlockSpec((rows, model), lambda n: (0, 0)),
        out_shape=jax.ShapeDtypeStruct((rows, model), parts[0].dtype),
        compiler_params=params(),
        name="unpack_text",
    )(*parts)


def per_device(img_qkv, txt_qkv, stale_kv, residual, gate_scale, proj_weight):
    patches, head_owners = lax.axis_size("patch"), lax.axis_size("head")
    patch = lax.axis_index("patch")
    owned_heads = stale_kv.shape[2] // HD
    pair = 2 if patches % 2 == 0 and owned_heads % 2 == 0 else 1
    planes = patches // pair
    plane, core = patch // pair, patch % pair
    width = stale_kv.shape[2] // pair
    heads = width // HD
    img_rows, model = residual.shape
    text_rows = txt_qkv.shape[0] // pair
    destinations = pair * head_owners

    def column_block(d):
        return (d % head_owners) * pair + d // head_owners

    order = [column_block(d) for d in range(destinations)]
    groups = [[g * destinations + d for d in range(destinations)] for g in range(planes)]

    def exchange(x):
        return lax.all_to_all(
            x, ("patch", "head"), split_axis=0, concat_axis=0, axis_index_groups=groups, tiled=True
        )

    swap_pairs = [(p, p + 1 - 2 * (p % 2)) for p in range(patches)]
    stale = [lax.dynamic_slice_in_dim(stale_kv, core * width, width, 2)]
    if pair == 2:
        theirs = lax.dynamic_slice_in_dim(stale_kv, (1 - core) * width, width, 2)
        stale.append(lax.ppermute(theirs, "patch", swap_pairs))

    core_only = core.astype(jnp.int32).reshape(1)
    qkv = exchange(pack(core_only, img_qkv, txt_qkv, text_rows, order, width))

    def relay(left, right, step):
        right_pairs = [(p, p + pair) for p in range((step - 1) * pair, patches - pair)]
        left_pairs = [(p + pair, p) for p in range(0, patches - step * pair)]
        return lax.ppermute(left, "patch", right_pairs), lax.ppermute(right, "patch", left_pairs)

    came = []
    for head in range(heads):
        own = jnp.concatenate([block[:, :, head * HD : (head + 1) * HD] for block in stale], axis=1)
        steps, held = [], (own, own)
        for step in range(1, planes - (head == heads - 1)):
            held = relay(*held, step)
            steps.append(held)
        came.append(steps)

    info = jnp.stack([core] + [plane >= step for step in range(1, planes)]).astype(jnp.int32)
    early = None
    for head in range(heads - 1):
        left, right = zip(*came[head])
        arrived = list(zip(left, reversed(right)))
        passing = came[-1][-1] if head == 0 else ()
        early, *passed = attend_head(
            info, qkv, img_rows, stale, arrived, head, head, heads - 1, early, passing
        )
        if passing:
            came[-1][-1] = tuple(passed)
    last = relay(*came[-1][-1], planes - 1)
    there = [(plane >= step, plane + step < planes) for step in range(1, planes)]
    info = jnp.stack([core] + [flag for both in there[:-1] for flag in both]).astype(jnp.int32)
    state = attend_most(
        info, qkv, img_rows, stale, [block for both in came[-1] for block in both], heads - 1, early
    )
    info = jnp.stack([core, *there[-1]]).astype(jnp.int32)
    late = exchange(attend_last(info, qkv, img_rows, state, last, heads - 1))
    early = exchange(early)
    weight = proj_weight.reshape(destinations, heads, HD, model)

    text_out = unpack_text([early, late], order, img_rows)
    if pair == 2:
        other = lax.ppermute(text_out, "patch", swap_pairs)
        lower = core == 0
        text_out = jnp.concatenate(
            [jnp.where(lower, text_out, other), jnp.where(lower, other, text_out)], 0
        )
    partial = project(early, order, weight, 0, img_rows)
    image_out = project(
        late, order, weight, heads - 1, img_rows, (residual, gate_scale, partial)
    )
    return (image_out, text_out)


def solution(mesh):
    return jax.shard_map(
        per_device,
        mesh=mesh,
        in_specs=(
            P(("patch", "head"), None),
            P("head", None),
            P(None, "patch", "head"),
            P(("patch", "head"), None),
            P(),
            P(),
        ),
        out_specs=(P(("patch", "head"), None), P("head", None)),
        check_vma=False,
    )
```

```python
import functools
import math

import jax
import jax.numpy as jnp
from jax import lax
from jax.experimental import pallas as pl
from jax.experimental.pallas import tpu as pltpu
from jax.sharding import PartitionSpec as P

HD = 128
SCALE = math.log2(math.e) / math.sqrt(HD)
VMEM_LIMIT = 12 * 1024 * 1024
WIDE_LIMIT = 48 * 1024 * 1024
TILE = 512
FIRST_KEYS = 256
LARGE = 2.0**60


def params(block_elements=0):
    return pltpu.CompilerParams(
        vmem_limit_bytes=VMEM_LIMIT + 4 * block_elements, dimension_semantics=("arbitrary",)
    )


def pack_body(text_rows, places, width, core, img, txt, packed, sem):
    img_rows, model = img.shape[0], img.shape[1] // 3
    first = pl.multiple_of(core[0] * text_rows, text_rows)
    copies = []
    for destination, place in enumerate(places):
        for part in range(3):
            source = pl.ds(part * model + place * width, width)
            target = pl.ds(part * width, width)
            copies.append((img.at[:, source], packed.at[destination, pl.ds(0, img_rows), target]))
            copies.append(
                (
                    txt.at[pl.ds(first, text_rows), source],
                    packed.at[destination, pl.ds(img_rows, text_rows), target],
                )
            )
    copies = [
        pltpu.make_async_copy(source, target, sem.at[index])
        for index, (source, target) in enumerate(copies)
    ]
    for copy in copies:
        copy.start()
    for copy in copies:
        copy.wait()


def pack(core, img_qkv, txt_qkv, text_rows, places, width):
    rows = img_qkv.shape[0] + text_rows
    anywhere = pl.BlockSpec(memory_space=pl.ANY)
    return pl.pallas_call(
        functools.partial(pack_body, text_rows, places, width),
        in_specs=[pl.BlockSpec(memory_space=pltpu.SMEM), anywhere, anywhere],
        out_specs=anywhere,
        out_shape=jax.ShapeDtypeStruct((len(places), rows, 3 * width), img_qkv.dtype),
        scratch_shapes=[pltpu.SemaphoreType.DMA((6 * len(places),))],
        compiler_params=pltpu.CompilerParams(vmem_limit_bytes=WIDE_LIMIT),
        name="pack_heads",
    )(core, img_qkv, txt_qkv)


def dot(first, second, contract):
    return lax.dot_general(
        first, second, ((contract[:1], contract[1:]), ((), ())), preferred_element_type=jnp.float32
    )


def with_ones(block):
    return jnp.concatenate([block, jnp.ones_like(block)], axis=1)


def reference_columns(row_max):
    reference = row_max.astype(jnp.bfloat16).astype(jnp.float32)
    return jnp.broadcast_to(reference * (-1.0 / HD), (row_max.shape[0], HD)).astype(jnp.bfloat16)


def weighted(queries, key_rows, values):
    weights = jnp.exp2(dot(queries, key_rows, (1, 1)) * SCALE).astype(jnp.bfloat16)
    return dot(weights, values, (1, 0))


def tiles_of(rows):
    tile = min(TILE, rows)
    return [slice(first, min(first + tile, rows)) for first in range(0, rows, tile)]


def until_small(flag, total, attempt):
    flag[0] = 1

    @pl.loop(0, 2)
    def _(turn):
        @pl.when(flag[0] == 1)
        def _():
            attempt(turn)
            flag[0] = jnp.where(jnp.max(total[:, HD:]) > LARGE, 1, 0).astype(jnp.int32)


class Sides:
    def __init__(self, sides, heads):
        self.operands, self.specs, self.counts = [], [], []
        for blocks, by_core in sides:
            self.counts.append(len(blocks))
            for block in blocks:
                self.operands.append(block)
                self.specs.append(stale_spec(block, heads, by_core))

    def each(self, info, refs, act):
        for index, count in enumerate(self.counts):
            blocks, refs = refs[:count], refs[count:]

            @pl.when(info[1 + index] == 1)
            def _():
                act(
                    jnp.concatenate([block[0] for block in blocks], 0),
                    jnp.concatenate([block[1] for block in blocks], 0),
                )


def stale_spec(block, heads, by_core):
    shape = (2, block.shape[1], HD)
    if by_core:
        return pl.BlockSpec(shape, lambda h, info: (0, 0, info[0] * heads + h))
    return pl.BlockSpec(shape, lambda h, info: (0, 0, h))


def column_spec(shape, offset=0):
    return pl.BlockSpec(shape[:2] + (HD,), lambda h, info: (0, 0, offset + h))


def head_spec(shape):
    return pl.BlockSpec((1,) + shape[1:], lambda h, info: (h, 0, 0))


def accumulate(flag, total, aug, shift, queries, first_keys, own, each_arrived):
    rows = total.shape[0]

    def scored(span, key_rows):
        return dot(queries[span, :], key_rows, (1, 1))

    def raise_to(span, key_rows):
        row_max = jnp.max(scored(span, key_rows), axis=1, keepdims=True)
        shift[span, :] = jnp.maximum(shift[span, :], jnp.broadcast_to(row_max, shift[span, :].shape))

    def attempt(turn):
        @pl.when(turn == 0)
        def _():
            for tile in tiles_of(rows):
                row_max = jnp.max(scored(tile, first_keys), axis=1, keepdims=True)
                aug[tile, :] = reference_columns(row_max)

        @pl.when(turn == 1)
        def _():
            shift[...] = jnp.full_like(shift, -jnp.inf)
            for span, key_rows, _ in own:
                raise_to(span, key_rows)
            each_arrived(lambda key_rows, _: raise_to(slice(0, rows), key_rows))
            aug[...] = reference_columns(shift[:, :1])

        def add(span, key_rows, values):
            both = jnp.concatenate([queries[span, :], aug[span, :]], axis=1)
            total[span, :] += weighted(both, with_ones(key_rows), with_ones(values))

        total[...] = jnp.zeros_like(total)
        for span, key_rows, values in own:
            add(span, key_rows, values)

        def add_everywhere(key_rows, values):
            for tile in tiles_of(rows):
                add(tile, key_rows, values)

        each_arrived(add_everywhere)

    until_small(flag, total, attempt)


def rows_of(block, first, last):
    return block[:, first:last, :].reshape(-1, HD)


def text_body(pair, img_rows, sides, wanted, info, *refs):
    q_ref, k_ref, v_ref = refs[:3]
    stale, arrived = refs[3 : 3 + pair], refs[3 + pair : 3 + pair + len(sides.operands)]
    out, aug, total, shift, flag = refs[3 + pair + len(sides.operands) :]

    @pl.when(info[wanted] == 1)
    def _():
        rows = total.shape[0]
        last = q_ref.shape[1]
        queries = rows_of(q_ref[...], img_rows, last)
        text_keys = rows_of(k_ref[...], img_rows, last)
        text_values = rows_of(v_ref[...], img_rows, last)
        everywhere = slice(0, rows)
        own = [
            (everywhere, text_keys, text_values),
            (
                everywhere,
                jnp.concatenate([block[0] for block in stale], 0),
                jnp.concatenate([block[1] for block in stale], 0),
            ),
        ]
        accumulate(
            flag, total, aug, shift, queries, text_keys[: min(FIRST_KEYS, rows), :], own,
            functools.partial(sides.each, info, arrived),
        )
        attended = (total[:, :HD] / total[:, HD:]).astype(out.dtype)
        out[...] = attended.reshape(out.shape)


def image_body(pair, img_rows, sides, info, *refs):
    q_ref, k_ref, v_ref = refs[:3]
    stale, arrived = refs[3 : 3 + pair], refs[3 + pair : 3 + pair + len(sides.operands)]
    aug, total, shift, flag = refs[4 + pair + len(sides.operands) :]
    aug, total = aug.at[0], total.at[0]
    rows = total.shape[0]
    last = q_ref.shape[1]
    core = info[0]
    queries = rows_of(q_ref[...], 0, img_rows)
    img_keys, img_values = rows_of(k_ref[...], 0, img_rows), rows_of(v_ref[...], 0, img_rows)
    text_keys = rows_of(k_ref[...], img_rows, last)
    text_values = rows_of(v_ref[...], img_rows, last)
    group_rows = rows // pair
    own = [(slice(0, rows), text_keys, text_values)]
    for group in range(pair):
        span = slice(group * group_rows, (group + 1) * group_rows)
        key_rows, values = [img_keys[span, :]], [img_values[span, :]]
        if pair == 2:
            mine = core == group
            key_rows.append(jnp.where(mine, stale[1][0], stale[0][0]))
            values.append(jnp.where(mine, stale[1][1], stale[0][1]))
        own.append((span, jnp.concatenate(key_rows, 0), jnp.concatenate(values, 0)))
    accumulate(
        flag, total, aug, shift, queries,
        text_keys[: min(FIRST_KEYS, text_keys.shape[0]), :], own,
        functools.partial(sides.each, info, arrived),
    )


def last_body(img_rows, sides, info, *refs):
    q_ref, aug_ref, total_ref = refs[:3]
    arrived = refs[3 : 3 + len(sides.operands)]
    out, total, shift, flag = refs[4 + len(sides.operands) :]
    rows = total.shape[0]
    queries = rows_of(q_ref[...], 0, img_rows)
    each_arrived = functools.partial(sides.each, info, arrived)

    def referred(span, key_rows):
        both = jnp.concatenate([queries[span, :], aug_ref[0, span, :]], axis=1)
        return dot(both, with_ones(key_rows), (1, 1))

    def add(key_rows, values):
        for tile in tiles_of(rows):
            weights = jnp.exp2(referred(tile, key_rows) * SCALE).astype(jnp.bfloat16)
            total[tile, :] += dot(weights, with_ones(values), (1, 0))

    def raise_to(key_rows, _):
        above = jnp.max(referred(slice(0, rows), key_rows), axis=1, keepdims=True)
        shift[...] = jnp.maximum(shift[...], jnp.broadcast_to(above, shift.shape))

    def add_shifted(key_rows, values):
        scores = referred(slice(0, rows), key_rows) - shift[:, :1]
        weights = jnp.exp2(scores * SCALE).astype(jnp.bfloat16)
        total[...] += dot(weights, with_ones(values), (1, 0))

    def attempt(turn):
        @pl.when(turn == 0)
        def _():
            total[...] = total_ref[0]
            each_arrived(add)

        @pl.when(turn == 1)
        def _():
            shift[...] = jnp.zeros_like(shift)
            each_arrived(raise_to)
            keep = jnp.exp2(shift[...] * -SCALE)
            total[...] = total_ref[0] * jnp.concatenate([keep, keep], axis=1)
            each_arrived(add_shifted)

    until_small(flag, total, attempt)
    attended = (total[:, :HD] / total[:, HD:]).astype(out.dtype)
    out[...] = attended.reshape(out.shape)


def attend_cost(queries, keys, heads):
    return pl.CostEstimate(
        flops=4 * queries * keys * heads * HD,
        bytes_accessed=4 * queries * heads * HD + 4 * keys * heads * HD,
        transcendentals=queries * keys * heads,
    )


def call_heads(body, name, heads, info, operands, specs, outs, out_specs, scratch, cost):
    return pl.pallas_call(
        body,
        grid_spec=pltpu.PrefetchScalarGridSpec(
            num_scalar_prefetch=1,
            grid=(heads,),
            in_specs=specs,
            out_specs=out_specs,
            scratch_shapes=scratch,
        ),
        out_shape=outs,
        compiler_params=params(
            sum(math.prod(spec.block_shape) for spec in specs if spec.block_shape is not None)
        ),
        cost_estimate=cost,
        name=name,
    )(info, *operands)


def common(qkv, stale, heads, sides):
    operands = [qkv] * 3 + list(stale) + sides.operands
    specs = [column_spec(qkv.shape, part * heads) for part in range(3)]
    specs += [stale_spec(block, heads, len(stale) > 1) for block in stale] + sides.specs
    return operands, specs


def scratch_of(rows):
    return [pltpu.VMEM((rows, HD), jnp.float32), pltpu.SMEM((1,), jnp.int32)]


def attend_text(info, wanted, qkv, img_rows, stale, sides):
    heads = qkv.shape[2] // (3 * HD)
    sides = Sides(sides, heads)
    operands, specs = common(qkv, stale, heads, sides)
    text_rows = qkv.shape[1] - img_rows
    rows = qkv.shape[0] * text_rows
    out = jax.ShapeDtypeStruct((qkv.shape[0], text_rows, heads * HD), qkv.dtype)
    return call_heads(
        functools.partial(text_body, len(stale), img_rows, sides, wanted),
        "attend_text", heads, info, operands, specs, out, column_spec(out.shape),
        [pltpu.VMEM((rows, HD), jnp.bfloat16), pltpu.VMEM((rows, 2 * HD), jnp.float32)]
        + scratch_of(rows),
        attend_cost(rows, 4 * rows, heads),
    )


def attend_image(info, qkv, img_rows, stale, sides, after):
    heads = qkv.shape[2] // (3 * HD)
    sides = Sides(sides, heads)
    operands, specs = common(qkv, stale, heads, sides)
    rows = qkv.shape[0] * img_rows
    outs = [
        jax.ShapeDtypeStruct((heads, rows, HD), jnp.bfloat16),
        jax.ShapeDtypeStruct((heads, rows, 2 * HD), jnp.float32),
    ]
    return call_heads(
        functools.partial(image_body, len(stale), img_rows, sides),
        "attend_image", heads, info, operands + [after],
        specs + [pl.BlockSpec(memory_space=pl.ANY)], outs,
        [head_spec(out.shape) for out in outs], scratch_of(rows),
        attend_cost(rows, 4 * rows, heads),
    )


def attend_last(info, qkv, img_rows, state, sides, after):
    heads = qkv.shape[2] // (3 * HD)
    sides = Sides(sides, heads)
    rows = qkv.shape[0] * img_rows
    out = jax.ShapeDtypeStruct((qkv.shape[0], img_rows, heads * HD), qkv.dtype)
    specs = [column_spec(qkv.shape)] + [head_spec(part.shape) for part in state] + sides.specs
    return call_heads(
        functools.partial(last_body, img_rows, sides),
        "attend_last", heads, info, [qkv, *state] + sides.operands + [after],
        specs + [pl.BlockSpec(memory_space=pl.ANY)], out, column_spec(out.shape),
        [pltpu.VMEM((rows, 2 * HD), jnp.float32)] + scratch_of(rows),
        attend_cost(rows, rows, heads),
    )


def project_body(order, x_ref, weight, residual, gate, out, held, total, sems):
    copies = [
        pltpu.make_async_copy(weight.at[place], held.at[place], sems.at[place])
        for place in order
    ]
    for copy in copies:
        copy.start()
    for source, (place, copy) in enumerate(zip(order, copies)):
        copy.wait()
        part = jnp.dot(x_ref[source], held[place], preferred_element_type=jnp.float32)
        if source == 0:
            total[...] = part
        else:
            total[...] += part
    out[...] = (residual[...].astype(jnp.float32) + gate[...] * total[...]).astype(out.dtype)


def project(x, order, weight, residual, gate):
    rows, model = residual.shape
    destinations, _, width = x.shape
    vmem = pl.BlockSpec(memory_space=pltpu.VMEM)
    return pl.pallas_call(
        functools.partial(project_body, order),
        in_specs=[vmem, pl.BlockSpec(memory_space=pl.ANY), vmem, vmem],
        out_specs=vmem,
        out_shape=jax.ShapeDtypeStruct((rows, model), residual.dtype),
        scratch_shapes=[
            pltpu.VMEM((destinations, width, model), weight.dtype),
            pltpu.VMEM((rows, model), jnp.float32),
            pltpu.SemaphoreType.DMA((destinations,)),
        ],
        compiler_params=pltpu.CompilerParams(vmem_limit_bytes=WIDE_LIMIT),
        cost_estimate=pl.CostEstimate(
            flops=2 * rows * model * model, bytes_accessed=2 * model * model, transcendentals=0
        ),
        name="project",
    )(x, weight.reshape(destinations, width, model), residual, gate.reshape(1, model))


def unpack_body(order, x_ref, out):
    width = x_ref.shape[2]
    for source, place in enumerate(order):
        out[:, place * width : (place + 1) * width] = x_ref[source]


def unpack(x, order):
    rows, model = x.shape[1], x.shape[0] * x.shape[2]
    return pl.pallas_call(
        functools.partial(unpack_body, order),
        grid=(1,),
        in_specs=[pl.BlockSpec(x.shape, lambda n: (0, 0, 0))],
        out_specs=pl.BlockSpec((rows, model), lambda n: (0, 0)),
        out_shape=jax.ShapeDtypeStruct((rows, model), x.dtype),
        compiler_params=params(),
        name="unpack_text",
    )(x)


def per_device(img_qkv, txt_qkv, stale_kv, residual, gate_scale, proj_weight):
    patches, head_owners = lax.axis_size("patch"), lax.axis_size("head")
    patch = lax.axis_index("patch")
    owned_heads = stale_kv.shape[2] // HD
    pair = 2 if patches % 2 == 0 and owned_heads % 2 == 0 else 1
    planes = patches // pair
    plane, core = patch // pair, patch % pair
    width = stale_kv.shape[2] // pair
    heads = width // HD
    img_rows, model = residual.shape
    text_rows = txt_qkv.shape[0] // pair
    destinations = pair * head_owners

    order = [(d % head_owners) * pair + d // head_owners for d in range(destinations)]
    groups = [[g * destinations + d for d in range(destinations)] for g in range(planes)]
    swap_pairs = [(p, p + 1 - 2 * (p % 2)) for p in range(patches)]

    def exchange(x):
        return lax.all_to_all(
            x, ("patch", "head"), split_axis=0, concat_axis=0, axis_index_groups=groups, tiled=True
        )

    def swap(x):
        return lax.ppermute(x, "patch", swap_pairs)

    def up_pairs(step):
        return [(z, z + 1) for z in range(step - 1, planes - 1)]

    def down_pairs(step):
        return [(z + 1, z) for z in range(0, planes - step)]

    core_only = core.astype(jnp.int32).reshape(1)
    qkv = exchange(pack(core_only, img_qkv, txt_qkv, text_rows, order, width))

    sides, there = [], []
    above = lambda step: plane + step < planes
    below = lambda step: plane >= step
    if pair == 2:
        stale = [stale_kv, swap(stale_kv)]
        held = stale
        for step in range(1, planes):
            pairs = [(2 * a, 2 * b) for a, b in up_pairs(step)]
            pairs += [(2 * a + 1, 2 * b + 1) for a, b in down_pairs(step)]
            held = [lax.ppermute(block, "patch", pairs) for block in held]
            others = [
                swap(lax.dynamic_slice_in_dim(block, (1 - core) * width, width, 2))
                for block in held
            ]
            sides.append([(held, True), (others, False)])
            upward = core == 0
            there.append(
                [
                    jnp.where(upward, below(step), above(step)),
                    jnp.where(upward, above(step), below(step)),
                ]
            )
    else:
        stale = [stale_kv]
        from_below = from_above = stale_kv
        for step in range(1, planes):
            from_below = lax.ppermute(from_below, "patch", up_pairs(step))
            from_above = lax.ppermute(from_above, "patch", down_pairs(step))
            sides.append([([from_below], False), ([from_above], False)])
            there.append([below(step), above(step)])

    early = planes > 2
    inner = (plane > 0) & (plane < planes - 1)
    before = [side for step in sides[:-1] for side in step]
    flags = [flag for step in there[:-1] for flag in step]
    info = jnp.stack([core] + flags + [inner]).astype(jnp.int32)
    last_info = jnp.stack([core] + there[-1]).astype(jnp.int32)

    if early:
        text_attn = attend_text(info, 1 + len(flags), qkv, img_rows, stale, before)
    else:
        all_info = jnp.stack([core] + flags + there[-1] + [core >= 0]).astype(jnp.int32)
        text_attn = attend_text(
            all_info, 3 + len(flags), qkv, img_rows, stale, before + sides[-1]
        )
    state = attend_image(info, qkv, img_rows, stale, before, text_attn)
    text_back = exchange(text_attn)
    image_attn = attend_last(last_info, qkv, img_rows, state, sides[-1], text_back)

    text_out = unpack(text_back, order)
    if early:
        ends = [(1, 0), (planes - 2, planes - 1)]
        ends = [(a * pair + c, b * pair + c) for a, b in ends for c in range(pair)]
        text_out = jnp.where(inner, text_out, lax.ppermute(text_out, "patch", ends))
    if pair == 2:
        other = swap(text_out)
        lower = core == 0
        text_out = jnp.concatenate(
            [jnp.where(lower, text_out, other), jnp.where(lower, other, text_out)], 0
        )

    image_out = project(exchange(image_attn), order, proj_weight, residual, gate_scale)
    return (image_out, text_out)


def solution(mesh):
    return jax.shard_map(
        per_device,
        mesh=mesh,
        in_specs=(
            P(("patch", "head"), None),
            P("head", None),
            P(None, "patch", "head"),
            P(("patch", "head"), None),
            P(),
            P(),
        ),
        out_specs=(P(("patch", "head"), None), P("head", None)),
        check_vma=False,
    )
```

```python
import functools
import math

import jax
import jax.numpy as jnp
from jax import lax
from jax.experimental import pallas as pl
from jax.experimental.pallas import tpu as pltpu
from jax.sharding import PartitionSpec as P

HD = 128
SCALE = math.log2(math.e) / math.sqrt(HD)
VMEM_LIMIT = 12 * 1024 * 1024
WIDE_LIMIT = 60 * 1024 * 1024
TILE = 256
FIRST_KEYS = 256
LARGE = 2.0**60


def params(block_elements=0):
    return pltpu.CompilerParams(
        vmem_limit_bytes=VMEM_LIMIT + 4 * block_elements, dimension_semantics=("arbitrary",)
    )


def pack_body(rows, places, width, first_block, array, *refs):
    packed, sem = refs[-2:]
    model = array.shape[1] // 3
    first = pl.multiple_of(first_block[0] * rows, rows)
    copies = []
    for destination, place in enumerate(places):
        for part in range(3):
            copies.append(
                pltpu.make_async_copy(
                    array.at[pl.ds(first, rows), pl.ds(part * model + place * width, width)],
                    packed.at[destination, :, pl.ds(part * width, width)],
                    sem.at[len(copies)],
                )
            )
    for copy in copies:
        copy.start()
    for copy in copies:
        copy.wait()


def pack(first_block, array, rows, places, width, after=()):
    anywhere = pl.BlockSpec(memory_space=pl.ANY)
    return pl.pallas_call(
        functools.partial(pack_body, rows, places, width),
        in_specs=[pl.BlockSpec(memory_space=pltpu.SMEM)] + [anywhere] * (1 + len(after)),
        out_specs=anywhere,
        out_shape=jax.ShapeDtypeStruct((len(places), rows, 3 * width), array.dtype),
        scratch_shapes=[pltpu.SemaphoreType.DMA((3 * len(places),))],
        compiler_params=pltpu.CompilerParams(vmem_limit_bytes=WIDE_LIMIT),
        name="pack_heads",
    )(first_block, array, *after)


def dot(first, second, contract):
    return lax.dot_general(
        first, second, ((contract[:1], contract[1:]), ((), ())), preferred_element_type=jnp.float32
    )


def with_ones(block):
    return jnp.concatenate([block, jnp.ones_like(block)], axis=1)


def reference_columns(row_max):
    reference = row_max.astype(jnp.bfloat16).astype(jnp.float32)
    return jnp.broadcast_to(reference * (-1.0 / HD), (row_max.shape[0], HD)).astype(jnp.bfloat16)


def weighted(queries, key_rows, values):
    weights = jnp.exp2(dot(queries, key_rows, (1, 1)) * SCALE).astype(jnp.bfloat16)
    return dot(weights, values, (1, 0))


def tiles_of(rows):
    tile = min(TILE, rows)
    return [slice(first, min(first + tile, rows)) for first in range(0, rows, tile)]


def until_small(flag, total, attempt):
    flag[0] = 1

    @pl.loop(0, 2)
    def _(turn):
        @pl.when(flag[0] == 1)
        def _():
            attempt(turn)
            flag[0] = jnp.where(jnp.max(total[:, HD:]) > LARGE, 1, 0).astype(jnp.int32)


class Sides:
    def __init__(self, sides, heads):
        self.operands = [block for blocks in sides for block in blocks]
        self.specs = [stale_spec(block, heads) for block in self.operands]
        self.counts = [len(blocks) for blocks in sides]

    def each(self, info, refs, act):
        for index, count in enumerate(self.counts):
            blocks, refs = refs[:count], refs[count:]

            @pl.when(info[1 + index] == 1)
            def _():
                act(
                    jnp.concatenate([block[0] for block in blocks], 0),
                    jnp.concatenate([block[1] for block in blocks], 0),
                )


def stale_spec(block, heads):
    shape = (2, block.shape[1], HD)
    return pl.BlockSpec(shape, lambda h, info: (0, 0, info[0] * heads + h))


def column_spec(shape, offset=0):
    return pl.BlockSpec(shape[:2] + (HD,), lambda h, info: (0, 0, offset + h))


def accumulate(flag, total, aug, shift, queries, first_keys, own, each_arrived):
    rows = total.shape[0]

    def scored(span, key_rows):
        return dot(queries[span, :], key_rows, (1, 1))

    def raise_to(span, key_rows):
        row_max = jnp.max(scored(span, key_rows), axis=1, keepdims=True)
        shift[span, :] = jnp.maximum(shift[span, :], jnp.broadcast_to(row_max, shift[span, :].shape))

    def attempt(turn):
        @pl.when(turn == 0)
        def _():
            for tile in tiles_of(rows):
                row_max = jnp.max(scored(tile, first_keys), axis=1, keepdims=True)
                aug[tile, :] = reference_columns(row_max)

        @pl.when(turn == 1)
        def _():
            shift[...] = jnp.full_like(shift, -jnp.inf)
            for span, key_rows, _ in own:
                raise_to(span, key_rows)
            each_arrived(lambda key_rows, _: raise_to(slice(0, rows), key_rows))
            aug[...] = reference_columns(shift[:, :1])

        def add(span, key_rows, values):
            both = jnp.concatenate([queries[span, :], aug[span, :]], axis=1)
            total[span, :] += weighted(both, with_ones(key_rows), with_ones(values))

        total[...] = jnp.zeros_like(total)
        for span, key_rows, values in own:
            for tile in tiles_of(span.stop - span.start):
                add(slice(span.start + tile.start, span.start + tile.stop), key_rows, values)

        def add_everywhere(key_rows, values):
            for tile in tiles_of(rows):
                add(tile, key_rows, values)

        each_arrived(add_everywhere)

    until_small(flag, total, attempt)


def flat(block):
    return block[...].reshape(-1, HD)


def text_body(pair, sides, wanted, info, *refs):
    q_ref, k_ref, v_ref = refs[:3]
    stale, arrived = refs[3 : 3 + pair], refs[3 + pair : 3 + pair + len(sides.operands)]
    out, aug, total, shift, flag = refs[3 + pair + len(sides.operands) :]

    @pl.when(info[wanted] == 1)
    def _():
        rows = total.shape[0]
        text_keys, text_values = flat(k_ref), flat(v_ref)
        everywhere = slice(0, rows)
        own = [
            (everywhere, text_keys, text_values),
            (
                everywhere,
                jnp.concatenate([block[0] for block in stale], 0),
                jnp.concatenate([block[1] for block in stale], 0),
            ),
        ]
        accumulate(
            flag, total, aug, shift, flat(q_ref), text_keys[: min(FIRST_KEYS, rows), :], own,
            functools.partial(sides.each, info, arrived),
        )
        attended = (total[:, :HD] / total[:, HD:]).astype(out.dtype)
        out[...] = attended.reshape(out.shape)


def image_body(pair, sides, info, *refs):
    q_ref, k_ref, v_ref, text_k_ref, text_v_ref = refs[:5]
    stale, arrived = refs[5 : 5 + pair], refs[5 + pair : 5 + pair + len(sides.operands)]
    out, aug, total, shift, flag = refs[6 + pair + len(sides.operands) :]
    rows = total.shape[0]
    core = info[0]
    img_keys, img_values = flat(k_ref), flat(v_ref)
    text_keys, text_values = flat(text_k_ref), flat(text_v_ref)
    group_rows = rows // pair
    own = [(slice(0, rows), text_keys, text_values)]
    for group in range(pair):
        span = slice(group * group_rows, (group + 1) * group_rows)
        key_rows, values = [img_keys[span, :]], [img_values[span, :]]
        if pair == 2:
            mine = core == group
            key_rows.append(jnp.where(mine, stale[1][0], stale[0][0]))
            values.append(jnp.where(mine, stale[1][1], stale[0][1]))
        own.append((span, jnp.concatenate(key_rows, 0), jnp.concatenate(values, 0)))
    accumulate(
        flag, total, aug, shift, flat(q_ref),
        text_keys[: min(FIRST_KEYS, text_keys.shape[0]), :], own,
        functools.partial(sides.each, info, arrived),
    )
    attended = (total[:, :HD] / total[:, HD:]).astype(out.dtype)
    out[...] = attended.reshape(out.shape)


def attend_cost(queries, keys, heads):
    return pl.CostEstimate(
        flops=4 * queries * keys * heads * HD,
        bytes_accessed=4 * queries * heads * HD + 4 * keys * heads * HD,
        transcendentals=queries * keys * heads,
    )


def call_heads(body, name, heads, info, operands, specs, outs, out_specs, scratch, cost):
    return pl.pallas_call(
        body,
        grid_spec=pltpu.PrefetchScalarGridSpec(
            num_scalar_prefetch=1,
            grid=(heads,),
            in_specs=specs,
            out_specs=out_specs,
            scratch_shapes=scratch,
        ),
        out_shape=outs,
        compiler_params=params(
            sum(math.prod(spec.block_shape) for spec in specs if spec.block_shape is not None)
        ),
        cost_estimate=cost,
        name=name,
    )(info, *operands)


def scratch_of(rows):
    return [
        pltpu.VMEM((rows, HD), jnp.bfloat16),
        pltpu.VMEM((rows, 2 * HD), jnp.float32),
        pltpu.VMEM((rows, HD), jnp.float32),
        pltpu.SMEM((1,), jnp.int32),
    ]


def attend_text(info, wanted, txt, stale, sides):
    heads = txt.shape[2] // (3 * HD)
    sides = Sides(sides, heads)
    rows = txt.shape[0] * txt.shape[1]
    out = jax.ShapeDtypeStruct(txt.shape[:2] + (heads * HD,), txt.dtype)
    return call_heads(
        functools.partial(text_body, len(stale), sides, wanted),
        "attend_text", heads, info, [txt] * 3 + list(stale) + sides.operands,
        [column_spec(txt.shape, part * heads) for part in range(3)]
        + [stale_spec(block, heads) for block in stale]
        + sides.specs,
        out, column_spec(out.shape), scratch_of(rows), attend_cost(rows, 4 * rows, heads),
    )


def attend_image(info, img, txt, stale, sides, after):
    heads = img.shape[2] // (3 * HD)
    sides = Sides(sides, heads)
    rows = img.shape[0] * img.shape[1]
    out = jax.ShapeDtypeStruct(img.shape[:2] + (heads * HD,), img.dtype)
    return call_heads(
        functools.partial(image_body, len(stale), sides),
        "attend_image", heads, info,
        [img] * 3 + [txt] * 2 + list(stale) + sides.operands + [after],
        [column_spec(img.shape, part * heads) for part in range(3)]
        + [column_spec(txt.shape, part * heads) for part in (1, 2)]
        + [stale_spec(block, heads) for block in stale]
        + sides.specs
        + [pl.BlockSpec(memory_space=pl.ANY)],
        out, column_spec(out.shape), scratch_of(rows), attend_cost(rows, 5 * rows, heads),
    )


def project_body(order, x_ref, weight, residual, gate, out, held, total, sems):
    copies = [
        pltpu.make_async_copy(weight.at[place], held.at[place], sems.at[place])
        for place in order
    ]
    for copy in copies:
        copy.start()
    for source, (place, copy) in enumerate(zip(order, copies)):
        copy.wait()
        part = jnp.dot(x_ref[source], held[place], preferred_element_type=jnp.float32)
        if source == 0:
            total[...] = part
        else:
            total[...] += part
    out[...] = (residual[...].astype(jnp.float32) + gate[...] * total[...]).astype(out.dtype)


def project(x, order, weight, residual, gate):
    rows, model = residual.shape
    destinations, _, width = x.shape
    vmem = pl.BlockSpec(memory_space=pltpu.VMEM)
    return pl.pallas_call(
        functools.partial(project_body, order),
        in_specs=[vmem, pl.BlockSpec(memory_space=pl.ANY), vmem, vmem],
        out_specs=vmem,
        out_shape=jax.ShapeDtypeStruct((rows, model), residual.dtype),
        scratch_shapes=[
            pltpu.VMEM((destinations, width, model), weight.dtype),
            pltpu.VMEM((rows, model), jnp.float32),
            pltpu.SemaphoreType.DMA((destinations,)),
        ],
        compiler_params=pltpu.CompilerParams(vmem_limit_bytes=WIDE_LIMIT),
        cost_estimate=pl.CostEstimate(
            flops=2 * rows * model * model, bytes_accessed=2 * model * model, transcendentals=0
        ),
        name="project",
    )(x, weight.reshape(destinations, width, model), residual, gate.reshape(1, model))


def unpack_body(order, x_ref, out):
    width = x_ref.shape[2]
    for source, place in enumerate(order):
        out[:, place * width : (place + 1) * width] = x_ref[source]


def unpack(x, order):
    rows, model = x.shape[1], x.shape[0] * x.shape[2]
    return pl.pallas_call(
        functools.partial(unpack_body, order),
        grid=(1,),
        in_specs=[pl.BlockSpec(x.shape, lambda n: (0, 0, 0))],
        out_specs=pl.BlockSpec((rows, model), lambda n: (0, 0)),
        out_shape=jax.ShapeDtypeStruct((rows, model), x.dtype),
        compiler_params=params(),
        name="unpack_text",
    )(x)


def per_device(img_qkv, txt_qkv, stale_kv, residual, gate_scale, proj_weight):
    patches, head_owners = lax.axis_size("patch"), lax.axis_size("head")
    patch = lax.axis_index("patch")
    owned_heads = stale_kv.shape[2] // HD
    pair = 2 if patches % 2 == 0 and owned_heads % 2 == 0 else 1
    planes = patches // pair
    plane, core = patch // pair, patch % pair
    width = stale_kv.shape[2] // pair
    heads = width // HD
    img_rows, model = residual.shape
    text_rows = txt_qkv.shape[0] // pair
    destinations = pair * head_owners

    order = [(d % head_owners) * pair + d // head_owners for d in range(destinations)]
    groups = [[g * destinations + d for d in range(destinations)] for g in range(planes)]
    swap_pairs = [(p, p + 1 - 2 * (p % 2)) for p in range(patches)]

    def exchange(x):
        return lax.all_to_all(
            x, ("patch", "head"), split_axis=0, concat_axis=0, axis_index_groups=groups, tiled=True
        )

    def swap(x):
        return lax.ppermute(x, "patch", swap_pairs)

    def up_pairs(step):
        return [(z, z + 1) for z in range(step - 1, planes - 1)]

    def down_pairs(step):
        return [(z + 1, z) for z in range(0, planes - step)]

    core_only = core.astype(jnp.int32).reshape(1)
    txt = exchange(pack(core_only, txt_qkv, text_rows, order, width))

    sides, there = [], []
    above = lambda step: plane + step < planes
    below = lambda step: plane >= step
    if pair == 2:
        stale = [stale_kv, swap(stale_kv)]
        held = [stale_kv, stale_kv]
        for step in range(1, planes):
            pairs = [
                [(2 * a + turn, 2 * b) for a, b in up_pairs(step)]
                + [(2 * a + 1 - turn, 2 * b + 1) for a, b in down_pairs(step)]
                for turn in ((0, 1) if step == 1 else (0, 0))
            ]
            held = [lax.ppermute(block, "patch", way) for block, way in zip(held, pairs)]
            sides += [held, [swap(block) for block in held]]
            upward = core == 0
            there += [
                jnp.where(upward, below(step), above(step)),
                jnp.where(upward, above(step), below(step)),
            ]
    else:
        stale = [stale_kv]
        from_below = from_above = stale_kv
        for step in range(1, planes):
            from_below = lax.ppermute(from_below, "patch", up_pairs(step))
            from_above = lax.ppermute(from_above, "patch", down_pairs(step))
            sides += [[from_below], [from_above]]
            there += [below(step), above(step)]
    zero_only = jnp.zeros((1,), jnp.int32)
    img = exchange(pack(zero_only, img_qkv, img_rows, order, width, [txt] + sides[0]))

    early = planes > 2
    inner = (plane > 0) & (plane < planes - 1)
    known = len(sides) - 2 if early else len(sides)
    wanted = inner if early else core >= 0
    info = jnp.stack([core] + there[:known] + [wanted]).astype(jnp.int32)
    text_attn = attend_text(info, 1 + known, txt, stale, sides[:known])
    info = jnp.stack([core] + there).astype(jnp.int32)
    image_attn = attend_image(info, img, txt, stale, sides, text_attn)
    text_back = exchange(text_attn)

    text_out = unpack(text_back, order)
    if early:
        ends = [(1, 0), (planes - 2, planes - 1)]
        ends = [(a * pair + c, b * pair + c) for a, b in ends for c in range(pair)]
        text_out = jnp.where(inner, text_out, lax.ppermute(text_out, "patch", ends))
    if pair == 2:
        other = swap(text_out)
        lower = core == 0
        text_out = jnp.concatenate(
            [jnp.where(lower, text_out, other), jnp.where(lower, other, text_out)], 0
        )

    image_out = project(exchange(image_attn), order, proj_weight, residual, gate_scale)
    return (image_out, text_out)


def solution(mesh):
    return jax.shard_map(
        per_device,
        mesh=mesh,
        in_specs=(
            P(("patch", "head"), None),
            P("head", None),
            P(None, "patch", "head"),
            P(("patch", "head"), None),
            P(),
            P(),
        ),
        out_specs=(P(("patch", "head"), None), P("head", None)),
        check_vma=False,
    )
```

```python
import functools
import math

import jax
import jax.numpy as jnp
from jax import lax
from jax.experimental import pallas as pl
from jax.experimental.pallas import tpu as pltpu
from jax.sharding import PartitionSpec as P

HD = 128
SCALE = math.log2(math.e) / math.sqrt(HD)
VMEM_LIMIT = 12 * 1024 * 1024
WIDE_LIMIT = 48 * 1024 * 1024
TILE = 256
FIRST_KEYS = 256
LARGE = 2.0**60


def params(block_elements=0):
    return pltpu.CompilerParams(
        vmem_limit_bytes=VMEM_LIMIT + 4 * block_elements, dimension_semantics=("arbitrary",)
    )


def pack_body(_, *refs):
    sources, packed = refs[:3], refs[-1]
    width = sources[0].shape[1]
    for part, source in enumerate(sources):
        packed[0, :, part * width : (part + 1) * width] = source[...]


def pack(first_block, array, rows, head_owners, pair, width, after=()):
    blocks = array.shape[1] // 3 // width
    destinations = head_owners * pair

    def source(part):
        def place(d, info):
            return (info[0], part * blocks + (d % head_owners) * pair + d // head_owners)

        return pl.BlockSpec((rows, width), place)

    return pl.pallas_call(
        pack_body,
        grid_spec=pltpu.PrefetchScalarGridSpec(
            num_scalar_prefetch=1,
            grid=(destinations,),
            in_specs=[source(0), source(1), source(2)]
            + [pl.BlockSpec(memory_space=pl.ANY)] * len(after),
            out_specs=pl.BlockSpec((1, rows, 3 * width), lambda d, info: (d, 0, 0)),
        ),
        out_shape=jax.ShapeDtypeStruct((destinations, rows, 3 * width), array.dtype),
        compiler_params=params(),
        name="pack_heads",
    )(first_block, array, array, array, *after)


def dot(first, second, contract):
    return lax.dot_general(
        first, second, ((contract[:1], contract[1:]), ((), ())), preferred_element_type=jnp.float32
    )


def with_ones(block):
    return jnp.concatenate([block, jnp.ones_like(block)], axis=1)


def reference_columns(row_max):
    reference = row_max.astype(jnp.bfloat16).astype(jnp.float32)
    return jnp.broadcast_to(reference * (-1.0 / HD), (row_max.shape[0], HD)).astype(jnp.bfloat16)


def weighted(queries, key_rows, values):
    weights = jnp.exp2(dot(queries, key_rows, (1, 1)) * SCALE).astype(jnp.bfloat16)
    return dot(weights, values, (1, 0))


def tiles_of(rows):
    tile = min(TILE, rows)
    return [slice(first, min(first + tile, rows)) for first in range(0, rows, tile)]


def until_small(flag, total, attempt):
    flag[0] = 1

    @pl.loop(0, 2)
    def _(turn):
        @pl.when(flag[0] == 1)
        def _():
            attempt(turn)
            flag[0] = jnp.where(jnp.max(total[:, HD:]) > LARGE, 1, 0).astype(jnp.int32)


class Arrivals:
    def __init__(self, entries, heads):
        self.entries = [[len(blocks) for blocks in candidates] for candidates in entries]
        self.operands = [b for candidates in entries for blocks in candidates for b in blocks]
        self.specs = [stale_spec(block, heads) for block in self.operands]
        rows = sum(block.shape[1] for block in entries[0][0])
        self.scratch = pltpu.VMEM((len(entries), 2, rows, HD), self.operands[0].dtype)

    def settle(self, info, refs, chosen):
        for index, counts in enumerate(self.entries):
            first, refs = refs[: counts[0]], refs[counts[0] :]
            second = None
            if len(counts) > 1:
                second, refs = refs[: counts[1]], refs[counts[1] :]
            at = 0
            for place, block in enumerate(first):
                value = block[...]
                if second is not None:
                    value = jnp.where(info[1 + index] == 1, value, second[place][...])
                chosen[index, :, at : at + block.shape[1], :] = value
                at += block.shape[1]

    def pieces(self, chosen):
        return [(chosen[index, 0], chosen[index, 1]) for index in range(len(self.entries))]


def stale_spec(block, heads):
    shape = (2, block.shape[1], HD)
    return pl.BlockSpec(shape, lambda h, info: (0, 0, info[0] * heads + h))


def column_spec(shape, offset=0):
    return pl.BlockSpec(shape[:2] + (HD,), lambda h, info: (0, 0, offset + h))


def accumulate(flag, total, aug, queries, first_keys, own, pieces):
    def raised(tile, row_max, some):
        for key_rows, _ in some:
            piece_max = jnp.max(dot(queries[tile, :], key_rows, (1, 1)), axis=1, keepdims=True)
            row_max = piece_max if row_max is None else jnp.maximum(row_max, piece_max)
        return row_max

    def tiles():
        for span, some in own:
            for tile in tiles_of(span.stop - span.start):
                yield slice(span.start + tile.start, span.start + tile.stop), some

    def attempt(turn):
        @pl.when(turn == 0)
        def _():
            for tile, _ in tiles():
                aug[tile, :] = reference_columns(raised(tile, None, [(first_keys, None)]))

        @pl.when(turn == 1)
        def _():
            for tile, some in tiles():
                aug[tile, :] = reference_columns(raised(tile, None, some + pieces))

        for tile, some in tiles():
            both = jnp.concatenate([queries[tile, :], aug[tile, :]], axis=1)
            summed = None
            for key_rows, values in some + pieces:
                part = weighted(both, with_ones(key_rows), with_ones(values))
                summed = part if summed is None else summed + part
            total[tile, :] = summed

    until_small(flag, total, attempt)


def flat(block):
    return block[...].reshape(-1, HD)


def joined(blocks):
    return (
        jnp.concatenate([block[0] for block in blocks], 0),
        jnp.concatenate([block[1] for block in blocks], 0),
    )


def text_body(pair, arrivals, wanted, info, *refs):
    q_ref, k_ref, v_ref = refs[:3]
    stale, came = refs[3 : 3 + pair], refs[3 + pair : 3 + pair + len(arrivals.operands)]
    out, chosen, aug, total, flag = refs[3 + pair + len(arrivals.operands) :]

    @pl.when(info[wanted] == 1)
    def _():
        arrivals.settle(info, came, chosen)
        rows = total.shape[0]
        text_keys, text_values = flat(k_ref), flat(v_ref)
        own = [(slice(0, rows), [(text_keys, text_values), joined(stale)])]
        accumulate(
            flag, total, aug, flat(q_ref), text_keys[: min(FIRST_KEYS, rows), :], own,
            arrivals.pieces(chosen),
        )
        attended = (total[:, :HD] / total[:, HD:]).astype(out.dtype)
        out[...] = attended.reshape(out.shape)


def image_body(pair, arrivals, info, *refs):
    q_ref, k_ref, v_ref, text_k_ref, text_v_ref = refs[:5]
    stale, came = refs[5 : 5 + pair], refs[5 + pair : 5 + pair + len(arrivals.operands)]
    out, chosen, aug, total, flag = refs[6 + pair + len(arrivals.operands) :]
    arrivals.settle(info, came, chosen)
    rows = total.shape[0]
    core = info[0]
    img_keys, img_values = flat(k_ref), flat(v_ref)
    text_keys, text_values = flat(text_k_ref), flat(text_v_ref)
    group_rows = rows // pair
    own = []
    for group in range(pair):
        span = slice(group * group_rows, (group + 1) * group_rows)
        key_rows, values = [img_keys[span, :]], [img_values[span, :]]
        if pair == 2:
            mine = core == group
            key_rows.append(jnp.where(mine, stale[1][0], stale[0][0]))
            values.append(jnp.where(mine, stale[1][1], stale[0][1]))
        fresh = (jnp.concatenate(key_rows, 0), jnp.concatenate(values, 0))
        own.append((span, [(text_keys, text_values), fresh]))
    accumulate(
        flag, total, aug, flat(q_ref), text_keys[: min(FIRST_KEYS, text_keys.shape[0]), :], own,
        arrivals.pieces(chosen),
    )
    attended = (total[:, :HD] / total[:, HD:]).astype(out.dtype)
    out[...] = attended.reshape(out.shape)


def attend_cost(queries, keys, heads):
    return pl.CostEstimate(
        flops=4 * queries * keys * heads * HD,
        bytes_accessed=4 * queries * heads * HD + 4 * keys * heads * HD,
        transcendentals=queries * keys * heads,
    )


def call_heads(body, name, heads, info, operands, specs, outs, out_specs, scratch, cost):
    return pl.pallas_call(
        body,
        grid_spec=pltpu.PrefetchScalarGridSpec(
            num_scalar_prefetch=1,
            grid=(heads,),
            in_specs=specs,
            out_specs=out_specs,
            scratch_shapes=scratch,
        ),
        out_shape=outs,
        compiler_params=params(
            sum(math.prod(spec.block_shape) for spec in specs if spec.block_shape is not None)
        ),
        cost_estimate=cost,
        name=name,
    )(info, *operands)


def scratch_of(rows, arrivals):
    return [
        arrivals.scratch,
        pltpu.VMEM((rows, HD), jnp.bfloat16),
        pltpu.VMEM((rows, 2 * HD), jnp.float32),
        pltpu.SMEM((1,), jnp.int32),
    ]


def attend_text(info, wanted, txt, stale, entries):
    heads = txt.shape[2] // (3 * HD)
    arrivals = Arrivals(entries, heads)
    rows = txt.shape[0] * txt.shape[1]
    out = jax.ShapeDtypeStruct(txt.shape[:2] + (heads * HD,), txt.dtype)
    return call_heads(
        functools.partial(text_body, len(stale), arrivals, wanted),
        "attend_text", heads, info, [txt] * 3 + list(stale) + arrivals.operands,
        [column_spec(txt.shape, part * heads) for part in range(3)]
        + [stale_spec(block, heads) for block in stale]
        + arrivals.specs,
        out, column_spec(out.shape), scratch_of(rows, arrivals), attend_cost(rows, 4 * rows, heads),
    )


def attend_image(info, img, txt, stale, entries, after):
    heads = img.shape[2] // (3 * HD)
    arrivals = Arrivals(entries, heads)
    rows = img.shape[0] * img.shape[1]
    out = jax.ShapeDtypeStruct(img.shape[:2] + (heads * HD,), img.dtype)
    return call_heads(
        functools.partial(image_body, len(stale), arrivals),
        "attend_image", heads, info,
        [img] * 3 + [txt] * 2 + list(stale) + arrivals.operands + [after],
        [column_spec(img.shape, part * heads) for part in range(3)]
        + [column_spec(txt.shape, part * heads) for part in (1, 2)]
        + [stale_spec(block, heads) for block in stale]
        + arrivals.specs
        + [pl.BlockSpec(memory_space=pl.ANY)],
        out, column_spec(out.shape), scratch_of(rows, arrivals), attend_cost(rows, 5 * rows, heads),
    )


def project_body(order, x_ref, weight, residual, gate, out, held, total, sems):
    copies = [
        pltpu.make_async_copy(weight.at[place], held.at[place], sems.at[place])
        for place in order
    ]
    for copy in copies:
        copy.start()
    for source, (place, copy) in enumerate(zip(order, copies)):
        copy.wait()
        part = jnp.dot(x_ref[source], held[place], preferred_element_type=jnp.float32)
        if source == 0:
            total[...] = part
        else:
            total[...] += part
    out[...] = (residual[...].astype(jnp.float32) + gate[...] * total[...]).astype(out.dtype)


def project(x, order, weight, residual, gate):
    rows, model = residual.shape
    destinations, _, width = x.shape
    vmem = pl.BlockSpec(memory_space=pltpu.VMEM)
    return pl.pallas_call(
        functools.partial(project_body, order),
        in_specs=[vmem, pl.BlockSpec(memory_space=pl.ANY), vmem, vmem],
        out_specs=vmem,
        out_shape=jax.ShapeDtypeStruct((rows, model), residual.dtype),
        scratch_shapes=[
            pltpu.VMEM((destinations, width, model), weight.dtype),
            pltpu.VMEM((rows, model), jnp.float32),
            pltpu.SemaphoreType.DMA((destinations,)),
        ],
        compiler_params=pltpu.CompilerParams(vmem_limit_bytes=WIDE_LIMIT),
        cost_estimate=pl.CostEstimate(
            flops=2 * rows * model * model, bytes_accessed=2 * model * model, transcendentals=0
        ),
        name="project",
    )(x, weight.reshape(destinations, width, model), residual, gate.reshape(1, model))


def after_body(*refs):
    del refs


def after(x, other):
    anywhere = pl.BlockSpec(memory_space=pl.ANY)
    return pl.pallas_call(
        after_body,
        in_specs=[anywhere, anywhere],
        out_specs=anywhere,
        out_shape=jax.ShapeDtypeStruct(x.shape, x.dtype),
        input_output_aliases={0: 0},
        name="after",
    )(x, other)


def unpack_body(order, x_ref, out):
    width = x_ref.shape[2]
    for source, place in enumerate(order):
        out[:, place * width : (place + 1) * width] = x_ref[source]


def unpack(x, order):
    rows, model = x.shape[1], x.shape[0] * x.shape[2]
    return pl.pallas_call(
        functools.partial(unpack_body, order),
        grid=(1,),
        in_specs=[pl.BlockSpec(x.shape, lambda n: (0, 0, 0))],
        out_specs=pl.BlockSpec((rows, model), lambda n: (0, 0)),
        out_shape=jax.ShapeDtypeStruct((rows, model), x.dtype),
        compiler_params=params(),
        name="unpack_text",
    )(x)


def per_device(img_qkv, txt_qkv, stale_kv, residual, gate_scale, proj_weight):
    patches, head_owners = lax.axis_size("patch"), lax.axis_size("head")
    patch = lax.axis_index("patch")
    owned_heads = stale_kv.shape[2] // HD
    pair = 2 if patches % 2 == 0 and owned_heads % 2 == 0 else 1
    planes = patches // pair
    plane, core = patch // pair, patch % pair
    width = stale_kv.shape[2] // pair
    heads = width // HD
    img_rows, model = residual.shape
    text_rows = txt_qkv.shape[0] // pair
    destinations = pair * head_owners

    order = [(d % head_owners) * pair + d // head_owners for d in range(destinations)]
    groups = [[g * destinations + d for d in range(destinations)] for g in range(planes)]
    swap_pairs = [(p, p + 1 - 2 * (p % 2)) for p in range(patches)]

    def exchange(x):
        return lax.all_to_all(
            x, ("patch", "head"), split_axis=0, concat_axis=0, axis_index_groups=groups, tiled=True
        )

    def swap(x):
        return lax.ppermute(x, "patch", swap_pairs)

    def up_pairs(step):
        return [(z, z + 1) for z in range(step - 1, planes - 1)]

    def down_pairs(step):
        return [(z + 1, z) for z in range(0, planes - step)]

    core_only = core.astype(jnp.int32).reshape(1)
    txt = exchange(pack(core_only, txt_qkv, text_rows, head_owners, pair, width))

    along, against = [], []
    if pair == 2:
        stale = [stale_kv, swap(stale_kv)]
        held = [stale_kv, stale_kv]
        for step in range(1, planes):
            pairs = [
                [(2 * a + turn, 2 * b) for a, b in up_pairs(step)]
                + [(2 * a + 1 - turn, 2 * b + 1) for a, b in down_pairs(step)]
                for turn in ((0, 1) if step == 1 else (0, 0))
            ]
            held = [lax.ppermute(block, "patch", way) for block, way in zip(held, pairs)]
            along.append(held)
            against.append([swap(block) for block in held])
        ahead = jnp.where(core == 0, plane, planes - 1 - plane)
    else:
        stale = [stale_kv]
        from_below = from_above = stale_kv
        for step in range(1, planes):
            from_below = lax.ppermute(from_below, "patch", up_pairs(step))
            from_above = lax.ppermute(from_above, "patch", down_pairs(step))
            along.append([from_below])
            against.append([from_above])
        ahead = plane
    held_first = along[0]
    entries = [[along[i - 1], against[planes - i - 1]] for i in range(1, planes)]
    first_holds = [ahead >= i for i in range(1, planes)]
    zero_only = jnp.zeros((1,), jnp.int32)
    img = exchange(pack(zero_only, img_qkv, img_rows, head_owners, pair, width, [txt] + held_first))

    early = planes > 2
    inner = (plane > 0) & (plane < planes - 1)
    info = jnp.stack([core] + first_holds + [inner if early else core >= 0]).astype(jnp.int32)
    known = entries
    if early:
        known = [[along[0]]] + entries[1:-1] + [[against[0]]]
    text_attn = attend_text(info, planes, txt, stale, known)
    image_attn = attend_image(info, img, txt, stale, entries, text_attn)
    text_back = exchange(after(text_attn, img))

    text_out = unpack(text_back, order)
    if early:
        ends = [(1, 0), (planes - 2, planes - 1)]
        ends = [(a * pair + c, b * pair + c) for a, b in ends for c in range(pair)]
        text_out = jnp.where(inner, text_out, lax.ppermute(text_out, "patch", ends))
    if pair == 2:
        other = swap(text_out)
        lower = core == 0
        text_out = jnp.concatenate(
            [jnp.where(lower, text_out, other), jnp.where(lower, other, text_out)], 0
        )

    image_out = project(exchange(image_attn), order, proj_weight, residual, gate_scale)
    return (image_out, text_out)


def solution(mesh):
    return jax.shard_map(
        per_device,
        mesh=mesh,
        in_specs=(
            P(("patch", "head"), None),
            P("head", None),
            P(None, "patch", "head"),
            P(("patch", "head"), None),
            P(),
            P(),
        ),
        out_specs=(P(("patch", "head"), None), P("head", None)),
        check_vma=False,
    )
```

```python
import functools
import math

import jax
import jax.numpy as jnp
from jax import lax
from jax.experimental import pallas as pl
from jax.experimental.pallas import tpu as pltpu
from jax.sharding import PartitionSpec as P

HD = 128
SCALE = math.log2(math.e) / math.sqrt(HD)
VMEM_LIMIT = 20 * 1024 * 1024
WIDE_LIMIT = 48 * 1024 * 1024
TILE = 512
FIRST_KEYS = 256
LARGE = 2.0**60


def params(block_elements=0):
    return pltpu.CompilerParams(
        vmem_limit_bytes=VMEM_LIMIT + 4 * block_elements, dimension_semantics=("arbitrary",)
    )


def pack_body(_, *refs):
    sources, packed = refs[:3], refs[-1]
    width = sources[0].shape[1]
    for part, source in enumerate(sources):
        packed[0, :, part * width : (part + 1) * width] = source[...]


def pack(first_block, array, rows, head_owners, pair, width, after=()):
    blocks = array.shape[1] // 3 // width
    destinations = head_owners * pair

    def source(part):
        def place(d, info):
            return (info[0], part * blocks + (d % head_owners) * pair + d // head_owners)

        return pl.BlockSpec((rows, width), place)

    return pl.pallas_call(
        pack_body,
        grid_spec=pltpu.PrefetchScalarGridSpec(
            num_scalar_prefetch=1,
            grid=(destinations,),
            in_specs=[source(0), source(1), source(2)]
            + [pl.BlockSpec(memory_space=pl.ANY)] * len(after),
            out_specs=pl.BlockSpec((1, rows, 3 * width), lambda d, info: (d, 0, 0)),
        ),
        out_shape=jax.ShapeDtypeStruct((destinations, rows, 3 * width), array.dtype),
        compiler_params=params(),
        name="pack_heads",
    )(first_block, array, array, array, *after)


def dot(first, second, contract):
    return lax.dot_general(
        first, second, ((contract[:1], contract[1:]), ((), ())), preferred_element_type=jnp.float32
    )


def with_ones(block):
    return jnp.concatenate([block, jnp.ones_like(block)], axis=1)


def reference_columns(row_max):
    reference = row_max.astype(jnp.bfloat16).astype(jnp.float32)
    return jnp.broadcast_to(reference * (-1.0 / HD), (row_max.shape[0], HD)).astype(jnp.bfloat16)


def weighted(queries, key_rows, values):
    weights = jnp.exp2(dot(queries, key_rows, (1, 1)) * SCALE).astype(jnp.bfloat16)
    return dot(weights, values, (1, 0))


def tiles_of(rows):
    tile = min(TILE, rows)
    return [slice(first, min(first + tile, rows)) for first in range(0, rows, tile)]


def until_small(flag, total, attempt):
    flag[0] = 1

    @pl.loop(0, 2)
    def _(turn):
        @pl.when(flag[0] == 1)
        def _():
            attempt(turn)
            flag[0] = jnp.where(jnp.max(total[:, HD:]) > LARGE, 1, 0).astype(jnp.int32)


class Arrivals:
    def __init__(self, entries, heads):
        self.entries = [[len(blocks) for blocks in candidates] for candidates in entries]
        self.operands = [b for candidates in entries for blocks in candidates for b in blocks]
        self.specs = [
            stale_spec(block, heads, (index, place) if len(candidates) > 1 else None)
            for index, candidates in enumerate(entries)
            for place, blocks in enumerate(candidates)
            for block in blocks
        ]
        rows = sum(block.shape[1] for block in entries[0][0])
        self.scratch = pltpu.VMEM((len(entries), 2, rows, HD), self.operands[0].dtype)

    def settle(self, info, refs, chosen):
        for index, counts in enumerate(self.entries):
            first, refs = refs[: counts[0]], refs[counts[0] :]
            second = None
            if len(counts) > 1:
                second, refs = refs[: counts[1]], refs[counts[1] :]
            at = 0
            for place, block in enumerate(first):
                value = block[...]
                if second is not None:
                    value = jnp.where(info[1 + index] == 1, value, second[place][...])
                chosen[index, :, at : at + block.shape[1], :] = value
                at += block.shape[1]

    def pieces(self, chosen):
        return [(chosen[index, 0], chosen[index, 1]) for index in range(len(self.entries))]


def stale_spec(block, heads, candidate=None):
    def place(h, info):
        column = info[0] * heads + h
        if candidate is not None:
            index, second = candidate
            column = jnp.where(info[1 + index] == 1 - second, column, 0)
        return (0, 0, column)

    return pl.BlockSpec((2, block.shape[1], HD), place)


def column_spec(shape, offset=0):
    return pl.BlockSpec(shape[:2] + (HD,), lambda h, info: (0, 0, offset + h))


def accumulate(flag, total, aug, queries, first_keys, own, pieces):
    def raised(tile, row_max, some):
        for key_rows, _ in some:
            piece_max = jnp.max(dot(queries[tile, :], key_rows, (1, 1)), axis=1, keepdims=True)
            row_max = piece_max if row_max is None else jnp.maximum(row_max, piece_max)
        return row_max

    def tiles():
        for span, some in own:
            for tile in tiles_of(span.stop - span.start):
                yield slice(span.start + tile.start, span.start + tile.stop), some

    def attempt(turn):
        @pl.when(turn == 0)
        def _():
            for tile, _ in tiles():
                aug[tile, :] = reference_columns(raised(tile, None, [(first_keys, None)]))

        @pl.when(turn == 1)
        def _():
            for tile, some in tiles():
                aug[tile, :] = reference_columns(raised(tile, None, some + pieces))

        for tile, some in tiles():
            both = jnp.concatenate([queries[tile, :], aug[tile, :]], axis=1)
            summed = None
            for key_rows, values in some + pieces:
                part = weighted(both, with_ones(key_rows), with_ones(values))
                summed = part if summed is None else summed + part
            total[tile, :] = summed

    until_small(flag, total, attempt)


def flat(block):
    return block[...].reshape(-1, HD)


def joined(blocks):
    return (
        jnp.concatenate([block[0] for block in blocks], 0),
        jnp.concatenate([block[1] for block in blocks], 0),
    )


def text_body(pair, arrivals, wanted, info, *refs):
    q_ref, k_ref, v_ref = refs[:3]
    stale, came = refs[3 : 3 + pair], refs[3 + pair : 3 + pair + len(arrivals.operands)]
    out, chosen, aug, total, flag = refs[3 + pair + len(arrivals.operands) :]

    @pl.when(info[wanted] == 1)
    def _():
        arrivals.settle(info, came, chosen)
        rows = total.shape[0]
        text_keys, text_values = flat(k_ref), flat(v_ref)
        own = [(slice(0, rows), [(text_keys, text_values), joined(stale)])]
        accumulate(
            flag, total, aug, flat(q_ref), text_keys[: min(FIRST_KEYS, rows), :], own,
            arrivals.pieces(chosen),
        )
        attended = (total[:, :HD] / total[:, HD:]).astype(out.dtype)
        out[...] = attended.reshape(out.shape)


def image_body(pair, arrivals, info, *refs):
    q_ref, k_ref, v_ref, text_k_ref, text_v_ref = refs[:5]
    stale, came = refs[5 : 5 + pair], refs[5 + pair : 5 + pair + len(arrivals.operands)]
    out, chosen, aug, total, flag = refs[6 + pair + len(arrivals.operands) :]
    arrivals.settle(info, came, chosen)
    rows = total.shape[0]
    core = info[0]
    img_keys, img_values = flat(k_ref), flat(v_ref)
    text_keys, text_values = flat(text_k_ref), flat(text_v_ref)
    group_rows = rows // pair
    own = []
    for group in range(pair):
        span = slice(group * group_rows, (group + 1) * group_rows)
        key_rows, values = [img_keys[span, :]], [img_values[span, :]]
        if pair == 2:
            mine = core == group
            key_rows.append(jnp.where(mine, stale[1][0], stale[0][0]))
            values.append(jnp.where(mine, stale[1][1], stale[0][1]))
        fresh = (jnp.concatenate(key_rows, 0), jnp.concatenate(values, 0))
        own.append((span, [(text_keys, text_values), fresh]))
    accumulate(
        flag, total, aug, flat(q_ref), text_keys[: min(FIRST_KEYS, text_keys.shape[0]), :], own,
        arrivals.pieces(chosen),
    )
    attended = (total[:, :HD] / total[:, HD:]).astype(out.dtype)
    out[...] = attended.reshape(out.shape)


def attend_cost(queries, keys, heads):
    return pl.CostEstimate(
        flops=4 * queries * keys * heads * HD,
        bytes_accessed=4 * queries * heads * HD + 4 * keys * heads * HD,
        transcendentals=queries * keys * heads,
    )


def call_heads(body, name, heads, info, operands, specs, outs, out_specs, scratch, cost):
    return pl.pallas_call(
        body,
        grid_spec=pltpu.PrefetchScalarGridSpec(
            num_scalar_prefetch=1,
            grid=(heads,),
            in_specs=specs,
            out_specs=out_specs,
            scratch_shapes=scratch,
        ),
        out_shape=outs,
        compiler_params=params(
            sum(math.prod(spec.block_shape) for spec in specs if spec.block_shape is not None)
        ),
        cost_estimate=cost,
        name=name,
    )(info, *operands)


def scratch_of(rows, arrivals):
    return [
        arrivals.scratch,
        pltpu.VMEM((rows, HD), jnp.bfloat16),
        pltpu.VMEM((rows, 2 * HD), jnp.float32),
        pltpu.SMEM((1,), jnp.int32),
    ]


def attend_text(info, wanted, txt, stale, entries):
    heads = txt.shape[2] // (3 * HD)
    arrivals = Arrivals(entries, heads)
    rows = txt.shape[0] * txt.shape[1]
    out = jax.ShapeDtypeStruct(txt.shape[:2] + (heads * HD,), txt.dtype)
    return call_heads(
        functools.partial(text_body, len(stale), arrivals, wanted),
        "attend_text", heads, info, [txt] * 3 + list(stale) + arrivals.operands,
        [column_spec(txt.shape, part * heads) for part in range(3)]
        + [stale_spec(block, heads) for block in stale]
        + arrivals.specs,
        out, column_spec(out.shape), scratch_of(rows, arrivals), attend_cost(rows, 4 * rows, heads),
    )


def attend_image(info, img, txt, stale, entries, after):
    heads = img.shape[2] // (3 * HD)
    arrivals = Arrivals(entries, heads)
    rows = img.shape[0] * img.shape[1]
    out = jax.ShapeDtypeStruct(img.shape[:2] + (heads * HD,), img.dtype)
    return call_heads(
        functools.partial(image_body, len(stale), arrivals),
        "attend_image", heads, info,
        [img] * 3 + [txt] * 2 + list(stale) + arrivals.operands + [after],
        [column_spec(img.shape, part * heads) for part in range(3)]
        + [column_spec(txt.shape, part * heads) for part in (1, 2)]
        + [stale_spec(block, heads) for block in stale]
        + arrivals.specs
        + [pl.BlockSpec(memory_space=pl.ANY)],
        out, column_spec(out.shape), scratch_of(rows, arrivals), attend_cost(rows, 5 * rows, heads),
    )


def project_body(order, x_ref, weight, residual, gate, out, held, total, sems):
    copies = [
        pltpu.make_async_copy(weight.at[place], held.at[place], sems.at[place])
        for place in order
    ]
    for copy in copies:
        copy.start()
    for source, (place, copy) in enumerate(zip(order, copies)):
        copy.wait()
        part = jnp.dot(x_ref[source], held[place], preferred_element_type=jnp.float32)
        if source == 0:
            total[...] = part
        else:
            total[...] += part
    out[...] = (residual[...].astype(jnp.float32) + gate[...] * total[...]).astype(out.dtype)


def project(x, order, weight, residual, gate):
    rows, model = residual.shape
    destinations, _, width = x.shape
    vmem = pl.BlockSpec(memory_space=pltpu.VMEM)
    return pl.pallas_call(
        functools.partial(project_body, order),
        in_specs=[vmem, pl.BlockSpec(memory_space=pl.ANY), vmem, vmem],
        out_specs=vmem,
        out_shape=jax.ShapeDtypeStruct((rows, model), residual.dtype),
        scratch_shapes=[
            pltpu.VMEM((destinations, width, model), weight.dtype),
            pltpu.VMEM((rows, model), jnp.float32),
            pltpu.SemaphoreType.DMA((destinations,)),
        ],
        compiler_params=pltpu.CompilerParams(vmem_limit_bytes=WIDE_LIMIT),
        cost_estimate=pl.CostEstimate(
            flops=2 * rows * model * model, bytes_accessed=2 * model * model, transcendentals=0
        ),
        name="project",
    )(x, weight.reshape(destinations, width, model), residual, gate.reshape(1, model))


def after_body(*refs):
    del refs


def after(x, other):
    anywhere = pl.BlockSpec(memory_space=pl.ANY)
    return pl.pallas_call(
        after_body,
        in_specs=[anywhere, anywhere],
        out_specs=anywhere,
        out_shape=jax.ShapeDtypeStruct(x.shape, x.dtype),
        input_output_aliases={0: 0},
        name="after",
    )(x, other)


def unpack_body(order, x_ref, out):
    width = x_ref.shape[2]
    for source, place in enumerate(order):
        out[:, place * width : (place + 1) * width] = x_ref[source]


def unpack(x, order):
    rows, model = x.shape[1], x.shape[0] * x.shape[2]
    return pl.pallas_call(
        functools.partial(unpack_body, order),
        grid=(1,),
        in_specs=[pl.BlockSpec(x.shape, lambda n: (0, 0, 0))],
        out_specs=pl.BlockSpec((rows, model), lambda n: (0, 0)),
        out_shape=jax.ShapeDtypeStruct((rows, model), x.dtype),
        compiler_params=params(),
        name="unpack_text",
    )(x)


def per_device(img_qkv, txt_qkv, stale_kv, residual, gate_scale, proj_weight):
    patches, head_owners = lax.axis_size("patch"), lax.axis_size("head")
    patch = lax.axis_index("patch")
    owned_heads = stale_kv.shape[2] // HD
    pair = 2 if patches % 2 == 0 and owned_heads % 2 == 0 else 1
    planes = patches // pair
    plane, core = patch // pair, patch % pair
    width = stale_kv.shape[2] // pair
    heads = width // HD
    img_rows, model = residual.shape
    text_rows = txt_qkv.shape[0] // pair
    destinations = pair * head_owners

    order = [(d % head_owners) * pair + d // head_owners for d in range(destinations)]
    groups = [[g * destinations + d for d in range(destinations)] for g in range(planes)]
    swap_pairs = [(p, p + 1 - 2 * (p % 2)) for p in range(patches)]

    def exchange(x):
        return lax.all_to_all(
            x, ("patch", "head"), split_axis=0, concat_axis=0, axis_index_groups=groups, tiled=True
        )

    def swap(x):
        return lax.ppermute(x, "patch", swap_pairs)

    def up_pairs(step):
        return [(z, z + 1) for z in range(step - 1, planes - 1)]

    def down_pairs(step):
        return [(z + 1, z) for z in range(0, planes - step)]

    core_only = core.astype(jnp.int32).reshape(1)
    txt = exchange(pack(core_only, txt_qkv, text_rows, head_owners, pair, width))

    along, against = [], []
    if pair == 2:
        stale = [stale_kv, swap(stale_kv)]
        held = [stale_kv, stale_kv]
        for step in range(1, planes):
            pairs = [
                [(2 * a + turn, 2 * b) for a, b in up_pairs(step)]
                + [(2 * a + 1 - turn, 2 * b + 1) for a, b in down_pairs(step)]
                for turn in ((0, 1) if step == 1 else (0, 0))
            ]
            held = [lax.ppermute(block, "patch", way) for block, way in zip(held, pairs)]
            along.append(held)
            against.append([swap(block) for block in held])
        ahead = jnp.where(core == 0, plane, planes - 1 - plane)
    else:
        stale = [stale_kv]
        from_below = from_above = stale_kv
        for step in range(1, planes):
            from_below = lax.ppermute(from_below, "patch", up_pairs(step))
            from_above = lax.ppermute(from_above, "patch", down_pairs(step))
            along.append([from_below])
            against.append([from_above])
        ahead = plane
    held_first = along[0]
    entries = [[along[i - 1], against[planes - i - 1]] for i in range(1, planes)]
    first_holds = [ahead >= i for i in range(1, planes)]
    zero_only = jnp.zeros((1,), jnp.int32)
    img = exchange(pack(zero_only, img_qkv, img_rows, head_owners, pair, width, [txt] + held_first))

    early = planes > 2
    inner = (plane > 0) & (plane < planes - 1)
    info = jnp.stack([core] + first_holds + [inner if early else core >= 0]).astype(jnp.int32)
    known = entries
    if early:
        known = [[along[0]]] + entries[1:-1] + [[against[0]]]
    text_attn = attend_text(info, planes, txt, stale, known)
    image_attn = attend_image(info, img, txt, stale, entries, text_attn)
    text_back = exchange(after(text_attn, img))

    text_out = unpack(after(text_back, image_attn), order)
    if early:
        ends = [(1, 0), (planes - 2, planes - 1)]
        ends = [(a * pair + c, b * pair + c) for a, b in ends for c in range(pair)]
        text_out = jnp.where(inner, text_out, lax.ppermute(text_out, "patch", ends))
    if pair == 2:
        other = swap(text_out)
        lower = core == 0
        text_out = jnp.concatenate(
            [jnp.where(lower, text_out, other), jnp.where(lower, other, text_out)], 0
        )

    image_out = project(exchange(image_attn), order, proj_weight, residual, gate_scale)
    return (image_out, text_out)


def solution(mesh):
    return jax.shard_map(
        per_device,
        mesh=mesh,
        in_specs=(
            P(("patch", "head"), None),
            P("head", None),
            P(None, "patch", "head"),
            P(("patch", "head"), None),
            P(),
            P(),
        ),
        out_specs=(P(("patch", "head"), None), P("head", None)),
        check_vma=False,
    )
```

```python
import functools
import math

import jax
import jax.numpy as jnp
from jax import lax
from jax.experimental import pallas as pl
from jax.experimental.pallas import tpu as pltpu
from jax.sharding import PartitionSpec as P

HD = 128
SCALE = math.log2(math.e) / math.sqrt(HD)
VMEM_LIMIT = 12 * 1024 * 1024
WIDE_LIMIT = 48 * 1024 * 1024
TILE = 256
FIRST_KEYS = 256
LARGE = 2.0**60


def params(block_elements=0):
    return pltpu.CompilerParams(
        vmem_limit_bytes=VMEM_LIMIT + 4 * block_elements, dimension_semantics=("arbitrary",)
    )


def pack_body(_, *refs):
    sources, packed = refs[:3], refs[-1]
    width = sources[0].shape[1]
    for part, source in enumerate(sources):
        packed[0, :, part * width : (part + 1) * width] = source[...]


def pack(first_block, array, rows, head_owners, pair, width, after=()):
    blocks = array.shape[1] // 3 // width
    destinations = head_owners * pair

    def source(part):
        def place(d, info):
            return (info[0], part * blocks + (d % head_owners) * pair + d // head_owners)

        return pl.BlockSpec((rows, width), place)

    return pl.pallas_call(
        pack_body,
        grid_spec=pltpu.PrefetchScalarGridSpec(
            num_scalar_prefetch=1,
            grid=(destinations,),
            in_specs=[source(0), source(1), source(2)]
            + [pl.BlockSpec(memory_space=pl.ANY)] * len(after),
            out_specs=pl.BlockSpec((1, rows, 3 * width), lambda d, info: (d, 0, 0)),
        ),
        out_shape=jax.ShapeDtypeStruct((destinations, rows, 3 * width), array.dtype),
        compiler_params=params(),
        name="pack_heads",
    )(first_block, array, array, array, *after)


def dot(first, second, contract):
    return lax.dot_general(
        first, second, ((contract[:1], contract[1:]), ((), ())), preferred_element_type=jnp.float32
    )


def with_ones(block):
    return jnp.concatenate([block, jnp.ones_like(block)], axis=1)


def reference_columns(row_max):
    reference = row_max.astype(jnp.bfloat16).astype(jnp.float32)
    return jnp.broadcast_to(reference * (-1.0 / HD), (row_max.shape[0], HD)).astype(jnp.bfloat16)


def weighted(queries, key_rows, values):
    weights = jnp.exp2(dot(queries, key_rows, (1, 1)) * SCALE).astype(jnp.bfloat16)
    return dot(weights, values, (1, 0))


def tiles_of(rows):
    tile = min(TILE, rows)
    return [slice(first, min(first + tile, rows)) for first in range(0, rows, tile)]


def until_small(flag, total, attempt):
    flag[0] = 1

    @pl.loop(0, 2)
    def _(turn):
        @pl.when(flag[0] == 1)
        def _():
            attempt(turn)
            flag[0] = jnp.where(jnp.max(total[:, :, HD:]) > LARGE, 1, 0).astype(jnp.int32)


def copy_columns(target, at, block, core, width):
    columns = pl.ds(pl.multiple_of(core * width, width), width)
    target[:, at : at + block.shape[1], :] = block[:, :, columns]


def settle(info, refs, entries, chosen):
    width = chosen.shape[3]
    for index, candidates in enumerate(entries):
        for place, count in enumerate(candidates):
            blocks, refs = refs[:count], refs[count:]

            def copy():
                at = 0
                for block in blocks:
                    copy_columns(chosen.at[index], at, block, info[0], width)
                    at += block.shape[1]

            if len(candidates) == 1:
                copy()
            else:
                pl.when(info[1 + index] == 1 - place)(copy)


def accumulate(flag, total, aug, heads, queries_of, first_keys_of, own, chosen):
    def columns(head):
        return slice(head * HD, (head + 1) * HD)

    def pieces(head, some):
        return some(head) + [
            (chosen[index, 0, :, columns(head)], chosen[index, 1, :, columns(head)])
            for index in range(chosen.shape[0])
        ]

    def tiles():
        for head in range(heads):
            queries = queries_of(head)
            for span, some in own:
                for tile in tiles_of(span.stop - span.start):
                    tile = slice(span.start + tile.start, span.start + tile.stop)
                    yield head, tile, queries[tile, :], some

    def largest(queries, key_rows):
        return jnp.max(dot(queries, key_rows, (1, 1)), axis=1, keepdims=True)

    def attempt(turn):
        @pl.when(turn == 0)
        def _():
            for head, tile, queries, _ in tiles():
                aug[head, tile, :] = reference_columns(largest(queries, first_keys_of(head)))

        @pl.when(turn == 1)
        def _():
            for head, tile, queries, some in tiles():
                row_max = None
                for key_rows, _ in pieces(head, some):
                    piece_max = largest(queries, key_rows)
                    row_max = piece_max if row_max is None else jnp.maximum(row_max, piece_max)
                aug[head, tile, :] = reference_columns(row_max)

        for head, tile, queries, some in tiles():
            both = jnp.concatenate([queries, aug[head, tile, :]], axis=1)
            summed = None
            for key_rows, values in pieces(head, some):
                part = weighted(both, with_ones(key_rows), with_ones(values))
                summed = part if summed is None else summed + part
            total[head, tile, :] = summed

    until_small(flag, total, attempt)


def finish(out, total):
    for head in range(total.shape[0]):
        attended = (total[head, :, :HD] / total[head, :, HD:]).astype(out.dtype)
        out[:, :, head * HD : (head + 1) * HD] = attended.reshape(out.shape[:2] + (HD,))


def part_of(ref, part, head, width):
    first = part * width + head * HD
    return ref[:, :, first : first + HD].reshape(-1, HD)


def text_body(pair, entries, info, txt, *refs, wanted):
    stale, came = refs[:pair], refs[pair:-6]
    out, chosen, beside, aug, total, flag = refs[-6:]
    width = chosen.shape[3]
    heads = width // HD

    @pl.when(info[wanted] == 1)
    def _():
        settle(info, came, entries, chosen)
        at = 0
        for block in stale:
            copy_columns(beside.at[0], at, block, info[0], width)
            at += block.shape[1]

        def own(head):
            columns = slice(head * HD, (head + 1) * HD)
            return [
                (part_of(txt, 1, head, width), part_of(txt, 2, head, width)),
                (beside[0, 0, :, columns], beside[0, 1, :, columns]),
            ]

        accumulate(
            flag, total, aug, heads,
            lambda head: part_of(txt, 0, head, width),
            lambda head: part_of(txt, 1, head, width)[: min(FIRST_KEYS, total.shape[1]), :],
            [(slice(0, total.shape[1]), own)], chosen,
        )
        finish(out, total)


def image_body(pair, entries, info, img, txt, *refs):
    stale, came = refs[:pair], refs[pair:-6]
    out, chosen, beside, aug, total, flag = refs[-6:]
    width = chosen.shape[3]
    heads = width // HD
    rows = total.shape[1]
    group_rows, sources = rows // pair, img.shape[0] // pair
    settle(info, came, entries, chosen)
    for group in range(pair):
        for part in range(2):
            fresh = img[
                group * sources : (group + 1) * sources, :, (1 + part) * width : (2 + part) * width
            ]
            beside[group, part, :group_rows, :] = fresh.reshape(group_rows, width)
        if pair == 2:
            for place, block in enumerate(stale):

                @pl.when((info[0] == group) == (place == 1))
                def _():
                    copy_columns(beside.at[group], group_rows, block, info[0], width)

    def own(group):
        def some(head):
            columns = slice(head * HD, (head + 1) * HD)
            return [
                (part_of(txt, 1, head, width), part_of(txt, 2, head, width)),
                (beside[group, 0, :, columns], beside[group, 1, :, columns]),
            ]

        return (slice(group * group_rows, (group + 1) * group_rows), some)

    text_keys = txt.shape[0] * txt.shape[1]
    accumulate(
        flag, total, aug, heads,
        lambda head: part_of(img, 0, head, width),
        lambda head: part_of(txt, 1, head, width)[: min(FIRST_KEYS, text_keys), :],
        [own(group) for group in range(pair)], chosen,
    )
    finish(out, total)


def attend(name, body, info, fresh, stale, entries, groups):
    first = fresh[0]
    width = first.shape[2] // 3
    heads, rows = width // HD, first.shape[0] * first.shape[1]
    keys = sum(block.shape[1] for block in stale)
    came = [b for candidates in entries for blocks in candidates for b in blocks]
    counts = [[len(blocks) for blocks in candidates] for candidates in entries]
    vmem = pl.BlockSpec(memory_space=pltpu.VMEM)
    scratch = [
        ((len(entries), 2, keys, width), first.dtype),
        ((groups, 2, keys, width), first.dtype),
        ((heads, rows, HD), jnp.bfloat16),
        ((heads, rows, 2 * HD), jnp.float32),
    ]
    needed = sum(math.prod(shape) * jnp.dtype(kind).itemsize for shape, kind in scratch)
    return pl.pallas_call(
        functools.partial(body, len(stale), counts),
        in_specs=[pl.BlockSpec(memory_space=pltpu.SMEM)]
        + [vmem] * (len(fresh) + len(stale) + len(came)),
        out_specs=vmem,
        out_shape=jax.ShapeDtypeStruct(first.shape[:2] + (width,), first.dtype),
        scratch_shapes=[pltpu.VMEM(*one) for one in scratch] + [pltpu.SMEM((1,), jnp.int32)],
        compiler_params=pltpu.CompilerParams(vmem_limit_bytes=VMEM_LIMIT + needed),
        cost_estimate=pl.CostEstimate(
            flops=4 * rows * keys * (2 + len(entries)) * width,
            bytes_accessed=4 * keys * (2 + len(entries)) * width,
            transcendentals=rows * keys * (2 + len(entries)) * heads,
        ),
        name=name,
    )(info, *fresh, *stale, *came)


def project_body(order, x_ref, weight, residual, gate, out, held, total, sems):
    copies = [
        pltpu.make_async_copy(weight.at[place], held.at[place], sems.at[place])
        for place in order
    ]
    for copy in copies:
        copy.start()
    for source, (place, copy) in enumerate(zip(order, copies)):
        copy.wait()
        part = jnp.dot(x_ref[source], held[place], preferred_element_type=jnp.float32)
        if source == 0:
            total[...] = part
        else:
            total[...] += part
    out[...] = (residual[...].astype(jnp.float32) + gate[...] * total[...]).astype(out.dtype)


def project(x, order, weight, residual, gate):
    rows, model = residual.shape
    destinations, _, width = x.shape
    vmem = pl.BlockSpec(memory_space=pltpu.VMEM)
    return pl.pallas_call(
        functools.partial(project_body, order),
        in_specs=[vmem, pl.BlockSpec(memory_space=pl.ANY), vmem, vmem],
        out_specs=vmem,
        out_shape=jax.ShapeDtypeStruct((rows, model), residual.dtype),
        scratch_shapes=[
            pltpu.VMEM((destinations, width, model), weight.dtype),
            pltpu.VMEM((rows, model), jnp.float32),
            pltpu.SemaphoreType.DMA((destinations,)),
        ],
        compiler_params=pltpu.CompilerParams(vmem_limit_bytes=WIDE_LIMIT),
        cost_estimate=pl.CostEstimate(
            flops=2 * rows * model * model, bytes_accessed=2 * model * model, transcendentals=0
        ),
        name="project",
    )(x, weight.reshape(destinations, width, model), residual, gate.reshape(1, model))


def after_body(*refs):
    del refs


def after(x, other):
    anywhere = pl.BlockSpec(memory_space=pl.ANY)
    return pl.pallas_call(
        after_body,
        in_specs=[anywhere, anywhere],
        out_specs=anywhere,
        out_shape=jax.ShapeDtypeStruct(x.shape, x.dtype),
        input_output_aliases={0: 0},
        name="after",
    )(x, other)


def unpack_body(order, x_ref, out):
    width = x_ref.shape[2]
    for source, place in enumerate(order):
        out[:, place * width : (place + 1) * width] = x_ref[source]


def unpack(x, order):
    rows, model = x.shape[1], x.shape[0] * x.shape[2]
    return pl.pallas_call(
        functools.partial(unpack_body, order),
        grid=(1,),
        in_specs=[pl.BlockSpec(x.shape, lambda n: (0, 0, 0))],
        out_specs=pl.BlockSpec((rows, model), lambda n: (0, 0)),
        out_shape=jax.ShapeDtypeStruct((rows, model), x.dtype),
        compiler_params=params(),
        name="unpack_text",
    )(x)


def per_device(img_qkv, txt_qkv, stale_kv, residual, gate_scale, proj_weight):
    patches, head_owners = lax.axis_size("patch"), lax.axis_size("head")
    patch = lax.axis_index("patch")
    owned_heads = stale_kv.shape[2] // HD
    pair = 2 if patches % 2 == 0 and owned_heads % 2 == 0 else 1
    planes = patches // pair
    plane, core = patch // pair, patch % pair
    width = stale_kv.shape[2] // pair
    heads = width // HD
    img_rows, model = residual.shape
    text_rows = txt_qkv.shape[0] // pair
    destinations = pair * head_owners

    order = [(d % head_owners) * pair + d // head_owners for d in range(destinations)]
    groups = [[g * destinations + d for d in range(destinations)] for g in range(planes)]
    swap_pairs = [(p, p + 1 - 2 * (p % 2)) for p in range(patches)]

    def exchange(x):
        return lax.all_to_all(
            x, ("patch", "head"), split_axis=0, concat_axis=0, axis_index_groups=groups, tiled=True
        )

    def swap(x):
        return lax.ppermute(x, "patch", swap_pairs)

    def up_pairs(step):
        return [(z, z + 1) for z in range(step - 1, planes - 1)]

    def down_pairs(step):
        return [(z + 1, z) for z in range(0, planes - step)]

    def pack_img(earlier):
        first = jnp.zeros((1,), jnp.int32)
        return pack(first, img_qkv, img_rows, head_owners, pair, width, earlier)

    core_only = core.astype(jnp.int32).reshape(1)
    packed = pack(core_only, txt_qkv, text_rows, head_owners, pair, width)
    txt = exchange(packed)

    along, against = [], []
    if pair == 2:
        stale = [stale_kv, swap(stale_kv)]
        held = [stale_kv, stale_kv]
        for step in range(1, planes):
            pairs = [
                [(2 * a + turn, 2 * b) for a, b in up_pairs(step)]
                + [(2 * a + 1 - turn, 2 * b + 1) for a, b in down_pairs(step)]
                for turn in ((0, 1) if step == 1 else (0, 0))
            ]
            held = [lax.ppermute(block, "patch", way) for block, way in zip(held, pairs)]
            if step == 1:
                held = [after(block, packed) for block in held]
            elif step == 2:
                packed = pack_img([txt] + along[0])
                held = [after(block, packed) for block in held]
            along.append(held)
            against.append([swap(block) for block in held])
        ahead = jnp.where(core == 0, plane, planes - 1 - plane)
    else:
        stale = [stale_kv]
        from_below = from_above = stale_kv
        for step in range(1, planes):
            from_below = lax.ppermute(from_below, "patch", up_pairs(step))
            from_above = lax.ppermute(from_above, "patch", down_pairs(step))
            along.append([from_below])
            against.append([from_above])
        ahead = plane
    entries = [[along[i - 1], against[planes - i - 1]] for i in range(1, planes)]
    first_holds = [ahead >= i for i in range(1, planes)]
    if pair == 1 or planes < 3:
        packed = pack_img([txt] + along[0])
    img = exchange(packed)

    early = planes > 2
    inner = (plane > 0) & (plane < planes - 1)
    info = jnp.stack([core] + first_holds + [inner if early else core >= 0]).astype(jnp.int32)
    known = entries
    if early:
        known = [[along[0]]] + entries[1:-1] + [[against[0]]]
    text_attn = attend(
        "attend_text", functools.partial(text_body, wanted=planes), info, [txt], stale, known, 1
    )
    text_attn = after(text_attn, img)
    img = after(img, text_attn)
    image_attn = attend("attend_image", image_body, info, [img, txt], stale, entries, pair)
    image_back = exchange(image_attn)
    text_out = unpack(after(exchange(text_attn), image_attn), order)
    image_out = project(image_back, order, proj_weight, residual, gate_scale)
    if early:
        ends = [(1, 0), (planes - 2, planes - 1)]
        ends = [(a * pair + c, b * pair + c) for a, b in ends for c in range(pair)]
        hopped = after(lax.ppermute(text_out, "patch", ends), image_out)
        text_out = jnp.where(inner, text_out, hopped)
    if pair == 2:
        other = swap(text_out)
        lower = core == 0
        text_out = jnp.concatenate(
            [jnp.where(lower, text_out, other), jnp.where(lower, other, text_out)], 0
        )

    return (image_out, text_out)


def solution(mesh):
    return jax.shard_map(
        per_device,
        mesh=mesh,
        in_specs=(
            P(("patch", "head"), None),
            P("head", None),
            P(None, "patch", "head"),
            P(("patch", "head"), None),
            P(),
            P(),
        ),
        out_specs=(P(("patch", "head"), None), P("head", None)),
        check_vma=False,
    )
```

```python
import functools
import math

import jax
import jax.numpy as jnp
from jax import lax
from jax.experimental import pallas as pl
from jax.experimental.pallas import tpu as pltpu
from jax.sharding import PartitionSpec as P

HD = 128
SCALE = math.log2(math.e) / math.sqrt(HD)
VMEM_LIMIT = 12 * 1024 * 1024
WIDE_LIMIT = 48 * 1024 * 1024
TILE = 256
TEXT_TILE = 128
FIRST_KEYS = 256
LARGE = 2.0**60


def params(block_elements=0):
    return pltpu.CompilerParams(
        vmem_limit_bytes=VMEM_LIMIT + 4 * block_elements, dimension_semantics=("arbitrary",)
    )


def pack_body(_, *refs):
    sources, packed = refs[:3], refs[-1]
    width = sources[0].shape[1]
    for part, source in enumerate(sources):
        packed[0, :, part * width : (part + 1) * width] = source[...]


def pack(first_block, array, rows, head_owners, pair, width, after=()):
    blocks = array.shape[1] // 3 // width
    destinations = head_owners * pair

    def source(part):
        def place(d, info):
            return (info[0], part * blocks + (d % head_owners) * pair + d // head_owners)

        return pl.BlockSpec((rows, width), place)

    return pl.pallas_call(
        pack_body,
        grid_spec=pltpu.PrefetchScalarGridSpec(
            num_scalar_prefetch=1,
            grid=(destinations,),
            in_specs=[source(0), source(1), source(2)]
            + [pl.BlockSpec(memory_space=pl.ANY)] * len(after),
            out_specs=pl.BlockSpec((1, rows, 3 * width), lambda d, info: (d, 0, 0)),
        ),
        out_shape=jax.ShapeDtypeStruct((destinations, rows, 3 * width), array.dtype),
        compiler_params=params(),
        name="pack_heads",
    )(first_block, array, array, array, *after)


def dot(first, second, contract):
    return lax.dot_general(
        first, second, ((contract[:1], contract[1:]), ((), ())), preferred_element_type=jnp.float32
    )


def with_ones(block):
    return jnp.concatenate([block, jnp.ones_like(block)], axis=1)


def reference_columns(row_max):
    reference = row_max.astype(jnp.bfloat16).astype(jnp.float32)
    return jnp.broadcast_to(reference * (-1.0 / HD), (row_max.shape[0], HD)).astype(jnp.bfloat16)


def weighted(queries, key_rows, values):
    weights = jnp.exp2(dot(queries, key_rows, (1, 1)) * SCALE).astype(jnp.bfloat16)
    return dot(weights, values, (1, 0))


def tiles_of(rows, most):
    tile = min(most, rows)
    return [slice(first, min(first + tile, rows)) for first in range(0, rows, tile)]


def until_small(flag, total, attempt):
    flag[0] = 1

    @pl.loop(0, 2)
    def _(turn):
        @pl.when(flag[0] == 1)
        def _():
            attempt(turn)
            flag[0] = jnp.where(jnp.max(total[:, :, HD:]) > LARGE, 1, 0).astype(jnp.int32)


class Fetch:
    def __init__(self, info, width, sems):
        self.columns = pl.ds(pl.multiple_of(info[0] * width, width), width)
        self.info, self.sems, self.waits = info, sems, []

    def start(self, candidates, flags, target, at):
        rows = candidates[0].shape[1]
        sem = self.sems.at[len(self.waits)]
        copies = [
            pltpu.make_async_copy(
                block.at[:, :, self.columns], target.at[:, pl.ds(at, rows), :], sem
            )
            for block in candidates
        ]
        if len(copies) == 1:
            copies[0].start()
        else:
            for copy, flag in zip(copies, flags):
                pl.when(flag)(copy.start)
        self.waits.append(copies[0])

    def wait(self):
        for copy in self.waits:
            copy.wait()


def settle(fetch, refs, entries, chosen):
    for index, candidates in enumerate(entries):
        sides = []
        for count in candidates:
            sides.append(refs[:count])
            refs = refs[count:]
        first = fetch.info[1 + index]
        at = 0
        for blocks in zip(*sides):
            fetch.start(blocks, [first == 1, first == 0], chosen.at[index], at)
            at += blocks[0].shape[1]


def accumulate(flag, total, aug, heads, queries_of, first_keys_of, own, chosen, tile_rows):
    def columns(head):
        return slice(head * HD, (head + 1) * HD)

    def pieces(head, some):
        return some(head) + [
            (chosen[index, 0, :, columns(head)], chosen[index, 1, :, columns(head)])
            for index in range(chosen.shape[0])
        ]

    def tiles():
        for head in range(heads):
            queries = queries_of(head)
            for span, some in own:
                for tile in tiles_of(span.stop - span.start, tile_rows):
                    tile = slice(span.start + tile.start, span.start + tile.stop)
                    yield head, tile, queries[tile, :], some

    def largest(queries, key_rows):
        return jnp.max(dot(queries, key_rows, (1, 1)), axis=1, keepdims=True)

    def attempt(turn):
        @pl.when(turn == 0)
        def _():
            for head, tile, queries, _ in tiles():
                aug[head, tile, :] = reference_columns(largest(queries, first_keys_of(head)))

        @pl.when(turn == 1)
        def _():
            for head, tile, queries, some in tiles():
                row_max = None
                for key_rows, _ in pieces(head, some):
                    piece_max = largest(queries, key_rows)
                    row_max = piece_max if row_max is None else jnp.maximum(row_max, piece_max)
                aug[head, tile, :] = reference_columns(row_max)

        for head, tile, queries, some in tiles():
            both = jnp.concatenate([queries, aug[head, tile, :]], axis=1)
            summed = None
            for key_rows, values in pieces(head, some):
                part = weighted(both, with_ones(key_rows), with_ones(values))
                summed = part if summed is None else summed + part
            total[head, tile, :] = summed

    until_small(flag, total, attempt)


def finish(out, total):
    for head in range(total.shape[0]):
        attended = (total[head, :, :HD] / total[head, :, HD:]).astype(out.dtype)
        out[:, :, head * HD : (head + 1) * HD] = attended.reshape(out.shape[:2] + (HD,))


def part_of(ref, part, head, width):
    first = part * width + head * HD
    return ref[:, :, first : first + HD].reshape(-1, HD)


def text_body(pair, entries, info, txt, *refs, wanted):
    stale, came = refs[:pair], refs[pair:-7]
    out, chosen, beside, aug, total, flag, sems = refs[-7:]
    width = chosen.shape[3]
    heads = width // HD

    @pl.when(info[wanted] == 1)
    def _():
        fetch = Fetch(info, width, sems)
        at = 0
        for block in stale:
            fetch.start([block], [], beside.at[0], at)
            at += block.shape[1]
        settle(fetch, came, entries, chosen)
        fetch.wait()

        def own(head):
            columns = slice(head * HD, (head + 1) * HD)
            return [
                (part_of(txt, 1, head, width), part_of(txt, 2, head, width)),
                (beside[0, 0, :, columns], beside[0, 1, :, columns]),
            ]

        accumulate(
            flag, total, aug, heads,
            lambda head: part_of(txt, 0, head, width),
            lambda head: part_of(txt, 1, head, width)[: min(FIRST_KEYS, total.shape[1]), :],
            [(slice(0, total.shape[1]), own)], chosen, TEXT_TILE,
        )
        finish(out, total)


def image_body(pair, entries, info, img, txt, *refs):
    stale, came = refs[:pair], refs[pair:-7]
    out, chosen, beside, aug, total, flag, sems = refs[-7:]
    width = chosen.shape[3]
    heads = width // HD
    rows = total.shape[1]
    group_rows, sources = rows // pair, img.shape[0] // pair
    fetch = Fetch(info, width, sems)
    if pair == 2:
        for group in range(pair):
            flags = [info[0] != group, info[0] == group]
            fetch.start(stale, flags, beside.at[group], group_rows)
    settle(fetch, came, entries, chosen)
    for group in range(pair):
        for part in range(2):
            fresh = img[
                group * sources : (group + 1) * sources, :, (1 + part) * width : (2 + part) * width
            ]
            beside[group, part, :group_rows, :] = fresh.reshape(group_rows, width)
    fetch.wait()

    def own(group):
        def some(head):
            columns = slice(head * HD, (head + 1) * HD)
            return [
                (part_of(txt, 1, head, width), part_of(txt, 2, head, width)),
                (beside[group, 0, :, columns], beside[group, 1, :, columns]),
            ]

        return (slice(group * group_rows, (group + 1) * group_rows), some)

    text_keys = txt.shape[0] * txt.shape[1]
    accumulate(
        flag, total, aug, heads,
        lambda head: part_of(img, 0, head, width),
        lambda head: part_of(txt, 1, head, width)[: min(FIRST_KEYS, text_keys), :],
        [own(group) for group in range(pair)], chosen, TILE,
    )
    finish(out, total)


def attend(name, body, info, fresh, stale, entries, groups):
    first = fresh[0]
    width = first.shape[2] // 3
    heads, rows = width // HD, first.shape[0] * first.shape[1]
    keys = sum(block.shape[1] for block in stale)
    came = [b for candidates in entries for blocks in candidates for b in blocks]
    counts = [[len(blocks) for blocks in candidates] for candidates in entries]
    vmem = pl.BlockSpec(memory_space=pltpu.VMEM)
    scratch = [
        ((len(entries), 2, keys, width), first.dtype),
        ((groups, 2, keys, width), first.dtype),
        ((heads, rows, HD), jnp.bfloat16),
        ((heads, rows, 2 * HD), jnp.float32),
    ]
    needed = sum(math.prod(shape) * jnp.dtype(kind).itemsize for shape, kind in scratch)
    return pl.pallas_call(
        functools.partial(body, len(stale), counts),
        in_specs=[pl.BlockSpec(memory_space=pltpu.SMEM)]
        + [vmem] * len(fresh)
        + [pl.BlockSpec(memory_space=pl.ANY)] * (len(stale) + len(came)),
        out_specs=vmem,
        out_shape=jax.ShapeDtypeStruct(first.shape[:2] + (width,), first.dtype),
        scratch_shapes=[pltpu.VMEM(*one) for one in scratch]
        + [
            pltpu.SMEM((1,), jnp.int32),
            pltpu.SemaphoreType.DMA((len(stale) * (1 + len(entries)),)),
        ],
        compiler_params=pltpu.CompilerParams(vmem_limit_bytes=VMEM_LIMIT + needed),
        cost_estimate=pl.CostEstimate(
            flops=4 * rows * keys * (2 + len(entries)) * width,
            bytes_accessed=4 * keys * (2 + len(entries)) * width,
            transcendentals=rows * keys * (2 + len(entries)) * heads,
        ),
        name=name,
    )(info, *fresh, *stale, *came)


def project_body(order, x_ref, weight, residual, gate, out, held, total, sems):
    copies = [
        pltpu.make_async_copy(weight.at[place], held.at[place], sems.at[place])
        for place in order
    ]
    for copy in copies:
        copy.start()
    for source, (place, copy) in enumerate(zip(order, copies)):
        copy.wait()
        part = jnp.dot(x_ref[source], held[place], preferred_element_type=jnp.float32)
        if source == 0:
            total[...] = part
        else:
            total[...] += part
    out[...] = (residual[...].astype(jnp.float32) + gate[...] * total[...]).astype(out.dtype)


def project(x, order, weight, residual, gate):
    rows, model = residual.shape
    destinations, _, width = x.shape
    vmem = pl.BlockSpec(memory_space=pltpu.VMEM)
    return pl.pallas_call(
        functools.partial(project_body, order),
        in_specs=[vmem, pl.BlockSpec(memory_space=pl.ANY), vmem, vmem],
        out_specs=vmem,
        out_shape=jax.ShapeDtypeStruct((rows, model), residual.dtype),
        scratch_shapes=[
            pltpu.VMEM((destinations, width, model), weight.dtype),
            pltpu.VMEM((rows, model), jnp.float32),
            pltpu.SemaphoreType.DMA((destinations,)),
        ],
        compiler_params=pltpu.CompilerParams(vmem_limit_bytes=WIDE_LIMIT),
        cost_estimate=pl.CostEstimate(
            flops=2 * rows * model * model, bytes_accessed=2 * model * model, transcendentals=0
        ),
        name="project",
    )(x, weight.reshape(destinations, width, model), residual, gate.reshape(1, model))


def after_body(x, other, out):
    del other
    out[...] = x[...]


def after(x, other):
    held = pl.BlockSpec(memory_space=pltpu.VMEM)
    return pl.pallas_call(
        after_body,
        in_specs=[held, pl.BlockSpec(memory_space=pl.ANY)],
        out_specs=held,
        out_shape=jax.ShapeDtypeStruct(x.shape, x.dtype),
        name="after",
    )(x, other)


def unpack_body(order, x_ref, out):
    width = x_ref.shape[2]
    for source, place in enumerate(order):
        out[:, place * width : (place + 1) * width] = x_ref[source]


def unpack(x, order):
    rows, model = x.shape[1], x.shape[0] * x.shape[2]
    return pl.pallas_call(
        functools.partial(unpack_body, order),
        grid=(1,),
        in_specs=[pl.BlockSpec(x.shape, lambda n: (0, 0, 0))],
        out_specs=pl.BlockSpec((rows, model), lambda n: (0, 0)),
        out_shape=jax.ShapeDtypeStruct((rows, model), x.dtype),
        compiler_params=params(),
        name="unpack_text",
    )(x)


def per_device(img_qkv, txt_qkv, stale_kv, residual, gate_scale, proj_weight):
    patches, head_owners = lax.axis_size("patch"), lax.axis_size("head")
    patch = lax.axis_index("patch")
    owned_heads = stale_kv.shape[2] // HD
    pair = 2 if patches % 2 == 0 and owned_heads % 2 == 0 else 1
    planes = patches // pair
    plane, core = patch // pair, patch % pair
    width = stale_kv.shape[2] // pair
    heads = width // HD
    img_rows, model = residual.shape
    text_rows = txt_qkv.shape[0] // pair
    destinations = pair * head_owners

    order = [(d % head_owners) * pair + d // head_owners for d in range(destinations)]
    groups = [[g * destinations + d for d in range(destinations)] for g in range(planes)]
    swap_pairs = [(p, p + 1 - 2 * (p % 2)) for p in range(patches)]

    def exchange(x):
        return lax.all_to_all(
            x, ("patch", "head"), split_axis=0, concat_axis=0, axis_index_groups=groups, tiled=True
        )

    def swap(x):
        return lax.ppermute(x, "patch", swap_pairs)

    def up_pairs(step):
        return [(z, z + 1) for z in range(step - 1, planes - 1)]

    def down_pairs(step):
        return [(z + 1, z) for z in range(0, planes - step)]

    def pack_img(earlier):
        first = jnp.zeros((1,), jnp.int32)
        return pack(first, img_qkv, img_rows, head_owners, pair, width, earlier)

    core_only = core.astype(jnp.int32).reshape(1)
    packed = pack(core_only, txt_qkv, text_rows, head_owners, pair, width)
    txt = exchange(packed)

    along, against = [], []
    if pair == 2:
        stale = [stale_kv, swap(stale_kv)]
        held = [stale_kv, stale_kv]
        for step in range(1, planes):
            pairs = [
                [(2 * a + turn, 2 * b) for a, b in up_pairs(step)]
                + [(2 * a + 1 - turn, 2 * b + 1) for a, b in down_pairs(step)]
                for turn in ((0, 1) if step == 1 else (0, 0))
            ]
            held = [lax.ppermute(block, "patch", way) for block, way in zip(held, pairs)]
            if step == 1:
                held = [after(block, packed) for block in held]
            elif step == 2:
                packed = pack_img([txt] + along[0])
                held = [after(block, packed) for block in held]
            along.append(held)
            against.append([swap(block) for block in held])
        ahead = jnp.where(core == 0, plane, planes - 1 - plane)
    else:
        stale = [stale_kv]
        from_below = from_above = stale_kv
        for step in range(1, planes):
            from_below = lax.ppermute(from_below, "patch", up_pairs(step))
            from_above = lax.ppermute(from_above, "patch", down_pairs(step))
            along.append([from_below])
            against.append([from_above])
        ahead = plane
    entries = [[along[i - 1], against[planes - i - 1]] for i in range(1, planes)]
    first_holds = [ahead >= i for i in range(1, planes)]
    if pair == 1 or planes < 3:
        packed = pack_img([txt] + along[0])
    img = exchange(packed)

    early = planes > 2
    inner = (plane > 0) & (plane < planes - 1)
    info = jnp.stack([core] + first_holds + [inner if early else core >= 0]).astype(jnp.int32)
    known = entries
    if early:
        known = [[along[0]]] + entries[1:-1] + [[against[0]]]
    text_attn = attend(
        "attend_text", functools.partial(text_body, wanted=planes), info, [txt], stale, known, 1
    )
    text_attn = after(text_attn, img)
    img = after(img, text_attn)
    image_attn = attend("attend_image", image_body, info, [img, txt], stale, entries, pair)
    image_back = exchange(image_attn)
    text_out = unpack(after(exchange(text_attn), image_attn), order)
    image_out = project(image_back, order, proj_weight, residual, gate_scale)
    if early:
        ends = [(1, 0), (planes - 2, planes - 1)]
        ends = [(a * pair + c, b * pair + c) for a, b in ends for c in range(pair)]
        hopped = after(lax.ppermute(text_out, "patch", ends), image_out)
        text_out = jnp.where(inner, text_out, hopped)
    if pair == 2:
        other = swap(text_out)
        lower = core == 0
        text_out = jnp.concatenate(
            [jnp.where(lower, text_out, other), jnp.where(lower, other, text_out)], 0
        )

    return (image_out, text_out)


def solution(mesh):
    return jax.shard_map(
        per_device,
        mesh=mesh,
        in_specs=(
            P(("patch", "head"), None),
            P("head", None),
            P(None, "patch", "head"),
            P(("patch", "head"), None),
            P(),
            P(),
        ),
        out_specs=(P(("patch", "head"), None), P("head", None)),
        check_vma=False,
    )
```

```python
import functools
import math

import jax
import jax.numpy as jnp
from jax import lax
from jax.experimental import pallas as pl
from jax.experimental.pallas import tpu as pltpu
from jax.sharding import PartitionSpec as P

HD = 128
SCALE = math.log2(math.e) / math.sqrt(HD)
VMEM_LIMIT = 12 * 1024 * 1024
ATTEND_LIMIT = 24 * 1024 * 1024
WIDE_LIMIT = 48 * 1024 * 1024
TILE = 512
FIRST_KEYS = 256
LARGE = 2.0**60


def params(block_elements=0):
    return pltpu.CompilerParams(
        vmem_limit_bytes=VMEM_LIMIT + 4 * block_elements, dimension_semantics=("arbitrary",)
    )


def pack_body(_, *refs):
    sources, packed = refs[:3], refs[-1]
    width = sources[0].shape[1]
    for part, source in enumerate(sources):
        packed[0, :, part * width : (part + 1) * width] = source[...]


def pack(first_block, array, rows, head_owners, pair, width, after=(), weight=1):
    blocks = array.shape[1] // 3 // width
    destinations = head_owners * pair

    def source(part):
        def place(d, info):
            return (info[0], part * blocks + (d % head_owners) * pair + d // head_owners)

        return pl.BlockSpec((rows, width), place)

    return pl.pallas_call(
        pack_body,
        grid_spec=pltpu.PrefetchScalarGridSpec(
            num_scalar_prefetch=1,
            grid=(destinations,),
            in_specs=[source(0), source(1), source(2)]
            + [pl.BlockSpec(memory_space=pl.ANY)] * len(after),
            out_specs=pl.BlockSpec((1, rows, 3 * width), lambda d, info: (d, 0, 0)),
        ),
        out_shape=jax.ShapeDtypeStruct((destinations, rows, 3 * width), array.dtype),
        compiler_params=params(),
        cost_estimate=pl.CostEstimate(
            flops=0, bytes_accessed=weight * 12 * destinations * rows * width, transcendentals=0
        ),
        name="pack_heads",
    )(first_block, array, array, array, *after)


def dot(first, second, contract):
    return lax.dot_general(
        first, second, ((contract[:1], contract[1:]), ((), ())), preferred_element_type=jnp.float32
    )


def with_ones(block):
    return jnp.concatenate([block, jnp.ones_like(block)], axis=1)


def reference_columns(row_max):
    reference = row_max.astype(jnp.bfloat16).astype(jnp.float32)
    return jnp.broadcast_to(reference * (-1.0 / HD), (row_max.shape[0], HD)).astype(jnp.bfloat16)


def weighted(queries, key_rows, values):
    weights = jnp.exp2(dot(queries, key_rows, (1, 1)) * SCALE).astype(jnp.bfloat16)
    return dot(weights, values, (1, 0))


def tiles_of(rows, most):
    tile = min(most, rows)
    return [slice(first, min(first + tile, rows)) for first in range(0, rows, tile)]


def until_small(flag, total, attempt):
    flag[0] = 1

    @pl.loop(0, 2)
    def _(turn):
        @pl.when(flag[0] == 1)
        def _():
            attempt(turn)
            flag[0] = jnp.where(jnp.max(total[:, :, HD:]) > LARGE, 1, 0).astype(jnp.int32)


class Fetch:
    def __init__(self, info, width, sems):
        self.columns = pl.ds(pl.multiple_of(info[0] * width, width), width)
        self.info, self.sems, self.waits = info, sems, []

    def start(self, candidates, flags, target, at):
        rows = candidates[0].shape[1]
        sem = self.sems.at[len(self.waits)]
        copies = [
            pltpu.make_async_copy(
                block.at[:, :, self.columns], target.at[:, pl.ds(at, rows), :], sem
            )
            for block in candidates
        ]
        if len(copies) == 1:
            copies[0].start()
        else:
            for copy, flag in zip(copies, flags):
                pl.when(flag)(copy.start)
        self.waits.append(copies[0])

    def wait(self):
        for copy in self.waits:
            copy.wait()


def settle(fetch, refs, entries, chosen):
    for index, candidates in enumerate(entries):
        sides = []
        for count in candidates:
            sides.append(refs[:count])
            refs = refs[count:]
        first = fetch.info[1 + index]
        at = 0
        for blocks in zip(*sides):
            fetch.start(blocks, [first == 1, first == 0], chosen.at[index], at)
            at += blocks[0].shape[1]


def accumulate(flag, total, aug, heads, queries_of, first_of, shared_of, own, chosen):
    rows = total.shape[1]

    def columns(head):
        return slice(head * HD, (head + 1) * HD)

    def shared(head):
        return shared_of(head) + [
            (chosen[index, 0, :, columns(head)], chosen[index, 1, :, columns(head)])
            for index in range(chosen.shape[0])
        ]

    def largest(queries, some):
        row_max = None
        for key_rows, _ in some:
            piece_max = jnp.max(dot(queries, key_rows, (1, 1)), axis=1, keepdims=True)
            row_max = piece_max if row_max is None else jnp.maximum(row_max, piece_max)
        return row_max

    def attempt(turn):
        @pl.when(turn == 0)
        def _():
            for head in range(heads):
                queries = queries_of(head)
                for tile in tiles_of(rows, TILE):
                    aug[head, tile, :] = reference_columns(
                        largest(queries[tile, :], [(first_of(head), None)])
                    )

        @pl.when(turn == 1)
        def _():
            for head in range(heads):
                queries = queries_of(head)
                for span, some in own:
                    row_max = largest(queries[span, :], shared(head) + some(head))
                    aug[head, span, :] = reference_columns(row_max)

        for head in range(heads):
            both = jnp.concatenate([queries_of(head), aug[head]], axis=1)
            for tile in tiles_of(rows, TILE):
                summed = None
                for key_rows, values in shared(head):
                    part = weighted(both[tile, :], with_ones(key_rows), with_ones(values))
                    summed = part if summed is None else summed + part
                total[head, tile, :] = summed
            for span, some in own:
                for key_rows, values in some(head):
                    total[head, span, :] += weighted(
                        both[span, :], with_ones(key_rows), with_ones(values)
                    )

    until_small(flag, total, attempt)


def finish(out, total):
    for head in range(total.shape[0]):
        attended = (total[head, :, :HD] / total[head, :, HD:]).astype(out.dtype)
        out[:, :, head * HD : (head + 1) * HD] = attended.reshape(out.shape[:2] + (HD,))


def part_of(ref, part, head, width):
    first = part * width + head * HD
    return ref[:, :, first : first + HD].reshape(-1, HD)


def text_body(pair, entries, info, txt, *refs, wanted):
    stale, came = refs[:pair], refs[pair:-10]
    result, held_txt, out, chosen, beside, aug, total, flag, sems, plain = refs[-10:]
    width = chosen.shape[3]
    heads = width // HD

    @pl.when(info[wanted] == 1)
    def _():
        fetch = Fetch(info, width, sems)
        whole = pltpu.make_async_copy(txt, held_txt, plain.at[0])
        whole.start()
        at = 0
        for block in stale:
            fetch.start([block], [], beside.at[0], at)
            at += block.shape[1]
        settle(fetch, came, entries, chosen)
        whole.wait()
        fetch.wait()

        def shared(head):
            columns = slice(head * HD, (head + 1) * HD)
            return [
                (part_of(held_txt, 1, head, width), part_of(held_txt, 2, head, width)),
                (beside[0, 0, :, columns], beside[0, 1, :, columns]),
            ]

        accumulate(
            flag, total, aug, heads,
            lambda head: part_of(held_txt, 0, head, width),
            lambda head: part_of(held_txt, 1, head, width)[: min(FIRST_KEYS, total.shape[1]), :],
            shared, [(slice(0, total.shape[1]), lambda head: [])], chosen,
        )
        finish(out, total)
        back = pltpu.make_async_copy(out, result, plain.at[0])
        back.start()
        back.wait()


def image_body(pair, entries, info, img, txt, *refs):
    stale, came = refs[:pair], refs[pair:-12]
    (result, held_img, held_txt, out, chosen, beside, aug, total, flag, sems, plain) = refs[-11:]
    width = chosen.shape[3]
    heads = width // HD
    rows = total.shape[1]
    group_rows, sources = rows // pair, img.shape[0] // pair
    fetch = Fetch(info, width, sems)
    wholes = [
        pltpu.make_async_copy(source, target, plain.at[index])
        for index, (source, target) in enumerate(((txt, held_txt), (img, held_img)))
    ]
    for whole in wholes:
        whole.start()
    if pair == 2:
        for group in range(pair):
            flags = [info[0] != group, info[0] == group]
            fetch.start(stale, flags, beside.at[group], group_rows)
    settle(fetch, came, entries, chosen)
    for whole in wholes:
        whole.wait()
    for group in range(pair):
        for part in range(2):
            fresh = held_img[
                group * sources : (group + 1) * sources, :, (1 + part) * width : (2 + part) * width
            ]
            beside[group, part, :group_rows, :] = fresh.reshape(group_rows, width)
    fetch.wait()

    def own(group):
        def some(head):
            columns = slice(head * HD, (head + 1) * HD)
            return [(beside[group, 0, :, columns], beside[group, 1, :, columns])]

        return (slice(group * group_rows, (group + 1) * group_rows), some)

    text_keys = txt.shape[0] * txt.shape[1]
    accumulate(
        flag, total, aug, heads,
        lambda head: part_of(held_img, 0, head, width),
        lambda head: part_of(held_txt, 1, head, width)[: min(FIRST_KEYS, text_keys), :],
        lambda head: [(part_of(held_txt, 1, head, width), part_of(held_txt, 2, head, width))],
        [own(group) for group in range(pair)], chosen,
    )
    finish(out, total)
    back = pltpu.make_async_copy(out, result, plain.at[0])
    back.start()
    back.wait()


def attend(name, body, info, fresh, stale, entries, groups, earlier=()):
    first = fresh[0]
    width = first.shape[2] // 3
    heads, rows = width // HD, first.shape[0] * first.shape[1]
    keys = sum(block.shape[1] for block in stale)
    came = [b for candidates in entries for blocks in candidates for b in blocks]
    counts = [[len(blocks) for blocks in candidates] for candidates in entries]
    anywhere = pl.BlockSpec(memory_space=pl.ANY)
    result = jax.ShapeDtypeStruct(first.shape[:2] + (width,), first.dtype)
    scratch = [(array.shape, array.dtype) for array in fresh] + [
        (result.shape, result.dtype),
        ((len(entries), 2, keys, width), first.dtype),
        ((groups, 2, keys, width), first.dtype),
        ((heads, rows, HD), jnp.bfloat16),
        ((heads, rows, 2 * HD), jnp.float32),
    ]
    operands = [*fresh, *stale, *came, *earlier]
    return pl.pallas_call(
        functools.partial(body, len(stale), counts),
        in_specs=[pl.BlockSpec(memory_space=pltpu.SMEM)] + [anywhere] * len(operands),
        out_specs=anywhere,
        out_shape=result,
        scratch_shapes=[pltpu.VMEM(*one) for one in scratch]
        + [
            pltpu.SMEM((1,), jnp.int32),
            pltpu.SemaphoreType.DMA((len(stale) * (1 + len(entries)),)),
            pltpu.SemaphoreType.DMA((2,)),
        ],
        compiler_params=pltpu.CompilerParams(vmem_limit_bytes=ATTEND_LIMIT),
        cost_estimate=pl.CostEstimate(
            flops=4 * rows * keys * (2 + len(entries)) * width,
            bytes_accessed=4 * keys * (2 + len(entries)) * width,
            transcendentals=rows * keys * (2 + len(entries)) * heads,
        ),
        name=name,
    )(info, *operands)


def project_body(order, x_ref, weight, residual, gate, out, held, total, sems):
    copies = [
        pltpu.make_async_copy(weight.at[place], held.at[place], sems.at[place])
        for place in order
    ]
    for copy in copies:
        copy.start()
    for source, (place, copy) in enumerate(zip(order, copies)):
        copy.wait()
        part = jnp.dot(x_ref[source], held[place], preferred_element_type=jnp.float32)
        if source == 0:
            total[...] = part
        else:
            total[...] += part
    out[...] = (residual[...].astype(jnp.float32) + gate[...] * total[...]).astype(out.dtype)


def project(x, order, weight, residual, gate):
    rows, model = residual.shape
    destinations, _, width = x.shape
    vmem = pl.BlockSpec(memory_space=pltpu.VMEM)
    return pl.pallas_call(
        functools.partial(project_body, order),
        in_specs=[vmem, pl.BlockSpec(memory_space=pl.ANY), vmem, vmem],
        out_specs=vmem,
        out_shape=jax.ShapeDtypeStruct((rows, model), residual.dtype),
        scratch_shapes=[
            pltpu.VMEM((destinations, width, model), weight.dtype),
            pltpu.VMEM((rows, model), jnp.float32),
            pltpu.SemaphoreType.DMA((destinations,)),
        ],
        compiler_params=pltpu.CompilerParams(vmem_limit_bytes=WIDE_LIMIT),
        cost_estimate=pl.CostEstimate(
            flops=2 * rows * model * model, bytes_accessed=2 * model * model, transcendentals=0
        ),
        name="project",
    )(x, weight.reshape(destinations, width, model), residual, gate.reshape(1, model))


def unpack_body(order, x_ref, earlier, out):
    del earlier
    width = x_ref.shape[2]
    for source, place in enumerate(order):
        out[:, place * width : (place + 1) * width] = x_ref[source]


def unpack(x, order, earlier):
    rows, model = x.shape[1], x.shape[0] * x.shape[2]
    vmem = pl.BlockSpec(memory_space=pltpu.VMEM)
    return pl.pallas_call(
        functools.partial(unpack_body, order),
        in_specs=[vmem, pl.BlockSpec(memory_space=pl.ANY)],
        out_specs=vmem,
        out_shape=jax.ShapeDtypeStruct((rows, model), x.dtype),
        name="unpack_text",
    )(x, earlier)


def choose_body(flag, first, second, earlier, out):
    del earlier

    @pl.when(flag[0] == 1)
    def _():
        out[...] = first[...]

    @pl.when(flag[0] == 0)
    def _():
        out[...] = second[...]


def choose(flag, first, second, earlier):
    vmem = pl.BlockSpec(memory_space=pltpu.VMEM)
    return pl.pallas_call(
        choose_body,
        in_specs=[pl.BlockSpec(memory_space=pltpu.SMEM), vmem, vmem]
        + [pl.BlockSpec(memory_space=pl.ANY)],
        out_specs=vmem,
        out_shape=jax.ShapeDtypeStruct(first.shape, first.dtype),
        name="choose_text",
    )(flag, first, second, earlier)


def per_device(img_qkv, txt_qkv, stale_kv, residual, gate_scale, proj_weight):
    patches, head_owners = lax.axis_size("patch"), lax.axis_size("head")
    patch = lax.axis_index("patch")
    owned_heads = stale_kv.shape[2] // HD
    pair = 2 if patches % 2 == 0 and owned_heads % 2 == 0 else 1
    planes = patches // pair
    plane, core = patch // pair, patch % pair
    width = stale_kv.shape[2] // pair
    heads = width // HD
    img_rows, model = residual.shape
    text_rows = txt_qkv.shape[0] // pair
    destinations = pair * head_owners

    order = [(d % head_owners) * pair + d // head_owners for d in range(destinations)]
    groups = [[g * destinations + d for d in range(destinations)] for g in range(planes)]
    swap_pairs = [(p, p + 1 - 2 * (p % 2)) for p in range(patches)]

    def exchange(x):
        return lax.all_to_all(
            x, ("patch", "head"), split_axis=0, concat_axis=0, axis_index_groups=groups, tiled=True
        )

    def swap(x):
        return lax.ppermute(x, "patch", swap_pairs)

    def up_pairs(step):
        return [(z, z + 1) for z in range(step - 1, planes - 1)]

    def down_pairs(step):
        return [(z + 1, z) for z in range(0, planes - step)]

    core_only = core.astype(jnp.int32).reshape(1)
    txt = exchange(pack(core_only, txt_qkv, text_rows, head_owners, pair, width))

    along, against = [], []
    if pair == 2:
        stale = [stale_kv, swap(stale_kv)]
        held = [stale_kv, stale_kv]
        for step in range(1, planes):
            pairs = [
                [(2 * a + turn, 2 * b) for a, b in up_pairs(step)]
                + [(2 * a + 1 - turn, 2 * b + 1) for a, b in down_pairs(step)]
                for turn in ((0, 1) if step == 1 else (0, 0))
            ]
            held = [lax.ppermute(block, "patch", way) for block, way in zip(held, pairs)]
            along.append(held)
            against.append([swap(block) for block in held])
        ahead = jnp.where(core == 0, plane, planes - 1 - plane)
    else:
        stale = [stale_kv]
        from_below = from_above = stale_kv
        for step in range(1, planes):
            from_below = lax.ppermute(from_below, "patch", up_pairs(step))
            from_above = lax.ppermute(from_above, "patch", down_pairs(step))
            along.append([from_below])
            against.append([from_above])
        ahead = plane
    entries = [[along[i - 1], against[planes - i - 1]] for i in range(1, planes)]
    first_holds = [ahead >= i for i in range(1, planes)]
    zero_only = jnp.zeros((1,), jnp.int32)
    img = exchange(
        pack(zero_only, img_qkv, img_rows, head_owners, pair, width, [txt] + along[0], 64)
    )

    early = planes > 2
    inner = (plane > 0) & (plane < planes - 1)
    info = jnp.stack([core] + first_holds + [inner if early else core >= 0]).astype(jnp.int32)
    known = entries
    if early:
        known = [[along[0]]] + entries[1:-1] + [[against[0]]]
    text_attn = attend(
        "attend_text", functools.partial(text_body, wanted=planes), info, [txt], stale, known, 1
    )
    image_attn = attend(
        "attend_image", image_body, info, [img, txt], stale, entries, pair, [text_attn]
    )
    text_out = unpack(exchange(text_attn), order, image_attn)
    image_out = project(exchange(image_attn), order, proj_weight, residual, gate_scale)
    if early:
        ends = [(1, 0), (planes - 2, planes - 1)]
        ends = [(a * pair + c, b * pair + c) for a, b in ends for c in range(pair)]
        hopped = lax.ppermute(text_out, "patch", ends)
        text_out = choose(inner.astype(jnp.int32).reshape(1), text_out, hopped, image_out)
    if pair == 2:
        other = swap(text_out)
        lower = core == 0
        text_out = jnp.concatenate(
            [jnp.where(lower, text_out, other), jnp.where(lower, other, text_out)], 0
        )

    return (image_out, text_out)


def solution(mesh):
    return jax.shard_map(
        per_device,
        mesh=mesh,
        in_specs=(
            P(("patch", "head"), None),
            P("head", None),
            P(None, "patch", "head"),
            P(("patch", "head"), None),
            P(),
            P(),
        ),
        out_specs=(P(("patch", "head"), None), P("head", None)),
        check_vma=False,
    )
```

```python
import functools
import math

import jax
import jax.numpy as jnp
from jax import lax
from jax.experimental import pallas as pl
from jax.experimental.pallas import tpu as pltpu
from jax.sharding import PartitionSpec as P

HD = 128
SCALE = math.log2(math.e) / math.sqrt(HD)
VMEM_LIMIT = 12 * 1024 * 1024
ATTEND_LIMIT = 24 * 1024 * 1024
WIDE_LIMIT = 48 * 1024 * 1024
TILE = 256
FIRST_KEYS = 256
LARGE = 2.0**60


def params(block_elements=0):
    return pltpu.CompilerParams(
        vmem_limit_bytes=VMEM_LIMIT + 4 * block_elements, dimension_semantics=("arbitrary",)
    )


def pack_body(_, *refs):
    sources, packed = refs[:3], refs[-1]
    width = sources[0].shape[1]
    for part, source in enumerate(sources):
        packed[0, :, part * width : (part + 1) * width] = source[...]


def pack(first_block, array, rows, head_owners, pair, width, after=(), weight=1):
    blocks = array.shape[1] // 3 // width
    destinations = head_owners * pair

    def source(part):
        def place(d, info):
            return (info[0], part * blocks + (d % head_owners) * pair + d // head_owners)

        return pl.BlockSpec((rows, width), place)

    return pl.pallas_call(
        pack_body,
        grid_spec=pltpu.PrefetchScalarGridSpec(
            num_scalar_prefetch=1,
            grid=(destinations,),
            in_specs=[source(0), source(1), source(2)]
            + [pl.BlockSpec(memory_space=pl.ANY)] * len(after),
            out_specs=pl.BlockSpec((1, rows, 3 * width), lambda d, info: (d, 0, 0)),
        ),
        out_shape=jax.ShapeDtypeStruct((destinations, rows, 3 * width), array.dtype),
        compiler_params=params(),
        cost_estimate=pl.CostEstimate(
            flops=0, bytes_accessed=weight * 12 * destinations * rows * width, transcendentals=0
        ),
        name="pack_heads",
    )(first_block, array, array, array, *after)


def dot(first, second, contract):
    return lax.dot_general(
        first, second, ((contract[:1], contract[1:]), ((), ())), preferred_element_type=jnp.float32
    )


def with_ones(block):
    return jnp.concatenate([block, jnp.ones_like(block)], axis=1)


def reference_columns(row_max):
    reference = row_max.astype(jnp.bfloat16).astype(jnp.float32)
    return jnp.broadcast_to(reference * (-1.0 / HD), (row_max.shape[0], HD)).astype(jnp.bfloat16)


def weighted(queries, key_rows, values):
    weights = jnp.exp2(dot(queries, key_rows, (1, 1)) * SCALE).astype(jnp.bfloat16)
    return dot(weights, values, (1, 0))


def tiles_of(rows, most):
    tile = min(most, rows)
    return [slice(first, min(first + tile, rows)) for first in range(0, rows, tile)]


def until_small(flag, total, attempt):
    flag[0] = 1

    @pl.loop(0, 2)
    def _(turn):
        @pl.when(flag[0] == 1)
        def _():
            attempt(turn)
            flag[0] = jnp.where(jnp.max(total[:, :, HD:]) > LARGE, 1, 0).astype(jnp.int32)


class Fetch:
    def __init__(self, info, width, sems):
        self.columns = pl.ds(pl.multiple_of(info[0] * width, width), width)
        self.info, self.sems, self.waits = info, sems, []

    def start(self, candidates, flags, target, at):
        rows = candidates[0].shape[1]
        sem = self.sems.at[len(self.waits)]
        copies = [
            pltpu.make_async_copy(
                block.at[:, :, self.columns], target.at[:, pl.ds(at, rows), :], sem
            )
            for block in candidates
        ]
        if len(copies) == 1:
            copies[0].start()
        else:
            for copy, flag in zip(copies, flags):
                pl.when(flag)(copy.start)
        self.waits.append(copies[0])

    def wait(self):
        for copy in self.waits:
            copy.wait()


def settle(fetch, refs, entries, chosen):
    for index, candidates in enumerate(entries):
        sides = []
        for count in candidates:
            sides.append(refs[:count])
            refs = refs[count:]
        first = fetch.info[1 + index]
        at = 0
        for blocks in zip(*sides):
            fetch.start(blocks, [first == 1, first == 0], chosen.at[index], at)
            at += blocks[0].shape[1]


def accumulate(flag, total, aug, heads, queries_of, first_keys_of, own, chosen):
    def columns(head):
        return slice(head * HD, (head + 1) * HD)

    def pieces(head, some):
        return some(head) + [
            (chosen[index, 0, :, columns(head)], chosen[index, 1, :, columns(head)])
            for index in range(chosen.shape[0])
        ]

    def tiles():
        for head in range(heads):
            queries = queries_of(head)
            for span, some in own:
                for tile in tiles_of(span.stop - span.start, TILE):
                    tile = slice(span.start + tile.start, span.start + tile.stop)
                    yield head, tile, queries[tile, :], some

    def largest(queries, key_rows):
        return jnp.max(dot(queries, key_rows, (1, 1)), axis=1, keepdims=True)

    def attempt(turn):
        @pl.when(turn == 0)
        def _():
            for head, tile, queries, _ in tiles():
                aug[head, tile, :] = reference_columns(largest(queries, first_keys_of(head)))

        @pl.when(turn == 1)
        def _():
            for head, tile, queries, some in tiles():
                row_max = None
                for key_rows, _ in pieces(head, some):
                    piece_max = largest(queries, key_rows)
                    row_max = piece_max if row_max is None else jnp.maximum(row_max, piece_max)
                aug[head, tile, :] = reference_columns(row_max)

        for head, tile, queries, some in tiles():
            both = jnp.concatenate([queries, aug[head, tile, :]], axis=1)
            summed = None
            for key_rows, values in pieces(head, some):
                part = weighted(both, with_ones(key_rows), with_ones(values))
                summed = part if summed is None else summed + part
            total[head, tile, :] = summed

    until_small(flag, total, attempt)


def finish(out, total):
    for head in range(total.shape[0]):
        attended = (total[head, :, :HD] / total[head, :, HD:]).astype(out.dtype)
        out[:, :, head * HD : (head + 1) * HD] = attended.reshape(out.shape[:2] + (HD,))


def part_of(ref, part, head, width):
    first = part * width + head * HD
    return ref[:, :, first : first + HD].reshape(-1, HD)


def text_body(pair, entries, info, txt, *refs, wanted):
    stale, came = refs[:pair], refs[pair:-10]
    result, held_txt, out, chosen, beside, aug, total, flag, sems, plain = refs[-10:]
    width = chosen.shape[3]
    heads = width // HD

    @pl.when(info[wanted] == 1)
    def _():
        fetch = Fetch(info, width, sems)
        whole = pltpu.make_async_copy(txt, held_txt, plain.at[0])
        whole.start()
        at = 0
        for block in stale:
            fetch.start([block], [], beside.at[0], at)
            at += block.shape[1]
        settle(fetch, came, entries, chosen)
        whole.wait()
        fetch.wait()

        def own(head):
            columns = slice(head * HD, (head + 1) * HD)
            return [
                (part_of(held_txt, 1, head, width), part_of(held_txt, 2, head, width)),
                (beside[0, 0, :, columns], beside[0, 1, :, columns]),
            ]

        accumulate(
            flag, total, aug, heads,
            lambda head: part_of(held_txt, 0, head, width),
            lambda head: part_of(held_txt, 1, head, width)[: min(FIRST_KEYS, total.shape[1]), :],
            [(slice(0, total.shape[1]), own)], chosen,
        )
        finish(out, total)
        back = pltpu.make_async_copy(out, result, plain.at[0])
        back.start()
        back.wait()


def image_body(pair, entries, info, img, txt, *refs):
    stale, came = refs[:pair], refs[pair:-12]
    (result, held_img, held_txt, out, chosen, beside, aug, total, flag, sems, plain) = refs[-11:]
    width = chosen.shape[3]
    heads = width // HD
    rows = total.shape[1]
    group_rows, sources = rows // pair, img.shape[0] // pair
    fetch = Fetch(info, width, sems)
    wholes = [
        pltpu.make_async_copy(source, target, plain.at[index])
        for index, (source, target) in enumerate(((txt, held_txt), (img, held_img)))
    ]
    for whole in wholes:
        whole.start()
    if pair == 2:
        for group in range(pair):
            flags = [info[0] != group, info[0] == group]
            fetch.start(stale, flags, beside.at[group], group_rows)
    settle(fetch, came, entries, chosen)
    for whole in wholes:
        whole.wait()
    for group in range(pair):
        for part in range(2):
            fresh = held_img[
                group * sources : (group + 1) * sources, :, (1 + part) * width : (2 + part) * width
            ]
            beside[group, part, :group_rows, :] = fresh.reshape(group_rows, width)
    fetch.wait()

    def own(group):
        def some(head):
            columns = slice(head * HD, (head + 1) * HD)
            return [
                (part_of(held_txt, 1, head, width), part_of(held_txt, 2, head, width)),
                (beside[group, 0, :, columns], beside[group, 1, :, columns]),
            ]

        return (slice(group * group_rows, (group + 1) * group_rows), some)

    text_keys = txt.shape[0] * txt.shape[1]
    accumulate(
        flag, total, aug, heads,
        lambda head: part_of(held_img, 0, head, width),
        lambda head: part_of(held_txt, 1, head, width)[: min(FIRST_KEYS, text_keys), :],
        [own(group) for group in range(pair)], chosen,
    )
    finish(out, total)
    back = pltpu.make_async_copy(out, result, plain.at[0])
    back.start()
    back.wait()


def attend(name, body, info, fresh, stale, entries, groups, earlier=()):
    first = fresh[0]
    width = first.shape[2] // 3
    heads, rows = width // HD, first.shape[0] * first.shape[1]
    keys = sum(block.shape[1] for block in stale)
    came = [b for candidates in entries for blocks in candidates for b in blocks]
    counts = [[len(blocks) for blocks in candidates] for candidates in entries]
    anywhere = pl.BlockSpec(memory_space=pl.ANY)
    result = jax.ShapeDtypeStruct(first.shape[:2] + (width,), first.dtype)
    scratch = [(array.shape, array.dtype) for array in fresh] + [
        (result.shape, result.dtype),
        ((len(entries), 2, keys, width), first.dtype),
        ((groups, 2, keys, width), first.dtype),
        ((heads, rows, HD), jnp.bfloat16),
        ((heads, rows, 2 * HD), jnp.float32),
    ]
    operands = [*fresh, *stale, *came, *earlier]
    return pl.pallas_call(
        functools.partial(body, len(stale), counts),
        in_specs=[pl.BlockSpec(memory_space=pltpu.SMEM)] + [anywhere] * len(operands),
        out_specs=anywhere,
        out_shape=result,
        scratch_shapes=[pltpu.VMEM(*one) for one in scratch]
        + [
            pltpu.SMEM((1,), jnp.int32),
            pltpu.SemaphoreType.DMA((len(stale) * (1 + len(entries)),)),
            pltpu.SemaphoreType.DMA((2,)),
        ],
        compiler_params=pltpu.CompilerParams(vmem_limit_bytes=ATTEND_LIMIT),
        cost_estimate=pl.CostEstimate(
            flops=4 * rows * keys * (2 + len(entries)) * width,
            bytes_accessed=4 * keys * (2 + len(entries)) * width,
            transcendentals=rows * keys * (2 + len(entries)) * heads,
        ),
        name=name,
    )(info, *operands)


def project_body(order, x_ref, weight, residual, gate, out, held, total, sems):
    copies = [
        pltpu.make_async_copy(weight.at[place], held.at[place], sems.at[place])
        for place in order
    ]
    for copy in copies:
        copy.start()
    for source, (place, copy) in enumerate(zip(order, copies)):
        copy.wait()
        part = jnp.dot(x_ref[source], held[place], preferred_element_type=jnp.float32)
        if source == 0:
            total[...] = part
        else:
            total[...] += part
    out[...] = (residual[...].astype(jnp.float32) + gate[...] * total[...]).astype(out.dtype)


def project(x, order, weight, residual, gate):
    rows, model = residual.shape
    destinations, _, width = x.shape
    vmem = pl.BlockSpec(memory_space=pltpu.VMEM)
    return pl.pallas_call(
        functools.partial(project_body, order),
        in_specs=[vmem, pl.BlockSpec(memory_space=pl.ANY), vmem, vmem],
        out_specs=vmem,
        out_shape=jax.ShapeDtypeStruct((rows, model), residual.dtype),
        scratch_shapes=[
            pltpu.VMEM((destinations, width, model), weight.dtype),
            pltpu.VMEM((rows, model), jnp.float32),
            pltpu.SemaphoreType.DMA((destinations,)),
        ],
        compiler_params=pltpu.CompilerParams(vmem_limit_bytes=WIDE_LIMIT),
        cost_estimate=pl.CostEstimate(
            flops=2 * rows * model * model, bytes_accessed=2 * model * model, transcendentals=0
        ),
        name="project",
    )(x, weight.reshape(destinations, width, model), residual, gate.reshape(1, model))


def unpack_body(order, x_ref, earlier, out):
    del earlier
    width = x_ref.shape[2]
    for source, place in enumerate(order):
        out[:, place * width : (place + 1) * width] = x_ref[source]


def unpack(x, order, earlier):
    rows, model = x.shape[1], x.shape[0] * x.shape[2]
    vmem = pl.BlockSpec(memory_space=pltpu.VMEM)
    return pl.pallas_call(
        functools.partial(unpack_body, order),
        in_specs=[vmem, pl.BlockSpec(memory_space=pl.ANY)],
        out_specs=vmem,
        out_shape=jax.ShapeDtypeStruct((rows, model), x.dtype),
        name="unpack_text",
    )(x, earlier)


def after_body(*refs):
    del refs


def after(x, other):
    anywhere = pl.BlockSpec(memory_space=pl.ANY)
    return pl.pallas_call(
        after_body,
        in_specs=[anywhere, anywhere],
        out_specs=anywhere,
        out_shape=jax.ShapeDtypeStruct(x.shape, x.dtype),
        input_output_aliases={0: 0},
        name="after",
    )(x, other)


def flag_body(flag, earlier, out):
    del earlier
    out[0] = flag[0]


def flag_after(flag, earlier):
    smem = pl.BlockSpec(memory_space=pltpu.SMEM)
    return pl.pallas_call(
        flag_body,
        in_specs=[smem, pl.BlockSpec(memory_space=pl.ANY)],
        out_specs=smem,
        out_shape=jax.ShapeDtypeStruct(flag.shape, flag.dtype),
        name="flag_after",
    )(flag, earlier)


def stack_body(core, mine, other, out):
    rows = mine.shape[0]

    @pl.when(core[0] == 0)
    def _():
        out[:rows, :] = mine[...]
        out[rows:, :] = other[...]

    @pl.when(core[0] == 1)
    def _():
        out[:rows, :] = other[...]
        out[rows:, :] = mine[...]


def stack_text(core, mine, other):
    vmem = pl.BlockSpec(memory_space=pltpu.VMEM)
    return pl.pallas_call(
        stack_body,
        in_specs=[pl.BlockSpec(memory_space=pltpu.SMEM), vmem, vmem],
        out_specs=vmem,
        out_shape=jax.ShapeDtypeStruct((2 * mine.shape[0], mine.shape[1]), mine.dtype),
        name="stack_text",
    )(core, mine, other)


def per_device(img_qkv, txt_qkv, stale_kv, residual, gate_scale, proj_weight):
    patches, head_owners = lax.axis_size("patch"), lax.axis_size("head")
    patch = lax.axis_index("patch")
    owned_heads = stale_kv.shape[2] // HD
    pair = 2 if patches % 2 == 0 and owned_heads % 2 == 0 else 1
    planes = patches // pair
    plane, core = patch // pair, patch % pair
    width = stale_kv.shape[2] // pair
    heads = width // HD
    img_rows, model = residual.shape
    text_rows = txt_qkv.shape[0] // pair
    destinations = pair * head_owners

    order = [(d % head_owners) * pair + d // head_owners for d in range(destinations)]
    groups = [[g * destinations + d for d in range(destinations)] for g in range(planes)]
    swap_pairs = [(p, p + 1 - 2 * (p % 2)) for p in range(patches)]

    def exchange(x):
        return lax.all_to_all(
            x, ("patch", "head"), split_axis=0, concat_axis=0, axis_index_groups=groups, tiled=True
        )

    def swap(x):
        return lax.ppermute(x, "patch", swap_pairs)

    def up_pairs(step):
        return [(z, z + 1) for z in range(step - 1, planes - 1)]

    def down_pairs(step):
        return [(z + 1, z) for z in range(0, planes - step)]

    core_only = core.astype(jnp.int32).reshape(1)
    packed_txt = pack(core_only, txt_qkv, text_rows, head_owners, pair, width)
    txt = exchange(packed_txt)

    along, against = [], []
    if pair == 2:
        stale = [stale_kv, swap(stale_kv)]
        held = [stale_kv, stale_kv]
        for step in range(1, planes):
            pairs = [
                [(2 * a + turn, 2 * b) for a, b in up_pairs(step)]
                + [(2 * a + 1 - turn, 2 * b + 1) for a, b in down_pairs(step)]
                for turn in ((0, 1) if step == 1 else (0, 0))
            ]
            held = [lax.ppermute(block, "patch", way) for block, way in zip(held, pairs)]
            if step == 1:
                held = [after(block, packed_txt) for block in held]
            along.append(held)
            against.append([swap(block) for block in held])
        ahead = jnp.where(core == 0, plane, planes - 1 - plane)
    else:
        stale = [stale_kv]
        from_below = from_above = stale_kv
        for step in range(1, planes):
            from_below = lax.ppermute(from_below, "patch", up_pairs(step))
            from_above = lax.ppermute(from_above, "patch", down_pairs(step))
            along.append([from_below])
            against.append([from_above])
        ahead = plane
    entries = [[along[i - 1], against[planes - i - 1]] for i in range(1, planes)]
    first_holds = [ahead >= i for i in range(1, planes)]
    zero_only = jnp.zeros((1,), jnp.int32)
    img = exchange(
        pack(zero_only, img_qkv, img_rows, head_owners, pair, width, [txt])
    )

    early = planes > 2
    inner = (plane > 0) & (plane < planes - 1)
    info = jnp.stack([core] + first_holds + [inner if early else core >= 0]).astype(jnp.int32)
    known = entries
    if early:
        known = [[along[0]]] + entries[1:-1] + [[against[0]]]
    text_attn = attend(
        "attend_text", functools.partial(text_body, wanted=planes), info, [txt], stale, known, 1
    )
    image_attn = attend(
        "attend_image", image_body, info, [img, txt], stale, entries, pair, [text_attn]
    )
    text_out = unpack(exchange(text_attn), order, image_attn)
    image_out = project(exchange(image_attn), order, proj_weight, residual, gate_scale)
    if early:
        ends = [(1, 0), (planes - 2, planes - 1)]
        ends = [(a * pair + c, b * pair + c) for a, b in ends for c in range(pair)]
        hopped = lax.ppermute(text_out, "patch", ends)
        keep = flag_after(inner.astype(jnp.int32).reshape(1), image_out)
        text_out = jnp.where(keep[0] == 1, text_out, hopped)
    if pair == 2:
        text_out = stack_text(core_only, text_out, swap(text_out))
    return (image_out, text_out)


def solution(mesh):
    return jax.shard_map(
        per_device,
        mesh=mesh,
        in_specs=(
            P(("patch", "head"), None),
            P("head", None),
            P(None, "patch", "head"),
            P(("patch", "head"), None),
            P(),
            P(),
        ),
        out_specs=(P(("patch", "head"), None), P("head", None)),
        check_vma=False,
    )
```

```python
import functools
import math

import jax
import jax.numpy as jnp
from jax import lax
from jax.experimental import pallas as pl
from jax.experimental.pallas import tpu as pltpu
from jax.sharding import PartitionSpec as P

HD = 128
SCALE = math.log2(math.e) / math.sqrt(HD)
VMEM_LIMIT = 12 * 1024 * 1024
ATTEND_LIMIT = 24 * 1024 * 1024
WIDE_LIMIT = 48 * 1024 * 1024
TILE = 256
FIRST_KEYS = 256
LARGE = 2.0**60


def params(block_elements=0):
    return pltpu.CompilerParams(
        vmem_limit_bytes=VMEM_LIMIT + 4 * block_elements, dimension_semantics=("arbitrary",)
    )


def pack_body(_, *refs):
    sources, packed = refs[:3], refs[-1]
    width = sources[0].shape[1]
    for part, source in enumerate(sources):
        packed[0, :, part * width : (part + 1) * width] = source[...]


def pack(first_block, array, rows, head_owners, pair, width, after=(), weight=1):
    blocks = array.shape[1] // 3 // width
    destinations = head_owners * pair

    def source(part):
        def place(d, info):
            return (info[0], part * blocks + (d % head_owners) * pair + d // head_owners)

        return pl.BlockSpec((rows, width), place)

    return pl.pallas_call(
        pack_body,
        grid_spec=pltpu.PrefetchScalarGridSpec(
            num_scalar_prefetch=1,
            grid=(destinations,),
            in_specs=[source(0), source(1), source(2)]
            + [pl.BlockSpec(memory_space=pl.ANY)] * len(after),
            out_specs=pl.BlockSpec((1, rows, 3 * width), lambda d, info: (d, 0, 0)),
        ),
        out_shape=jax.ShapeDtypeStruct((destinations, rows, 3 * width), array.dtype),
        compiler_params=params(),
        cost_estimate=pl.CostEstimate(
            flops=0, bytes_accessed=weight * 12 * destinations * rows * width, transcendentals=0
        ),
        name="pack_heads",
    )(first_block, array, array, array, *after)


def dot(first, second, contract):
    return lax.dot_general(
        first, second, ((contract[:1], contract[1:]), ((), ())), preferred_element_type=jnp.float32
    )


def with_ones(block):
    return jnp.concatenate([block, jnp.ones_like(block)], axis=1)


def reference_columns(row_max):
    reference = row_max.astype(jnp.bfloat16).astype(jnp.float32)
    return jnp.broadcast_to(reference * (-1.0 / HD), (row_max.shape[0], HD)).astype(jnp.bfloat16)


def weighted(queries, key_rows, values):
    weights = jnp.exp2(dot(queries, key_rows, (1, 1)) * SCALE).astype(jnp.bfloat16)
    return dot(weights, values, (1, 0))


def tiles_of(rows, most):
    tile = min(most, rows)
    return [slice(first, min(first + tile, rows)) for first in range(0, rows, tile)]


def until_small(flag, total, attempt):
    flag[0] = 1

    @pl.loop(0, 2)
    def _(turn):
        @pl.when(flag[0] == 1)
        def _():
            attempt(turn)
            flag[0] = jnp.where(jnp.max(total[:, :, HD:]) > LARGE, 1, 0).astype(jnp.int32)


class Fetch:
    def __init__(self, info, width, sems):
        self.columns = pl.ds(pl.multiple_of(info[0] * width, width), width)
        self.info, self.sems, self.waits = info, sems, []

    def start(self, candidates, flags, target, at):
        rows = candidates[0].shape[1]
        sem = self.sems.at[len(self.waits)]
        copies = [
            pltpu.make_async_copy(
                block.at[:, :, self.columns], target.at[:, pl.ds(at, rows), :], sem
            )
            for block in candidates
        ]
        if len(copies) == 1:
            copies[0].start()
        else:
            for copy, flag in zip(copies, flags):
                pl.when(flag)(copy.start)
        self.waits.append(copies[0])

    def wait(self):
        for copy in self.waits:
            copy.wait()


def settle(fetch, refs, entries, chosen):
    for index, candidates in enumerate(entries):
        sides = []
        for count in candidates:
            sides.append(refs[:count])
            refs = refs[count:]
        first = fetch.info[1 + index]
        at = 0
        for blocks in zip(*sides):
            fetch.start(blocks, [first == 1, first == 0], chosen.at[index], at)
            at += blocks[0].shape[1]


def accumulate(flag, total, aug, heads, queries_of, first_keys_of, own, chosen, ready):
    def columns(head):
        return slice(head * HD, (head + 1) * HD)

    def pieces(head, some):
        return some(head) + [
            (chosen[index, 0, :, columns(head)], chosen[index, 1, :, columns(head)])
            for index in range(chosen.shape[0])
        ]

    def tiles():
        for head in range(heads):
            queries = queries_of(head)
            for span, some in own:
                for tile in tiles_of(span.stop - span.start, TILE):
                    tile = slice(span.start + tile.start, span.start + tile.stop)
                    yield head, tile, queries[tile, :], some

    def largest(queries, key_rows):
        return jnp.max(dot(queries, key_rows, (1, 1)), axis=1, keepdims=True)

    def attempt(turn):
        @pl.when(turn == 0)
        def _():
            for head, tile, queries, _ in tiles():
                aug[head, tile, :] = reference_columns(largest(queries, first_keys_of(head)))
            ready()

        @pl.when(turn == 1)
        def _():
            for head, tile, queries, some in tiles():
                row_max = None
                for key_rows, _ in pieces(head, some):
                    piece_max = largest(queries, key_rows)
                    row_max = piece_max if row_max is None else jnp.maximum(row_max, piece_max)
                aug[head, tile, :] = reference_columns(row_max)

        for head, tile, queries, some in tiles():
            both = jnp.concatenate([queries, aug[head, tile, :]], axis=1)
            summed = None
            for key_rows, values in pieces(head, some):
                part = weighted(both, with_ones(key_rows), with_ones(values))
                summed = part if summed is None else summed + part
            total[head, tile, :] = summed

    until_small(flag, total, attempt)


def finish(out, total):
    for head in range(total.shape[0]):
        attended = (total[head, :, :HD] / total[head, :, HD:]).astype(out.dtype)
        out[:, :, head * HD : (head + 1) * HD] = attended.reshape(out.shape[:2] + (HD,))


def part_of(ref, part, head, width):
    first = part * width + head * HD
    return ref[:, :, first : first + HD].reshape(-1, HD)


def text_body(pair, entries, info, txt, *refs, wanted):
    stale, came = refs[:pair], refs[pair:-10]
    result, held_txt, out, chosen, beside, aug, total, flag, sems, plain = refs[-10:]
    width = chosen.shape[3]
    heads = width // HD

    @pl.when(info[wanted] == 1)
    def _():
        fetch = Fetch(info, width, sems)
        whole = pltpu.make_async_copy(txt, held_txt, plain.at[0])
        whole.start()
        at = 0
        for block in stale:
            fetch.start([block], [], beside.at[0], at)
            at += block.shape[1]
        settle(fetch, came, entries, chosen)
        whole.wait()

        def own(head):
            columns = slice(head * HD, (head + 1) * HD)
            return [
                (part_of(held_txt, 1, head, width), part_of(held_txt, 2, head, width)),
                (beside[0, 0, :, columns], beside[0, 1, :, columns]),
            ]

        accumulate(
            flag, total, aug, heads,
            lambda head: part_of(held_txt, 0, head, width),
            lambda head: part_of(held_txt, 1, head, width)[: min(FIRST_KEYS, total.shape[1]), :],
            [(slice(0, total.shape[1]), own)], chosen, fetch.wait,
        )
        finish(out, total)
        back = pltpu.make_async_copy(out, result, plain.at[0])
        back.start()
        back.wait()


def image_body(pair, entries, info, img, txt, *refs):
    stale, came = refs[:pair], refs[pair:-12]
    (result, held_img, held_txt, out, chosen, beside, aug, total, flag, sems, plain) = refs[-11:]
    width = chosen.shape[3]
    heads = width // HD
    rows = total.shape[1]
    group_rows, sources = rows // pair, img.shape[0] // pair
    fetch = Fetch(info, width, sems)
    wholes = [
        pltpu.make_async_copy(source, target, plain.at[index])
        for index, (source, target) in enumerate(((txt, held_txt), (img, held_img)))
    ]
    for whole in wholes:
        whole.start()
    if pair == 2:
        for group in range(pair):
            flags = [info[0] != group, info[0] == group]
            fetch.start(stale, flags, beside.at[group], group_rows)
    settle(fetch, came, entries, chosen)
    for whole in wholes:
        whole.wait()
    for group in range(pair):
        for part in range(2):
            fresh = held_img[
                group * sources : (group + 1) * sources, :, (1 + part) * width : (2 + part) * width
            ]
            beside[group, part, :group_rows, :] = fresh.reshape(group_rows, width)

    def own(group):
        def some(head):
            columns = slice(head * HD, (head + 1) * HD)
            return [
                (part_of(held_txt, 1, head, width), part_of(held_txt, 2, head, width)),
                (beside[group, 0, :, columns], beside[group, 1, :, columns]),
            ]

        return (slice(group * group_rows, (group + 1) * group_rows), some)

    text_keys = txt.shape[0] * txt.shape[1]
    accumulate(
        flag, total, aug, heads,
        lambda head: part_of(held_img, 0, head, width),
        lambda head: part_of(held_txt, 1, head, width)[: min(FIRST_KEYS, text_keys), :],
        [own(group) for group in range(pair)], chosen, fetch.wait,
    )
    finish(out, total)
    back = pltpu.make_async_copy(out, result, plain.at[0])
    back.start()
    back.wait()


def attend(name, body, info, fresh, stale, entries, groups, earlier=()):
    first = fresh[0]
    width = first.shape[2] // 3
    heads, rows = width // HD, first.shape[0] * first.shape[1]
    keys = sum(block.shape[1] for block in stale)
    came = [b for candidates in entries for blocks in candidates for b in blocks]
    counts = [[len(blocks) for blocks in candidates] for candidates in entries]
    anywhere = pl.BlockSpec(memory_space=pl.ANY)
    result = jax.ShapeDtypeStruct(first.shape[:2] + (width,), first.dtype)
    scratch = [(array.shape, array.dtype) for array in fresh] + [
        (result.shape, result.dtype),
        ((len(entries), 2, keys, width), first.dtype),
        ((groups, 2, keys, width), first.dtype),
        ((heads, rows, HD), jnp.bfloat16),
        ((heads, rows, 2 * HD), jnp.float32),
    ]
    operands = [*fresh, *stale, *came, *earlier]
    return pl.pallas_call(
        functools.partial(body, len(stale), counts),
        in_specs=[pl.BlockSpec(memory_space=pltpu.SMEM)] + [anywhere] * len(operands),
        out_specs=anywhere,
        out_shape=result,
        scratch_shapes=[pltpu.VMEM(*one) for one in scratch]
        + [
            pltpu.SMEM((1,), jnp.int32),
            pltpu.SemaphoreType.DMA((len(stale) * (1 + len(entries)),)),
            pltpu.SemaphoreType.DMA((2,)),
        ],
        compiler_params=pltpu.CompilerParams(vmem_limit_bytes=ATTEND_LIMIT),
        cost_estimate=pl.CostEstimate(
            flops=4 * rows * keys * (2 + len(entries)) * width,
            bytes_accessed=4 * keys * (2 + len(entries)) * width,
            transcendentals=rows * keys * (2 + len(entries)) * heads,
        ),
        name=name,
    )(info, *operands)


def project_body(order, x_ref, weight, residual, gate, out, held, total, sems):
    copies = [
        pltpu.make_async_copy(weight.at[place], held.at[place], sems.at[place])
        for place in order
    ]
    for copy in copies:
        copy.start()
    for source, (place, copy) in enumerate(zip(order, copies)):
        copy.wait()
        part = jnp.dot(x_ref[source], held[place], preferred_element_type=jnp.float32)
        if source == 0:
            total[...] = part
        else:
            total[...] += part
    out[...] = (residual[...].astype(jnp.float32) + gate[...] * total[...]).astype(out.dtype)


def project(x, order, weight, residual, gate):
    rows, model = residual.shape
    destinations, _, width = x.shape
    vmem = pl.BlockSpec(memory_space=pltpu.VMEM)
    return pl.pallas_call(
        functools.partial(project_body, order),
        in_specs=[vmem, pl.BlockSpec(memory_space=pl.ANY), vmem, vmem],
        out_specs=vmem,
        out_shape=jax.ShapeDtypeStruct((rows, model), residual.dtype),
        scratch_shapes=[
            pltpu.VMEM((destinations, width, model), weight.dtype),
            pltpu.VMEM((rows, model), jnp.float32),
            pltpu.SemaphoreType.DMA((destinations,)),
        ],
        compiler_params=pltpu.CompilerParams(vmem_limit_bytes=WIDE_LIMIT),
        cost_estimate=pl.CostEstimate(
            flops=2 * rows * model * model, bytes_accessed=2 * model * model, transcendentals=0
        ),
        name="project",
    )(x, weight.reshape(destinations, width, model), residual, gate.reshape(1, model))


def unpack_body(order, x_ref, earlier, out):
    del earlier
    width = x_ref.shape[2]
    for source, place in enumerate(order):
        out[:, place * width : (place + 1) * width] = x_ref[source]


def unpack(x, order, earlier):
    rows, model = x.shape[1], x.shape[0] * x.shape[2]
    vmem = pl.BlockSpec(memory_space=pltpu.VMEM)
    return pl.pallas_call(
        functools.partial(unpack_body, order),
        in_specs=[vmem, pl.BlockSpec(memory_space=pl.ANY)],
        out_specs=vmem,
        out_shape=jax.ShapeDtypeStruct((rows, model), x.dtype),
        name="unpack_text",
    )(x, earlier)


def after_body(*refs):
    del refs


def after(x, other):
    anywhere = pl.BlockSpec(memory_space=pl.ANY)
    return pl.pallas_call(
        after_body,
        in_specs=[anywhere, anywhere],
        out_specs=anywhere,
        out_shape=jax.ShapeDtypeStruct(x.shape, x.dtype),
        input_output_aliases={0: 0},
        name="after",
    )(x, other)


def flag_body(flag, earlier, out):
    del earlier
    out[0] = flag[0]


def flag_after(flag, earlier):
    smem = pl.BlockSpec(memory_space=pltpu.SMEM)
    return pl.pallas_call(
        flag_body,
        in_specs=[smem, pl.BlockSpec(memory_space=pl.ANY)],
        out_specs=smem,
        out_shape=jax.ShapeDtypeStruct(flag.shape, flag.dtype),
        name="flag_after",
    )(flag, earlier)


def per_device(img_qkv, txt_qkv, stale_kv, residual, gate_scale, proj_weight):
    patches, head_owners = lax.axis_size("patch"), lax.axis_size("head")
    patch = lax.axis_index("patch")
    owned_heads = stale_kv.shape[2] // HD
    pair = 2 if patches % 2 == 0 and owned_heads % 2 == 0 else 1
    planes = patches // pair
    plane, core = patch // pair, patch % pair
    width = stale_kv.shape[2] // pair
    heads = width // HD
    img_rows, model = residual.shape
    text_rows = txt_qkv.shape[0] // pair
    destinations = pair * head_owners

    order = [(d % head_owners) * pair + d // head_owners for d in range(destinations)]
    groups = [[g * destinations + d for d in range(destinations)] for g in range(planes)]
    swap_pairs = [(p, p + 1 - 2 * (p % 2)) for p in range(patches)]

    def exchange(x):
        return lax.all_to_all(
            x, ("patch", "head"), split_axis=0, concat_axis=0, axis_index_groups=groups, tiled=True
        )

    def swap(x):
        return lax.ppermute(x, "patch", swap_pairs)

    def up_pairs(step):
        return [(z, z + 1) for z in range(step - 1, planes - 1)]

    def down_pairs(step):
        return [(z + 1, z) for z in range(0, planes - step)]

    core_only = core.astype(jnp.int32).reshape(1)
    txt = exchange(pack(core_only, txt_qkv, text_rows, head_owners, pair, width))

    along, against = [], []
    if pair == 2:
        stale = [stale_kv, swap(stale_kv)]
        held = [stale_kv, stale_kv]
        for step in range(1, planes):
            pairs = [
                [(2 * a + turn, 2 * b) for a, b in up_pairs(step)]
                + [(2 * a + 1 - turn, 2 * b + 1) for a, b in down_pairs(step)]
                for turn in ((0, 1) if step == 1 else (0, 0))
            ]
            held = [lax.ppermute(block, "patch", way) for block, way in zip(held, pairs)]
            if step == 1:
                held = [held[0], after(held[1], txt)]
            along.append(held)
            against.append([swap(block) for block in held])
        ahead = jnp.where(core == 0, plane, planes - 1 - plane)
    else:
        stale = [stale_kv]
        from_below = from_above = stale_kv
        for step in range(1, planes):
            from_below = lax.ppermute(from_below, "patch", up_pairs(step))
            from_above = lax.ppermute(from_above, "patch", down_pairs(step))
            along.append([from_below])
            against.append([from_above])
        ahead = plane
    entries = [[along[i - 1], against[planes - i - 1]] for i in range(1, planes)]
    first_holds = [ahead >= i for i in range(1, planes)]
    zero_only = jnp.zeros((1,), jnp.int32)
    img = exchange(
        pack(zero_only, img_qkv, img_rows, head_owners, pair, width, [txt])
    )

    early = planes > 2
    inner = (plane > 0) & (plane < planes - 1)
    info = jnp.stack([core] + first_holds + [inner if early else core >= 0]).astype(jnp.int32)
    known = entries
    if early:
        known = [[along[0]]] + entries[1:-1] + [[against[0]]]
    text_attn = attend(
        "attend_text", functools.partial(text_body, wanted=planes), info, [txt], stale, known, 1
    )
    image_attn = attend(
        "attend_image", image_body, info, [img, txt], stale, entries, pair, [text_attn]
    )
    text_out = unpack(exchange(text_attn), order, image_attn)
    image_out = project(exchange(image_attn), order, proj_weight, residual, gate_scale)
    if early:
        ends = [(1, 0), (planes - 2, planes - 1)]
        ends = [(a * pair + c, b * pair + c) for a, b in ends for c in range(pair)]
        hopped = lax.ppermute(text_out, "patch", ends)
        keep = flag_after(inner.astype(jnp.int32).reshape(1), image_out)
        text_out = jnp.where(keep[0] == 1, text_out, hopped)
    if pair == 2:
        other = swap(text_out)
        lower = core == 0
        text_out = jnp.concatenate(
            [jnp.where(lower, text_out, other), jnp.where(lower, other, text_out)], 0
        )
    return (image_out, text_out)


def solution(mesh):
    return jax.shard_map(
        per_device,
        mesh=mesh,
        in_specs=(
            P(("patch", "head"), None),
            P("head", None),
            P(None, "patch", "head"),
            P(("patch", "head"), None),
            P(),
            P(),
        ),
        out_specs=(P(("patch", "head"), None), P("head", None)),
        check_vma=False,
    )
```

```python
import functools
import math

import jax
import jax.numpy as jnp
from jax import lax
from jax.experimental import pallas as pl
from jax.experimental.pallas import tpu as pltpu
from jax.sharding import PartitionSpec as P

HD = 128
SCALE = math.log2(math.e) / math.sqrt(HD)
VMEM_LIMIT = 12 * 1024 * 1024
ATTEND_LIMIT = 24 * 1024 * 1024
WIDE_LIMIT = 48 * 1024 * 1024
TILE = 256
FIRST_KEYS = 256
LARGE = 2.0**60


def params(block_elements=0):
    return pltpu.CompilerParams(
        vmem_limit_bytes=VMEM_LIMIT + 4 * block_elements, dimension_semantics=("arbitrary",)
    )


def pack_body(_, *refs):
    sources, packed = refs[:3], refs[-1]
    width = sources[0].shape[1]
    for part, source in enumerate(sources):
        packed[0, :, part * width : (part + 1) * width] = source[...]


def pack(first_block, array, rows, head_owners, pair, width, after=(), weight=1):
    blocks = array.shape[1] // 3 // width
    destinations = head_owners * pair

    def source(part):
        def place(d, info):
            return (info[0], part * blocks + (d % head_owners) * pair + d // head_owners)

        return pl.BlockSpec((rows, width), place)

    return pl.pallas_call(
        pack_body,
        grid_spec=pltpu.PrefetchScalarGridSpec(
            num_scalar_prefetch=1,
            grid=(destinations,),
            in_specs=[source(0), source(1), source(2)]
            + [pl.BlockSpec(memory_space=pl.ANY)] * len(after),
            out_specs=pl.BlockSpec((1, rows, 3 * width), lambda d, info: (d, 0, 0)),
        ),
        out_shape=jax.ShapeDtypeStruct((destinations, rows, 3 * width), array.dtype),
        compiler_params=params(),
        cost_estimate=pl.CostEstimate(
            flops=0, bytes_accessed=weight * 12 * destinations * rows * width, transcendentals=0
        ),
        name="pack_heads",
    )(first_block, array, array, array, *after)


def dot(first, second, contract):
    return lax.dot_general(
        first, second, ((contract[:1], contract[1:]), ((), ())), preferred_element_type=jnp.float32
    )


def with_ones(block):
    return jnp.concatenate([block, jnp.ones_like(block)], axis=1)


def reference_columns(row_max):
    reference = row_max.astype(jnp.bfloat16).astype(jnp.float32)
    return jnp.broadcast_to(reference * (-1.0 / HD), (row_max.shape[0], HD)).astype(jnp.bfloat16)


def weighted(queries, key_rows, values):
    weights = jnp.exp2(dot(queries, key_rows, (1, 1)) * SCALE).astype(jnp.bfloat16)
    return dot(weights, values, (1, 0))


def tiles_of(rows, most):
    tile = min(most, rows)
    return [slice(first, min(first + tile, rows)) for first in range(0, rows, tile)]


def until_small(flag, total, attempt):
    flag[0] = 1

    @pl.loop(0, 2)
    def _(turn):
        @pl.when(flag[0] == 1)
        def _():
            attempt(turn)
            flag[0] = jnp.where(jnp.max(total[:, :, HD:]) > LARGE, 1, 0).astype(jnp.int32)


class Fetch:
    def __init__(self, info, width, sems):
        self.columns = pl.ds(pl.multiple_of(info[0] * width, width), width)
        self.info, self.sems, self.waits = info, sems, []

    def start(self, candidates, flags, target, at):
        rows = candidates[0].shape[1]
        sem = self.sems.at[len(self.waits)]
        copies = [
            pltpu.make_async_copy(
                block.at[:, :, self.columns], target.at[:, pl.ds(at, rows), :], sem
            )
            for block in candidates
        ]
        if len(copies) == 1:
            copies[0].start()
        else:
            for copy, flag in zip(copies, flags):
                pl.when(flag)(copy.start)
        self.waits.append(copies[0])

    def wait(self):
        for copy in self.waits:
            copy.wait()


def settle(fetch, refs, entries, chosen):
    for index, candidates in enumerate(entries):
        sides = []
        for count in candidates:
            sides.append(refs[:count])
            refs = refs[count:]
        first = fetch.info[1 + index]
        at = 0
        for blocks in zip(*sides):
            fetch.start(blocks, [first == 1, first == 0], chosen.at[index], at)
            at += blocks[0].shape[1]


def accumulate(flag, total, aug, heads, queries_of, first_keys_of, own, chosen, ready):
    def columns(head):
        return slice(head * HD, (head + 1) * HD)

    def pieces(head, some):
        return some(head) + [
            (chosen[index, 0, :, columns(head)], chosen[index, 1, :, columns(head)])
            for index in range(chosen.shape[0])
        ]

    def tiles():
        for head in range(heads):
            queries = queries_of(head)
            for span, some in own:
                for tile in tiles_of(span.stop - span.start, TILE):
                    tile = slice(span.start + tile.start, span.start + tile.stop)
                    yield head, tile, queries[tile, :], some

    def largest(queries, key_rows):
        return jnp.max(dot(queries, key_rows, (1, 1)), axis=1, keepdims=True)

    def attempt(turn):
        @pl.when(turn == 0)
        def _():
            for head, tile, queries, _ in tiles():
                aug[head, tile, :] = reference_columns(largest(queries, first_keys_of(head)))
            ready()

        @pl.when(turn == 1)
        def _():
            for head, tile, queries, some in tiles():
                row_max = None
                for key_rows, _ in pieces(head, some):
                    piece_max = largest(queries, key_rows)
                    row_max = piece_max if row_max is None else jnp.maximum(row_max, piece_max)
                aug[head, tile, :] = reference_columns(row_max)

        for head, tile, queries, some in tiles():
            both = jnp.concatenate([queries, aug[head, tile, :]], axis=1)
            summed = None
            for key_rows, values in pieces(head, some):
                part = weighted(both, with_ones(key_rows), with_ones(values))
                summed = part if summed is None else summed + part
            total[head, tile, :] = summed

    until_small(flag, total, attempt)


def finish(out, total):
    for head in range(total.shape[0]):
        attended = (total[head, :, :HD] / total[head, :, HD:]).astype(out.dtype)
        out[:, :, head * HD : (head + 1) * HD] = attended.reshape(out.shape[:2] + (HD,))


def part_of(ref, part, head, width):
    first = part * width + head * HD
    return ref[:, :, first : first + HD].reshape(-1, HD)


def text_body(pair, entries, info, txt, *refs, wanted):
    stale, came = refs[:pair], refs[pair:-10]
    result, held_txt, out, chosen, beside, aug, total, flag, sems, plain = refs[-10:]
    width = chosen.shape[3]
    heads = width // HD

    @pl.when(info[wanted] == 1)
    def _():
        fetch = Fetch(info, width, sems)
        whole = pltpu.make_async_copy(txt, held_txt, plain.at[0])
        whole.start()
        at = 0
        for block in stale:
            fetch.start([block], [], beside.at[0], at)
            at += block.shape[1]
        settle(fetch, came, entries, chosen)
        whole.wait()

        def own(head):
            columns = slice(head * HD, (head + 1) * HD)
            return [
                (part_of(held_txt, 1, head, width), part_of(held_txt, 2, head, width)),
                (beside[0, 0, :, columns], beside[0, 1, :, columns]),
            ]

        accumulate(
            flag, total, aug, heads,
            lambda head: part_of(held_txt, 0, head, width),
            lambda head: part_of(held_txt, 1, head, width)[: min(FIRST_KEYS, total.shape[1]), :],
            [(slice(0, total.shape[1]), own)], chosen, fetch.wait,
        )
        finish(out, total)
        back = pltpu.make_async_copy(out, result, plain.at[0])
        back.start()
        back.wait()


def image_body(pair, entries, info, img, txt, *refs):
    stale, came = refs[:pair], refs[pair:-12]
    (result, held_img, held_txt, out, chosen, beside, aug, total, flag, sems, plain) = refs[-11:]
    width = chosen.shape[3]
    heads = width // HD
    rows = total.shape[1]
    group_rows, sources = rows // pair, img.shape[0] // pair
    fetch = Fetch(info, width, sems)
    wholes = [
        pltpu.make_async_copy(source, target, plain.at[index])
        for index, (source, target) in enumerate(((txt, held_txt), (img, held_img)))
    ]
    for whole in wholes:
        whole.start()
    if pair == 2:
        for group in range(pair):
            flags = [info[0] != group, info[0] == group]
            fetch.start(stale, flags, beside.at[group], group_rows)
    settle(fetch, came, entries, chosen)
    for whole in wholes:
        whole.wait()
    for group in range(pair):
        for part in range(2):
            fresh = held_img[
                group * sources : (group + 1) * sources, :, (1 + part) * width : (2 + part) * width
            ]
            beside[group, part, :group_rows, :] = fresh.reshape(group_rows, width)

    def own(group):
        def some(head):
            columns = slice(head * HD, (head + 1) * HD)
            return [
                (part_of(held_txt, 1, head, width), part_of(held_txt, 2, head, width)),
                (beside[group, 0, :, columns], beside[group, 1, :, columns]),
            ]

        return (slice(group * group_rows, (group + 1) * group_rows), some)

    text_keys = txt.shape[0] * txt.shape[1]
    accumulate(
        flag, total, aug, heads,
        lambda head: part_of(held_img, 0, head, width),
        lambda head: part_of(held_txt, 1, head, width)[: min(FIRST_KEYS, text_keys), :],
        [own(group) for group in range(pair)], chosen, fetch.wait,
    )
    finish(out, total)
    back = pltpu.make_async_copy(out, result, plain.at[0])
    back.start()
    back.wait()


def attend(name, body, info, fresh, stale, entries, groups, earlier=(), weight=1):
    first = fresh[0]
    width = first.shape[2] // 3
    heads, rows = width // HD, first.shape[0] * first.shape[1]
    keys = sum(block.shape[1] for block in stale)
    came = [b for candidates in entries for blocks in candidates for b in blocks]
    counts = [[len(blocks) for blocks in candidates] for candidates in entries]
    anywhere = pl.BlockSpec(memory_space=pl.ANY)
    result = jax.ShapeDtypeStruct(first.shape[:2] + (width,), first.dtype)
    scratch = [(array.shape, array.dtype) for array in fresh] + [
        (result.shape, result.dtype),
        ((len(entries), 2, keys, width), first.dtype),
        ((groups, 2, keys, width), first.dtype),
        ((heads, rows, HD), jnp.bfloat16),
        ((heads, rows, 2 * HD), jnp.float32),
    ]
    operands = [*fresh, *stale, *came, *earlier]
    return pl.pallas_call(
        functools.partial(body, len(stale), counts),
        in_specs=[pl.BlockSpec(memory_space=pltpu.SMEM)] + [anywhere] * len(operands),
        out_specs=anywhere,
        out_shape=result,
        scratch_shapes=[pltpu.VMEM(*one) for one in scratch]
        + [
            pltpu.SMEM((1,), jnp.int32),
            pltpu.SemaphoreType.DMA((len(stale) * (1 + len(entries)),)),
            pltpu.SemaphoreType.DMA((2,)),
        ],
        compiler_params=pltpu.CompilerParams(vmem_limit_bytes=ATTEND_LIMIT),
        cost_estimate=pl.CostEstimate(
            flops=weight * 4 * rows * keys * (2 + len(entries)) * width,
            bytes_accessed=weight * 4 * keys * (2 + len(entries)) * width,
            transcendentals=rows * keys * (2 + len(entries)) * heads,
        ),
        name=name,
    )(info, *operands)


def project_body(order, x_ref, weight, residual, gate, out, held, total, sems):
    copies = [
        pltpu.make_async_copy(weight.at[place], held.at[place], sems.at[place])
        for place in order
    ]
    for copy in copies:
        copy.start()
    for source, (place, copy) in enumerate(zip(order, copies)):
        copy.wait()
        part = jnp.dot(x_ref[source], held[place], preferred_element_type=jnp.float32)
        if source == 0:
            total[...] = part
        else:
            total[...] += part
    out[...] = (residual[...].astype(jnp.float32) + gate[...] * total[...]).astype(out.dtype)


def project(x, order, weight, residual, gate):
    rows, model = residual.shape
    destinations, _, width = x.shape
    vmem = pl.BlockSpec(memory_space=pltpu.VMEM)
    return pl.pallas_call(
        functools.partial(project_body, order),
        in_specs=[vmem, pl.BlockSpec(memory_space=pl.ANY), vmem, vmem],
        out_specs=vmem,
        out_shape=jax.ShapeDtypeStruct((rows, model), residual.dtype),
        scratch_shapes=[
            pltpu.VMEM((destinations, width, model), weight.dtype),
            pltpu.VMEM((rows, model), jnp.float32),
            pltpu.SemaphoreType.DMA((destinations,)),
        ],
        compiler_params=pltpu.CompilerParams(vmem_limit_bytes=WIDE_LIMIT),
        cost_estimate=pl.CostEstimate(
            flops=2 * rows * model * model, bytes_accessed=2 * model * model, transcendentals=0
        ),
        name="project",
    )(x, weight.reshape(destinations, width, model), residual, gate.reshape(1, model))


def unpack_body(order, x_ref, earlier, out):
    del earlier
    width = x_ref.shape[2]
    for source, place in enumerate(order):
        out[:, place * width : (place + 1) * width] = x_ref[source]


def unpack(x, order, earlier):
    rows, model = x.shape[1], x.shape[0] * x.shape[2]
    vmem = pl.BlockSpec(memory_space=pltpu.VMEM)
    return pl.pallas_call(
        functools.partial(unpack_body, order),
        in_specs=[vmem, pl.BlockSpec(memory_space=pl.ANY)],
        out_specs=vmem,
        out_shape=jax.ShapeDtypeStruct((rows, model), x.dtype),
        name="unpack_text",
    )(x, earlier)


def after_body(*refs):
    del refs


def after(x, other):
    anywhere = pl.BlockSpec(memory_space=pl.ANY)
    return pl.pallas_call(
        after_body,
        in_specs=[anywhere, anywhere],
        out_specs=anywhere,
        out_shape=jax.ShapeDtypeStruct(x.shape, x.dtype),
        input_output_aliases={0: 0},
        name="after",
    )(x, other)


def flag_body(flag, earlier, out):
    del earlier
    out[0] = flag[0]


def flag_after(flag, earlier):
    smem = pl.BlockSpec(memory_space=pltpu.SMEM)
    return pl.pallas_call(
        flag_body,
        in_specs=[smem, pl.BlockSpec(memory_space=pl.ANY)],
        out_specs=smem,
        out_shape=jax.ShapeDtypeStruct(flag.shape, flag.dtype),
        name="flag_after",
    )(flag, earlier)


def per_device(img_qkv, txt_qkv, stale_kv, residual, gate_scale, proj_weight):
    patches, head_owners = lax.axis_size("patch"), lax.axis_size("head")
    patch = lax.axis_index("patch")
    owned_heads = stale_kv.shape[2] // HD
    pair = 2 if patches % 2 == 0 and owned_heads % 2 == 0 else 1
    planes = patches // pair
    plane, core = patch // pair, patch % pair
    width = stale_kv.shape[2] // pair
    heads = width // HD
    img_rows, model = residual.shape
    text_rows = txt_qkv.shape[0] // pair
    destinations = pair * head_owners

    order = [(d % head_owners) * pair + d // head_owners for d in range(destinations)]
    groups = [[g * destinations + d for d in range(destinations)] for g in range(planes)]
    swap_pairs = [(p, p + 1 - 2 * (p % 2)) for p in range(patches)]

    def exchange(x):
        return lax.all_to_all(
            x, ("patch", "head"), split_axis=0, concat_axis=0, axis_index_groups=groups, tiled=True
        )

    def swap(x):
        return lax.ppermute(x, "patch", swap_pairs)

    def up_pairs(step):
        return [(z, z + 1) for z in range(step - 1, planes - 1)]

    def down_pairs(step):
        return [(z + 1, z) for z in range(0, planes - step)]

    core_only = core.astype(jnp.int32).reshape(1)
    txt = exchange(pack(core_only, txt_qkv, text_rows, head_owners, pair, width))

    along, against = [], []
    if pair == 2:
        stale = [stale_kv, swap(stale_kv)]
        held = [stale_kv, stale_kv]
        for step in range(1, planes):
            pairs = [
                [(2 * a + turn, 2 * b) for a, b in up_pairs(step)]
                + [(2 * a + 1 - turn, 2 * b + 1) for a, b in down_pairs(step)]
                for turn in ((0, 1) if step == 1 else (0, 0))
            ]
            held = [lax.ppermute(block, "patch", way) for block, way in zip(held, pairs)]
            if step == 1:
                held = [held[0], after(held[1], txt)]
            along.append(held)
            against.append([swap(block) for block in held])
        ahead = jnp.where(core == 0, plane, planes - 1 - plane)
    else:
        stale = [stale_kv]
        from_below = from_above = stale_kv
        for step in range(1, planes):
            from_below = lax.ppermute(from_below, "patch", up_pairs(step))
            from_above = lax.ppermute(from_above, "patch", down_pairs(step))
            along.append([from_below])
            against.append([from_above])
        ahead = plane
    entries = [[along[i - 1], against[planes - i - 1]] for i in range(1, planes)]
    first_holds = [ahead >= i for i in range(1, planes)]
    zero_only = jnp.zeros((1,), jnp.int32)
    img = exchange(
        pack(zero_only, img_qkv, img_rows, head_owners, pair, width, [txt])
    )

    early = planes > 2
    inner = (plane > 0) & (plane < planes - 1)
    info = jnp.stack([core] + first_holds + [inner if early else core >= 0]).astype(jnp.int32)
    known = entries
    if early:
        known = [[along[0]]] + entries[1:-1] + [[against[0]]]
    text_attn = attend(
        "attend_text", functools.partial(text_body, wanted=planes), info, [txt], stale, known, 1,
        [img], 16,
    )
    image_attn = attend(
        "attend_image", image_body, info, [img, txt], stale, entries, pair, [text_attn]
    )
    text_out = unpack(exchange(text_attn), order, image_attn)
    image_out = project(exchange(image_attn), order, proj_weight, residual, gate_scale)
    if early:
        ends = [(1, 0), (planes - 2, planes - 1)]
        ends = [(a * pair + c, b * pair + c) for a, b in ends for c in range(pair)]
        hopped = lax.ppermute(text_out, "patch", ends)
        keep = flag_after(inner.astype(jnp.int32).reshape(1), image_out)
        text_out = jnp.where(keep[0] == 1, text_out, hopped)
    if pair == 2:
        other = swap(text_out)
        lower = core == 0
        text_out = jnp.concatenate(
            [jnp.where(lower, text_out, other), jnp.where(lower, other, text_out)], 0
        )
    return (image_out, text_out)


def solution(mesh):
    return jax.shard_map(
        per_device,
        mesh=mesh,
        in_specs=(
            P(("patch", "head"), None),
            P("head", None),
            P(None, "patch", "head"),
            P(("patch", "head"), None),
            P(),
            P(),
        ),
        out_specs=(P(("patch", "head"), None), P("head", None)),
        check_vma=False,
    )
```

```python
import functools
import math

import jax
import jax.numpy as jnp
from jax import lax
from jax.experimental import pallas as pl
from jax.experimental.pallas import tpu as pltpu
from jax.sharding import PartitionSpec as P

HD = 128
SCALE = math.log2(math.e) / math.sqrt(HD)
VMEM_LIMIT = 12 * 1024 * 1024
ATTEND_LIMIT = 24 * 1024 * 1024
WIDE_LIMIT = 48 * 1024 * 1024
TILE = 256
FIRST_KEYS = 256
LARGE = 2.0**60


def params(block_elements=0):
    return pltpu.CompilerParams(
        vmem_limit_bytes=VMEM_LIMIT + 4 * block_elements, dimension_semantics=("arbitrary",)
    )


def pack_body(_, *refs):
    sources, packed = refs[:3], refs[-1]
    width = sources[0].shape[1]
    for part, source in enumerate(sources):
        packed[0, :, part * width : (part + 1) * width] = source[...]


def pack(first_block, array, rows, head_owners, pair, width, after=(), weight=1):
    blocks = array.shape[1] // 3 // width
    destinations = head_owners * pair

    def source(part):
        def place(d, info):
            return (info[0], part * blocks + (d % head_owners) * pair + d // head_owners)

        return pl.BlockSpec((rows, width), place)

    return pl.pallas_call(
        pack_body,
        grid_spec=pltpu.PrefetchScalarGridSpec(
            num_scalar_prefetch=1,
            grid=(destinations,),
            in_specs=[source(0), source(1), source(2)]
            + [pl.BlockSpec(memory_space=pl.ANY)] * len(after),
            out_specs=pl.BlockSpec((1, rows, 3 * width), lambda d, info: (d, 0, 0)),
        ),
        out_shape=jax.ShapeDtypeStruct((destinations, rows, 3 * width), array.dtype),
        compiler_params=params(),
        cost_estimate=pl.CostEstimate(
            flops=0, bytes_accessed=weight * 12 * destinations * rows * width, transcendentals=0
        ),
        name="pack_heads",
    )(first_block, array, array, array, *after)


def dot(first, second, contract):
    return lax.dot_general(
        first, second, ((contract[:1], contract[1:]), ((), ())), preferred_element_type=jnp.float32
    )


def with_ones(block):
    return jnp.concatenate([block, jnp.ones_like(block)], axis=1)


def reference_columns(row_max):
    reference = row_max.astype(jnp.bfloat16).astype(jnp.float32)
    return jnp.broadcast_to(reference * (-1.0 / HD), (row_max.shape[0], HD)).astype(jnp.bfloat16)


def weighted(queries, key_rows, values):
    weights = jnp.exp2(dot(queries, key_rows, (1, 1)) * SCALE).astype(jnp.bfloat16)
    return dot(weights, values, (1, 0))


def tiles_of(rows, most):
    tile = min(most, rows)
    return [slice(first, min(first + tile, rows)) for first in range(0, rows, tile)]


def until_small(flag, total, attempt):
    flag[0] = 1

    @pl.loop(0, 2)
    def _(turn):
        @pl.when(flag[0] == 1)
        def _():
            attempt(turn)
            flag[0] = jnp.where(jnp.max(total[:, :, HD:]) > LARGE, 1, 0).astype(jnp.int32)


class Fetch:
    def __init__(self, info, width, sems):
        self.columns = pl.ds(pl.multiple_of(info[0] * width, width), width)
        self.info, self.sems, self.waits = info, sems, []

    def start(self, candidates, flags, target, at):
        rows = candidates[0].shape[1]
        sem = self.sems.at[len(self.waits)]
        copies = [
            pltpu.make_async_copy(
                block.at[:, :, self.columns], target.at[:, pl.ds(at, rows), :], sem
            )
            for block in candidates
        ]
        if len(copies) == 1:
            copies[0].start()
        else:
            for copy, flag in zip(copies, flags):
                pl.when(flag)(copy.start)
        self.waits.append(copies[0])

    def wait(self):
        for copy in self.waits:
            copy.wait()


def settle(fetch, refs, entries, chosen):
    for index, candidates in enumerate(entries):
        sides = []
        for count in candidates:
            sides.append(refs[:count])
            refs = refs[count:]
        first = fetch.info[1 + index]
        at = 0
        for blocks in zip(*sides):
            fetch.start(blocks, [first == 1, first == 0], chosen.at[index], at)
            at += blocks[0].shape[1]


def accumulate(flag, total, aug, heads, queries_of, first_keys_of, own, chosen, ready):
    def columns(head):
        return slice(head * HD, (head + 1) * HD)

    def pieces(head, some):
        return some(head) + [
            (chosen[index, 0, :, columns(head)], chosen[index, 1, :, columns(head)])
            for index in range(chosen.shape[0])
        ]

    def tiles():
        for head in range(heads):
            queries = queries_of(head)
            for span, some in own:
                for tile in tiles_of(span.stop - span.start, TILE):
                    tile = slice(span.start + tile.start, span.start + tile.stop)
                    yield head, tile, queries[tile, :], some

    def largest(queries, key_rows):
        return jnp.max(dot(queries, key_rows, (1, 1)), axis=1, keepdims=True)

    def attempt(turn):
        @pl.when(turn == 0)
        def _():
            for head, tile, queries, _ in tiles():
                aug[head, tile, :] = reference_columns(largest(queries, first_keys_of(head)))
            ready()

        @pl.when(turn == 1)
        def _():
            for head, tile, queries, some in tiles():
                row_max = None
                for key_rows, _ in pieces(head, some):
                    piece_max = largest(queries, key_rows)
                    row_max = piece_max if row_max is None else jnp.maximum(row_max, piece_max)
                aug[head, tile, :] = reference_columns(row_max)

        for head, tile, queries, some in tiles():
            both = jnp.concatenate([queries, aug[head, tile, :]], axis=1)
            summed = None
            for key_rows, values in pieces(head, some):
                part = weighted(both, with_ones(key_rows), with_ones(values))
                summed = part if summed is None else summed + part
            total[head, tile, :] = summed

    until_small(flag, total, attempt)


def finish(out, total):
    for head in range(total.shape[0]):
        attended = (total[head, :, :HD] / total[head, :, HD:]).astype(out.dtype)
        out[:, :, head * HD : (head + 1) * HD] = attended.reshape(out.shape[:2] + (HD,))


def part_of(ref, part, head, width):
    first = part * width + head * HD
    return ref[:, :, first : first + HD].reshape(-1, HD)


def text_body(pair, entries, info, txt, *refs, wanted):
    stale, came = refs[:pair], refs[pair:-10]
    result, held_txt, out, chosen, beside, aug, total, flag, sems, plain = refs[-10:]
    width = chosen.shape[3]
    heads = width // HD

    @pl.when(info[wanted] == 1)
    def _():
        fetch = Fetch(info, width, sems)
        whole = pltpu.make_async_copy(txt, held_txt, plain.at[0])
        whole.start()
        at = 0
        for block in stale:
            fetch.start([block], [], beside.at[0], at)
            at += block.shape[1]
        settle(fetch, came, entries, chosen)
        whole.wait()

        def own(head):
            columns = slice(head * HD, (head + 1) * HD)
            return [
                (part_of(held_txt, 1, head, width), part_of(held_txt, 2, head, width)),
                (beside[0, 0, :, columns], beside[0, 1, :, columns]),
            ]

        accumulate(
            flag, total, aug, heads,
            lambda head: part_of(held_txt, 0, head, width),
            lambda head: part_of(held_txt, 1, head, width)[: min(FIRST_KEYS, total.shape[1]), :],
            [(slice(0, total.shape[1]), own)], chosen, fetch.wait,
        )
        finish(out, total)
        back = pltpu.make_async_copy(out, result, plain.at[0])
        back.start()
        back.wait()


def image_body(pair, entries, info, img, txt, *refs):
    stale, came = refs[:pair], refs[pair:-12]
    (result, held_img, held_txt, out, chosen, beside, aug, total, flag, sems, plain) = refs[-11:]
    width = chosen.shape[3]
    heads = width // HD
    rows = total.shape[1]
    group_rows, sources = rows // pair, img.shape[0] // pair
    fetch = Fetch(info, width, sems)
    wholes = [
        pltpu.make_async_copy(source, target, plain.at[index])
        for index, (source, target) in enumerate(((txt, held_txt), (img, held_img)))
    ]
    for whole in wholes:
        whole.start()
    if pair == 2:
        for group in range(pair):
            flags = [info[0] != group, info[0] == group]
            fetch.start(stale, flags, beside.at[group], group_rows)
    settle(fetch, came, entries, chosen)
    for whole in wholes:
        whole.wait()
    for group in range(pair):
        for part in range(2):
            fresh = held_img[
                group * sources : (group + 1) * sources, :, (1 + part) * width : (2 + part) * width
            ]
            beside[group, part, :group_rows, :] = fresh.reshape(group_rows, width)

    def own(group):
        def some(head):
            columns = slice(head * HD, (head + 1) * HD)
            return [
                (part_of(held_txt, 1, head, width), part_of(held_txt, 2, head, width)),
                (beside[group, 0, :, columns], beside[group, 1, :, columns]),
            ]

        return (slice(group * group_rows, (group + 1) * group_rows), some)

    text_keys = txt.shape[0] * txt.shape[1]
    accumulate(
        flag, total, aug, heads,
        lambda head: part_of(held_img, 0, head, width),
        lambda head: part_of(held_txt, 1, head, width)[: min(FIRST_KEYS, text_keys), :],
        [own(group) for group in range(pair)], chosen, fetch.wait,
    )
    finish(out, total)
    back = pltpu.make_async_copy(out, result, plain.at[0])
    back.start()
    back.wait()


def attend(name, body, info, fresh, stale, entries, groups, earlier=(), weight=1):
    first = fresh[0]
    width = first.shape[2] // 3
    heads, rows = width // HD, first.shape[0] * first.shape[1]
    keys = sum(block.shape[1] for block in stale)
    came = [b for candidates in entries for blocks in candidates for b in blocks]
    counts = [[len(blocks) for blocks in candidates] for candidates in entries]
    anywhere = pl.BlockSpec(memory_space=pl.ANY)
    result = jax.ShapeDtypeStruct(first.shape[:2] + (width,), first.dtype)
    scratch = [(array.shape, array.dtype) for array in fresh] + [
        (result.shape, result.dtype),
        ((len(entries), 2, keys, width), first.dtype),
        ((groups, 2, keys, width), first.dtype),
        ((heads, rows, HD), jnp.bfloat16),
        ((heads, rows, 2 * HD), jnp.float32),
    ]
    operands = [*fresh, *stale, *came, *earlier]
    return pl.pallas_call(
        functools.partial(body, len(stale), counts),
        in_specs=[pl.BlockSpec(memory_space=pltpu.SMEM)] + [anywhere] * len(operands),
        out_specs=anywhere,
        out_shape=result,
        scratch_shapes=[pltpu.VMEM(*one) for one in scratch]
        + [
            pltpu.SMEM((1,), jnp.int32),
            pltpu.SemaphoreType.DMA((len(stale) * (1 + len(entries)),)),
            pltpu.SemaphoreType.DMA((2,)),
        ],
        compiler_params=pltpu.CompilerParams(vmem_limit_bytes=ATTEND_LIMIT),
        cost_estimate=pl.CostEstimate(
            flops=weight * 4 * rows * keys * (2 + len(entries)) * width,
            bytes_accessed=weight * 4 * keys * (2 + len(entries)) * width,
            transcendentals=rows * keys * (2 + len(entries)) * heads,
        ),
        name=name,
    )(info, *operands)


def project_body(order, x_ref, weight, residual, gate, out, held, total, sems):
    copies = [
        pltpu.make_async_copy(weight.at[place], held.at[place], sems.at[place])
        for place in order
    ]
    for copy in copies:
        copy.start()
    for source, (place, copy) in enumerate(zip(order, copies)):
        copy.wait()
        part = jnp.dot(x_ref[source], held[place], preferred_element_type=jnp.float32)
        if source == 0:
            total[...] = part
        else:
            total[...] += part
    out[...] = (residual[...].astype(jnp.float32) + gate[...] * total[...]).astype(out.dtype)


def project(x, order, weight, residual, gate):
    rows, model = residual.shape
    destinations, _, width = x.shape
    vmem = pl.BlockSpec(memory_space=pltpu.VMEM)
    return pl.pallas_call(
        functools.partial(project_body, order),
        in_specs=[vmem, pl.BlockSpec(memory_space=pl.ANY), vmem, vmem],
        out_specs=vmem,
        out_shape=jax.ShapeDtypeStruct((rows, model), residual.dtype),
        scratch_shapes=[
            pltpu.VMEM((destinations, width, model), weight.dtype),
            pltpu.VMEM((rows, model), jnp.float32),
            pltpu.SemaphoreType.DMA((destinations,)),
        ],
        compiler_params=pltpu.CompilerParams(vmem_limit_bytes=WIDE_LIMIT),
        cost_estimate=pl.CostEstimate(
            flops=2 * rows * model * model, bytes_accessed=2 * model * model, transcendentals=0
        ),
        name="project",
    )(x, weight.reshape(destinations, width, model), residual, gate.reshape(1, model))


def unpack_body(order, x_ref, earlier, out):
    del earlier
    width = x_ref.shape[2]
    for source, place in enumerate(order):
        out[:, place * width : (place + 1) * width] = x_ref[source]


def unpack(x, order, earlier):
    rows, model = x.shape[1], x.shape[0] * x.shape[2]
    vmem = pl.BlockSpec(memory_space=pltpu.VMEM)
    return pl.pallas_call(
        functools.partial(unpack_body, order),
        in_specs=[vmem, pl.BlockSpec(memory_space=pl.ANY)],
        out_specs=vmem,
        out_shape=jax.ShapeDtypeStruct((rows, model), x.dtype),
        name="unpack_text",
    )(x, earlier)


def after_body(*refs):
    del refs


def after(x, other):
    anywhere = pl.BlockSpec(memory_space=pl.ANY)
    return pl.pallas_call(
        after_body,
        in_specs=[anywhere, anywhere],
        out_specs=anywhere,
        out_shape=jax.ShapeDtypeStruct(x.shape, x.dtype),
        input_output_aliases={0: 0},
        name="after",
    )(x, other)


def flag_body(flag, earlier, out):
    del earlier
    out[0] = flag[0]


def flag_after(flag, earlier):
    smem = pl.BlockSpec(memory_space=pltpu.SMEM)
    return pl.pallas_call(
        flag_body,
        in_specs=[smem, pl.BlockSpec(memory_space=pl.ANY)],
        out_specs=smem,
        out_shape=jax.ShapeDtypeStruct(flag.shape, flag.dtype),
        name="flag_after",
    )(flag, earlier)


def per_device(img_qkv, txt_qkv, stale_kv, residual, gate_scale, proj_weight):
    patches, head_owners = lax.axis_size("patch"), lax.axis_size("head")
    patch = lax.axis_index("patch")
    owned_heads = stale_kv.shape[2] // HD
    pair = 2 if patches % 2 == 0 and owned_heads % 2 == 0 else 1
    planes = patches // pair
    plane, core = patch // pair, patch % pair
    width = stale_kv.shape[2] // pair
    heads = width // HD
    img_rows, model = residual.shape
    text_rows = txt_qkv.shape[0] // pair
    destinations = pair * head_owners

    order = [(d % head_owners) * pair + d // head_owners for d in range(destinations)]
    groups = [[g * destinations + d for d in range(destinations)] for g in range(planes)]
    swap_pairs = [(p, p + 1 - 2 * (p % 2)) for p in range(patches)]

    def exchange(x):
        return lax.all_to_all(
            x, ("patch", "head"), split_axis=0, concat_axis=0, axis_index_groups=groups, tiled=True
        )

    def swap(x):
        return lax.ppermute(x, "patch", swap_pairs)

    def up_pairs(step):
        return [(z, z + 1) for z in range(step - 1, planes - 1)]

    def down_pairs(step):
        return [(z + 1, z) for z in range(0, planes - step)]

    core_only = core.astype(jnp.int32).reshape(1)
    txt = exchange(pack(core_only, txt_qkv, text_rows, head_owners, pair, width))

    zero_only = jnp.zeros((1,), jnp.int32)
    img = exchange(
        pack(zero_only, img_qkv, img_rows, head_owners, pair, width, [txt])
    )

    early = planes > 2
    inner = (plane > 0) & (plane < planes - 1)
    ahead = jnp.where(core == 0, plane, planes - 1 - plane) if pair == 2 else plane
    first_holds = [ahead >= i for i in range(1, planes)]
    info = jnp.stack([core] + first_holds + [inner if early else core >= 0]).astype(jnp.int32)

    def attend_text(known):
        if early:
            known = [[along[0]]] + known[1:-1] + [[against[0]]]
        return attend(
            "attend_text", functools.partial(text_body, wanted=planes), info, [txt], stale,
            known, 1, [img], 16,
        )

    along, against = [], []
    ordered = early and pair == 2
    if pair == 2:
        stale = [stale_kv, swap(stale_kv)]
        held = [stale_kv, stale_kv]
        for step in range(1, planes):
            pairs = [
                [(2 * a + turn, 2 * b) for a, b in up_pairs(step)]
                + [(2 * a + 1 - turn, 2 * b + 1) for a, b in down_pairs(step)]
                for turn in ((0, 1) if step == 1 else (0, 0))
            ]
            held = [lax.ppermute(block, "patch", way) for block, way in zip(held, pairs)]
            if step == 1:
                held = [held[0], after(held[1], txt)]
            if ordered and step == planes - 1:
                known = [[along[i - 1], against[planes - i - 1]] for i in range(2, planes - 1)]
                text_attn = attend_text([[]] + known + [[]])
                held = [after(block, text_attn) for block in held]
            along.append(held)
            against.append([swap(block) for block in held])
    else:
        stale = [stale_kv]
        from_below = from_above = stale_kv
        for step in range(1, planes):
            from_below = lax.ppermute(from_below, "patch", up_pairs(step))
            from_above = lax.ppermute(from_above, "patch", down_pairs(step))
            along.append([from_below])
            against.append([from_above])
    entries = [[along[i - 1], against[planes - i - 1]] for i in range(1, planes)]
    if not ordered:
        text_attn = attend_text(entries)
    image_attn = attend(
        "attend_image", image_body, info, [img, txt], stale, entries, pair, [text_attn]
    )
    text_out = unpack(exchange(text_attn), order, image_attn)
    image_out = project(exchange(image_attn), order, proj_weight, residual, gate_scale)
    if early:
        ends = [(1, 0), (planes - 2, planes - 1)]
        ends = [(a * pair + c, b * pair + c) for a, b in ends for c in range(pair)]
        hopped = lax.ppermute(text_out, "patch", ends)
        keep = flag_after(inner.astype(jnp.int32).reshape(1), image_out)
        text_out = jnp.where(keep[0] == 1, text_out, hopped)
    if pair == 2:
        other = swap(text_out)
        lower = core == 0
        text_out = jnp.concatenate(
            [jnp.where(lower, text_out, other), jnp.where(lower, other, text_out)], 0
        )
    return (image_out, text_out)


def solution(mesh):
    return jax.shard_map(
        per_device,
        mesh=mesh,
        in_specs=(
            P(("patch", "head"), None),
            P("head", None),
            P(None, "patch", "head"),
            P(("patch", "head"), None),
            P(),
            P(),
        ),
        out_specs=(P(("patch", "head"), None), P("head", None)),
        check_vma=False,
    )
```

```python
import functools
import math

import jax
import jax.numpy as jnp
from jax import lax
from jax.experimental import pallas as pl
from jax.experimental.pallas import tpu as pltpu
from jax.sharding import PartitionSpec as P

HD = 128
SCALE = math.log2(math.e) / math.sqrt(HD)
VMEM_LIMIT = 24 * 1024 * 1024
WIDE_LIMIT = 48 * 1024 * 1024
TILE = 256
LARGE = 2.0**60


def params():
    return pltpu.CompilerParams(
        vmem_limit_bytes=VMEM_LIMIT, dimension_semantics=("arbitrary",)
    )


def pack_body(info, *refs):
    sources, packed = refs[:6], refs[-1]
    first = 0
    for group in (sources[:3], sources[3:]):
        rows, width = group[0].shape
        for part, source in enumerate(group):
            packed[0, first : first + rows, part * width : (part + 1) * width] = source[...]
        first += rows


def pack(core, img_qkv, txt_qkv, text_rows, destinations, column_block, width, after):
    img_rows = img_qkv.shape[0]
    blocks = img_qkv.shape[1] // 3 // width

    def source(rows, part, by_core):
        def place(d, info):
            return (info[0] if by_core else 0, part * blocks + column_block(d))

        return pl.BlockSpec((rows, width), place)

    return pl.pallas_call(
        pack_body,
        grid_spec=pltpu.PrefetchScalarGridSpec(
            num_scalar_prefetch=1,
            grid=(destinations,),
            in_specs=[source(img_rows, part, False) for part in range(3)]
            + [source(text_rows, part, True) for part in range(3)]
            + [pl.BlockSpec(memory_space=pl.ANY)] * len(after),
            out_specs=pl.BlockSpec(
                (1, img_rows + text_rows, 3 * width), lambda d, info: (d, 0, 0)
            ),
        ),
        out_shape=jax.ShapeDtypeStruct(
            (destinations, img_rows + text_rows, 3 * width), img_qkv.dtype
        ),
        compiler_params=params(),
        name="pack_heads",
    )(core, img_qkv, img_qkv, img_qkv, txt_qkv, txt_qkv, txt_qkv, *after)


def dot(first, second, contract):
    return lax.dot_general(
        first, second, ((contract[:1], contract[1:]), ((), ())), preferred_element_type=jnp.float32
    )


def with_ones(block):
    return jnp.concatenate([block, jnp.ones_like(block)], axis=1)


def reference_columns(row_max):
    reference = row_max.astype(jnp.bfloat16).astype(jnp.float32)
    return jnp.broadcast_to(reference * (-1.0 / HD), (row_max.shape[0], HD)).astype(jnp.bfloat16)


def weighted(queries, key_rows, values):
    weights = jnp.exp2(dot(queries, key_rows, (1, 1)) * SCALE).astype(jnp.bfloat16)
    return dot(weights, values, (1, 0))


def tiles_of(rows):
    tile = min(TILE, rows)
    return [slice(first, min(first + tile, rows)) for first in range(0, rows, tile)]


def split_rows(block, img_rows):
    return (
        block[:, :img_rows, :].reshape(-1, HD),
        block[:, img_rows:, :].reshape(-1, HD),
    )


def until_small(flag, total, attempt):
    flag[0] = 1

    @pl.loop(0, 2)
    def _(turn):
        @pl.when(flag[0] == 1)
        def _():
            attempt(turn)
            flag[0] = jnp.where(jnp.max(total[0, :, HD:]) > LARGE, 1, 0).astype(jnp.int32)


def most_body(pair, img_rows, sides, info, *refs):
    q_ref, k_ref, v_ref = refs[:3]
    stale = refs[3 : 3 + pair]
    arrived = refs[3 + pair : 3 + pair + sides * pair]
    aug, total, flag = refs[3 + pair + sides * pair :]
    core = info[0]
    k_img, k_txt = split_rows(k_ref[...], img_rows)
    v_img, v_txt = split_rows(v_ref[...], img_rows)
    q_img, q_txt = split_rows(q_ref[...], img_rows)
    fresh_rows = q_img.shape[0]
    group_rows = fresh_rows // pair
    rows = fresh_rows + q_txt.shape[0]

    def queries_at(span):
        if span.stop <= fresh_rows:
            return q_img[span, :]
        return q_txt[span.start - fresh_rows : span.stop - fresh_rows, :]

    def own_sets():
        sets = []
        for group in range(pair):
            span = slice(group * group_rows, (group + 1) * group_rows)
            key_rows, values = [k_txt, k_img[span, :]], [v_txt, v_img[span, :]]
            if pair == 2:
                mine = core == group
                key_rows.append(jnp.where(mine, stale[1][0], stale[0][0]))
                values.append(jnp.where(mine, stale[1][1], stale[0][1]))
            sets.append((span, key_rows, values))
        sets.append(
            (
                slice(fresh_rows, rows),
                [k_txt] + [block[0] for block in stale],
                [v_txt] + [block[1] for block in stale],
            )
        )
        for span, key_rows, values in sets:
            key_rows, values = jnp.concatenate(key_rows, 0), jnp.concatenate(values, 0)
            spans = [
                slice(span.start + t.start, span.start + t.stop)
                for t in tiles_of(span.stop - span.start)
            ]
            yield spans, key_rows, values

    def each_arrived(act):
        for side in range(sides):
            blocks = arrived[side * pair : (side + 1) * pair]

            @pl.when(info[1 + side] == 1)
            def _():
                key_rows = jnp.concatenate([block[0] for block in blocks], 0)
                values = jnp.concatenate([block[1] for block in blocks], 0)
                for first in range(0, rows, fresh_rows):
                    for tile in tiles_of(min(fresh_rows, rows - first)):
                        act(slice(first + tile.start, first + tile.stop), key_rows, values)

    def largest(span, key_rows):
        return jnp.max(dot(queries_at(span), key_rows, (1, 1)), axis=1, keepdims=True)

    def attempt(turn):
        @pl.when(turn == 0)
        def _():
            for spans, key_rows, _ in own_sets():
                for span in spans:
                    aug[0, span, :] = reference_columns(
                        largest(span, key_rows[: min(256, key_rows.shape[0]), :])
                    )

        @pl.when(turn == 1)
        def _():
            def raise_to(span, key_rows, _):
                total[0, span, :] = jnp.maximum(
                    total[0, span, :], jnp.broadcast_to(largest(span, key_rows), total[0, span, :].shape)
                )

            for spans, key_rows, _ in own_sets():
                for span in spans:
                    total[0, span, :] = jnp.broadcast_to(
                        largest(span, key_rows), total[0, span, :].shape
                    )
            each_arrived(raise_to)
            for spans, _, _ in own_sets():
                for span in spans:
                    aug[0, span, :] = reference_columns(total[0, span, :1])

        def queries_of(span):
            return jnp.concatenate([queries_at(span), aug[0, span, :]], axis=1)

        def add(span, key_rows, values):
            total[0, span, :] += weighted(queries_of(span), with_ones(key_rows), with_ones(values))

        for spans, key_rows, values in own_sets():
            key_rows, values = with_ones(key_rows), with_ones(values)
            for span in spans:
                total[0, span, :] = weighted(queries_of(span), key_rows, values)
        each_arrived(add)

    until_small(flag, total, attempt)


def column_spec(array, offset):
    return pl.BlockSpec(array.shape[:2] + (HD,), lambda h, info: (0, 0, offset + h))


def head_spec(shape):
    return pl.BlockSpec((1,) + shape[1:], lambda h, info: (h, 0, 0))


def attend_cost(queries, keys, heads):
    return pl.CostEstimate(
        flops=4 * queries * keys * heads * HD,
        bytes_accessed=4 * queries * heads * HD + 4 * keys * heads * HD,
        transcendentals=queries * keys * heads,
    )


def attend_most(info, qkv, img_rows, stale, arrived):
    heads = qkv.shape[2] // (3 * HD)
    rows = qkv.shape[0] * qkv.shape[1]
    blocks = list(stale) + [block for side in arrived for block in side]
    shapes = [
        jax.ShapeDtypeStruct((heads, rows, HD), jnp.bfloat16),
        jax.ShapeDtypeStruct((heads, rows, 2 * HD), jnp.float32),
    ]
    keys = sum(block.shape[1] for block in blocks) // 2 + rows // 2
    return pl.pallas_call(
        functools.partial(most_body, len(stale), img_rows, len(arrived)),
        grid_spec=pltpu.PrefetchScalarGridSpec(
            num_scalar_prefetch=1,
            grid=(heads,),
            in_specs=[column_spec(qkv, part * heads) for part in range(3)]
            + [column_spec(block, 0) for block in blocks],
            out_specs=[head_spec(shape.shape) for shape in shapes],
            scratch_shapes=[pltpu.SMEM((1,), jnp.int32)],
        ),
        out_shape=shapes,
        compiler_params=params(),
        cost_estimate=attend_cost(rows, keys, heads),
        name="attend_most",
    )(info, qkv, qkv, qkv, *blocks)


def last_body(pair, img_rows, sides, info, *refs):
    q_ref, aug_ref, total_ref = refs[:3]
    arrived = refs[3 : 3 + sides * pair]
    out, total, shift, flag = refs[3 + sides * pair :]
    q_img, q_txt = split_rows(q_ref[...], img_rows)
    fresh_rows = q_img.shape[0]
    rows = total.shape[1]

    def queries_at(span):
        if span.stop <= fresh_rows:
            queries = q_img[span, :]
        else:
            queries = q_txt[span.start - fresh_rows : span.stop - fresh_rows, :]
        return jnp.concatenate([queries, aug_ref[0, span, :]], axis=1)

    def each_arrived(act):
        for side in range(sides):
            blocks = arrived[side * pair : (side + 1) * pair]

            @pl.when(info[1 + side] == 1)
            def _():
                key_rows = with_ones(jnp.concatenate([block[0] for block in blocks], 0))
                values = with_ones(jnp.concatenate([block[1] for block in blocks], 0))
                for first, last in ((0, fresh_rows), (fresh_rows, rows)):
                    for tile in tiles_of(last - first):
                        act(slice(first + tile.start, first + tile.stop), key_rows, values)

    def add(span, key_rows, values):
        total[0, span, :] += weighted(queries_at(span), key_rows, values)

    def raise_to(span, key_rows, _):
        above = jnp.max(dot(queries_at(span), key_rows, (1, 1)), axis=1, keepdims=True)
        shift[span, :] = jnp.maximum(shift[span, :], jnp.broadcast_to(above, shift[span, :].shape))

    def add_shifted(span, key_rows, values):
        scores = dot(queries_at(span), key_rows, (1, 1)) - shift[span, :1]
        total[0, span, :] += dot(jnp.exp2(scores * SCALE).astype(jnp.bfloat16), values, (1, 0))

    def attempt(turn):
        @pl.when(turn == 0)
        def _():
            total[...] = total_ref[...]
            each_arrived(add)

        @pl.when(turn == 1)
        def _():
            shift[...] = jnp.zeros_like(shift)
            each_arrived(raise_to)
            keep = jnp.exp2(shift[...] * -SCALE)
            total[0] = total_ref[0] * jnp.concatenate([keep, keep], axis=1)
            each_arrived(add_shifted)

    until_small(flag, total, attempt)
    attended = (total[0, :, :HD] / total[0, :, HD:]).astype(out.dtype)
    destinations = out.shape[0]
    out[:, :img_rows, :] = attended[:fresh_rows].reshape(destinations, img_rows, HD)
    out[:, img_rows:, :] = attended[fresh_rows:].reshape(destinations, -1, HD)


def attend_last(info, qkv, img_rows, state, arrived):
    heads = qkv.shape[2] // (3 * HD)
    rows = qkv.shape[0] * qkv.shape[1]
    blocks = [block for side in arrived for block in side]
    return pl.pallas_call(
        functools.partial(last_body, len(arrived[0]), img_rows, len(arrived)),
        grid_spec=pltpu.PrefetchScalarGridSpec(
            num_scalar_prefetch=1,
            grid=(heads,),
            in_specs=[column_spec(qkv, 0)]
            + [head_spec(part.shape) for part in state]
            + [column_spec(block, 0) for block in blocks],
            out_specs=pl.BlockSpec(qkv.shape[:2] + (HD,), lambda h, info: (0, 0, h)),
            scratch_shapes=[
                pltpu.VMEM((1, rows, 2 * HD), jnp.float32),
                pltpu.VMEM((rows, HD), jnp.float32),
                pltpu.SMEM((1,), jnp.int32),
            ],
        ),
        out_shape=jax.ShapeDtypeStruct(qkv.shape[:2] + (heads * HD,), qkv.dtype),
        compiler_params=params(),
        cost_estimate=attend_cost(rows, blocks[0].shape[1] * len(arrived[0]), heads),
        name="attend_last",
    )(info, qkv, *state, *blocks)


def project_body(order, x_ref, weight, residual, gate, out, held, total, sems):
    rows = out.shape[0]
    copies = [
        pltpu.make_async_copy(weight.at[place], held.at[place], sems.at[place])
        for place in order
    ]
    for copy in copies:
        copy.start()
    for source, (place, copy) in enumerate(zip(order, copies)):
        copy.wait()
        part = jnp.dot(x_ref[source, :rows, :], held[place], preferred_element_type=jnp.float32)
        if source == 0:
            total[...] = part
        else:
            total[...] += part
    out[...] = (residual[...].astype(jnp.float32) + gate[...] * total[...]).astype(out.dtype)


def project(x, order, weight, residual, gate):
    rows, model = residual.shape
    destinations, _, width = x.shape
    vmem = pl.BlockSpec(memory_space=pltpu.VMEM)
    return pl.pallas_call(
        functools.partial(project_body, order),
        in_specs=[vmem, pl.BlockSpec(memory_space=pl.ANY), vmem, vmem],
        out_specs=vmem,
        out_shape=jax.ShapeDtypeStruct((rows, model), residual.dtype),
        scratch_shapes=[
            pltpu.VMEM((destinations, width, model), weight.dtype),
            pltpu.VMEM((rows, model), jnp.float32),
            pltpu.SemaphoreType.DMA((destinations,)),
        ],
        compiler_params=pltpu.CompilerParams(vmem_limit_bytes=WIDE_LIMIT),
        cost_estimate=pl.CostEstimate(
            flops=2 * rows * model * model, bytes_accessed=2 * model * model, transcendentals=0
        ),
        name="project",
    )(x, weight.reshape(destinations, width, model), residual, gate.reshape(1, model))


def unpack_body(order, first, x_ref, out):
    width = x_ref.shape[2]
    for source, place in enumerate(order):
        out[:, place * width : (place + 1) * width] = x_ref[source, first:, :]


def unpack_text(x, order, first):
    model = x.shape[0] * x.shape[2]
    return pl.pallas_call(
        functools.partial(unpack_body, order, first),
        grid=(1,),
        in_specs=[pl.BlockSpec(x.shape, lambda n: (0, 0, 0))],
        out_specs=pl.BlockSpec((x.shape[1] - first, model), lambda n: (0, 0)),
        out_shape=jax.ShapeDtypeStruct((x.shape[1] - first, model), x.dtype),
        compiler_params=params(),
        name="unpack_text",
    )(x)


def per_device(img_qkv, txt_qkv, stale_kv, residual, gate_scale, proj_weight):
    patches, head_owners = lax.axis_size("patch"), lax.axis_size("head")
    patch = lax.axis_index("patch")
    owned_heads = stale_kv.shape[2] // HD
    pair = 2 if patches % 2 == 0 and owned_heads % 2 == 0 else 1
    planes = patches // pair
    plane, core = patch // pair, patch % pair
    width = stale_kv.shape[2] // pair
    img_rows = img_qkv.shape[0]
    text_rows = txt_qkv.shape[0] // pair
    destinations = pair * head_owners

    def column_block(d):
        return (d % head_owners) * pair + d // head_owners

    order = [column_block(d) for d in range(destinations)]
    groups = [[g * destinations + d for d in range(destinations)] for g in range(planes)]

    def exchange(x):
        return lax.all_to_all(
            x, ("patch", "head"), split_axis=0, concat_axis=0, axis_index_groups=groups, tiled=True
        )

    swap_pairs = [(p, p + 1 - 2 * (p % 2)) for p in range(patches)]
    stale = [lax.dynamic_slice_in_dim(stale_kv, core * width, width, 2)]
    if pair == 2:
        theirs = lax.dynamic_slice_in_dim(stale_kv, (1 - core) * width, width, 2)
        stale.append(lax.ppermute(theirs, "patch", swap_pairs))

    core_only = core.astype(jnp.int32).reshape(1)
    qkv = exchange(
        pack(core_only, img_qkv, txt_qkv, text_rows, destinations, column_block, width, stale[1:])
    )

    arrived, valid = [], []
    from_left, from_right = stale, stale
    for step in range(1, planes):
        right_pairs = [(p, p + pair) for p in range((step - 1) * pair, patches - pair)]
        left_pairs = [(p + pair, p) for p in range(0, patches - step * pair)]
        from_left = [lax.ppermute(block, "patch", right_pairs) for block in from_left]
        from_right = [lax.ppermute(block, "patch", left_pairs) for block in from_right]
        arrived += [from_left, from_right]
        valid += [plane >= step, plane + step < planes]
    early = max(0, len(arrived) - 2)
    info = jnp.stack([core] + valid[:early]).astype(jnp.int32)
    last_info = jnp.stack([core] + valid[early:]).astype(jnp.int32)
    state = attend_most(info, qkv, img_rows, stale, arrived[:early])
    attended = attend_last(last_info, qkv, img_rows, state, arrived[early:])

    back = exchange(attended)
    text_out = unpack_text(back, order, img_rows)
    if pair == 2:
        other = lax.ppermute(text_out, "patch", swap_pairs)
        lower = core == 0
        text_out = jnp.concatenate(
            [jnp.where(lower, text_out, other), jnp.where(lower, other, text_out)], 0
        )
    image_out = project(back, order, proj_weight, residual, gate_scale)
    return (image_out, text_out)


def solution(mesh):
    return jax.shard_map(
        per_device,
        mesh=mesh,
        in_specs=(
            P(("patch", "head"), None),
            P("head", None),
            P(None, "patch", "head"),
            P(("patch", "head"), None),
            P(),
            P(),
        ),
        out_specs=(P(("patch", "head"), None), P("head", None)),
        check_vma=False,
    )
```

```python
import functools
import math

import jax
import jax.numpy as jnp
from jax import lax
from jax.experimental import pallas as pl
from jax.experimental.pallas import tpu as pltpu
from jax.sharding import PartitionSpec as P

HD = 128
SCALE = math.log2(math.e) / math.sqrt(HD)
VMEM_LIMIT = 24 * 1024 * 1024
WIDE_LIMIT = 48 * 1024 * 1024
TILE = 256
LARGE = 2.0**60


def params():
    return pltpu.CompilerParams(
        vmem_limit_bytes=VMEM_LIMIT, dimension_semantics=("arbitrary",)
    )


def pack_body(info, *refs):
    sources, packed = refs[:6], refs[-1]
    first = 0
    for group in (sources[:3], sources[3:]):
        rows, width = group[0].shape
        for part, source in enumerate(group):
            packed[0, first : first + rows, part * width : (part + 1) * width] = source[...]
        first += rows


def pack(core, img_qkv, txt_qkv, text_rows, destinations, column_block, width, after):
    img_rows = img_qkv.shape[0]
    blocks = img_qkv.shape[1] // 3 // width

    def source(rows, part, by_core):
        def place(d, info):
            return (info[0] if by_core else 0, part * blocks + column_block(d))

        return pl.BlockSpec((rows, width), place)

    return pl.pallas_call(
        pack_body,
        grid_spec=pltpu.PrefetchScalarGridSpec(
            num_scalar_prefetch=1,
            grid=(destinations,),
            in_specs=[source(img_rows, part, False) for part in range(3)]
            + [source(text_rows, part, True) for part in range(3)]
            + [pl.BlockSpec(memory_space=pl.ANY)] * len(after),
            out_specs=pl.BlockSpec(
                (1, img_rows + text_rows, 3 * width), lambda d, info: (d, 0, 0)
            ),
        ),
        out_shape=jax.ShapeDtypeStruct(
            (destinations, img_rows + text_rows, 3 * width), img_qkv.dtype
        ),
        compiler_params=params(),
        name="pack_heads",
    )(core, img_qkv, img_qkv, img_qkv, txt_qkv, txt_qkv, txt_qkv, *after)


def dot(first, second, contract):
    return lax.dot_general(
        first, second, ((contract[:1], contract[1:]), ((), ())), preferred_element_type=jnp.float32
    )


def with_ones(block):
    return jnp.concatenate([block, jnp.ones_like(block)], axis=1)


def reference_columns(row_max):
    reference = row_max.astype(jnp.bfloat16).astype(jnp.float32)
    return jnp.broadcast_to(reference * (-1.0 / HD), (row_max.shape[0], HD)).astype(jnp.bfloat16)


def weighted(queries, key_rows, values):
    weights = jnp.exp2(dot(queries, key_rows, (1, 1)) * SCALE).astype(jnp.bfloat16)
    return dot(weights, values, (1, 0))


def tiles_of(rows):
    tile = min(TILE, rows)
    return [slice(first, min(first + tile, rows)) for first in range(0, rows, tile)]


def split_rows(block, img_rows):
    return (
        block[:, :img_rows, :].reshape(-1, HD),
        block[:, img_rows:, :].reshape(-1, HD),
    )


def until_small(flag, total, attempt):
    flag[0] = 1

    @pl.loop(0, 2)
    def _(turn):
        @pl.when(flag[0] == 1)
        def _():
            attempt(turn)
            flag[0] = jnp.where(jnp.max(total[0, :, HD:]) > LARGE, 1, 0).astype(jnp.int32)


def whereabouts(pair, first_step, sides):
    patch, planes = lax.axis_index("patch"), lax.axis_size("patch") // pair
    plane = patch // pair
    flags = []
    for side in range(sides):
        step = first_step + side // 2
        there = plane >= step if side % 2 == 0 else plane + step < planes
        flags.append(there.astype(jnp.int32))
    return [patch % pair] + flags


def most_body(pair, img_rows, sides, _, *refs):
    info = whereabouts(pair, 1, sides)
    q_ref, k_ref, v_ref = refs[:3]
    stale = refs[3 : 3 + pair]
    arrived = refs[3 + pair : 3 + pair + sides * pair]
    aug, total, flag = refs[3 + pair + sides * pair :]
    core = info[0]
    k_img, k_txt = split_rows(k_ref[...], img_rows)
    v_img, v_txt = split_rows(v_ref[...], img_rows)
    q_img, q_txt = split_rows(q_ref[...], img_rows)
    fresh_rows = q_img.shape[0]
    group_rows = fresh_rows // pair
    rows = fresh_rows + q_txt.shape[0]

    def queries_at(span):
        if span.stop <= fresh_rows:
            return q_img[span, :]
        return q_txt[span.start - fresh_rows : span.stop - fresh_rows, :]

    def own_sets():
        sets = []
        for group in range(pair):
            span = slice(group * group_rows, (group + 1) * group_rows)
            key_rows, values = [k_txt, k_img[span, :]], [v_txt, v_img[span, :]]
            if pair == 2:
                mine = core == group
                key_rows.append(jnp.where(mine, stale[1][0], stale[0][0]))
                values.append(jnp.where(mine, stale[1][1], stale[0][1]))
            sets.append((span, key_rows, values))
        sets.append(
            (
                slice(fresh_rows, rows),
                [k_txt] + [block[0] for block in stale],
                [v_txt] + [block[1] for block in stale],
            )
        )
        for span, key_rows, values in sets:
            key_rows, values = jnp.concatenate(key_rows, 0), jnp.concatenate(values, 0)
            spans = [
                slice(span.start + t.start, span.start + t.stop)
                for t in tiles_of(span.stop - span.start)
            ]
            yield spans, key_rows, values

    def each_arrived(act):
        for side in range(sides):
            blocks = arrived[side * pair : (side + 1) * pair]

            @pl.when(info[1 + side] == 1)
            def _():
                key_rows = jnp.concatenate([block[0] for block in blocks], 0)
                values = jnp.concatenate([block[1] for block in blocks], 0)
                for first in range(0, rows, fresh_rows):
                    for tile in tiles_of(min(fresh_rows, rows - first)):
                        act(slice(first + tile.start, first + tile.stop), key_rows, values)

    def largest(span, key_rows):
        return jnp.max(dot(queries_at(span), key_rows, (1, 1)), axis=1, keepdims=True)

    def attempt(turn):
        @pl.when(turn == 0)
        def _():
            for spans, key_rows, _ in own_sets():
                for span in spans:
                    aug[0, span, :] = reference_columns(
                        largest(span, key_rows[: min(256, key_rows.shape[0]), :])
                    )

        @pl.when(turn == 1)
        def _():
            def raise_to(span, key_rows, _):
                total[0, span, :] = jnp.maximum(
                    total[0, span, :], jnp.broadcast_to(largest(span, key_rows), total[0, span, :].shape)
                )

            for spans, key_rows, _ in own_sets():
                for span in spans:
                    total[0, span, :] = jnp.broadcast_to(
                        largest(span, key_rows), total[0, span, :].shape
                    )
            each_arrived(raise_to)
            for spans, _, _ in own_sets():
                for span in spans:
                    aug[0, span, :] = reference_columns(total[0, span, :1])

        def queries_of(span):
            return jnp.concatenate([queries_at(span), aug[0, span, :]], axis=1)

        def add(span, key_rows, values):
            total[0, span, :] += weighted(queries_of(span), with_ones(key_rows), with_ones(values))

        for spans, key_rows, values in own_sets():
            key_rows, values = with_ones(key_rows), with_ones(values)
            for span in spans:
                total[0, span, :] = weighted(queries_of(span), key_rows, values)
        each_arrived(add)

    until_small(flag, total, attempt)


def column_spec(array, offset):
    return pl.BlockSpec(array.shape[:2] + (HD,), lambda h, info: (0, 0, offset + h))


def head_spec(shape):
    return pl.BlockSpec((1,) + shape[1:], lambda h, info: (h, 0, 0))


def attend_cost(queries, keys, heads):
    return pl.CostEstimate(
        flops=4 * queries * keys * heads * HD,
        bytes_accessed=4 * queries * heads * HD + 4 * keys * heads * HD,
        transcendentals=queries * keys * heads,
    )


def attend_most(info, qkv, img_rows, stale, arrived):
    heads = qkv.shape[2] // (3 * HD)
    rows = qkv.shape[0] * qkv.shape[1]
    blocks = list(stale) + [block for side in arrived for block in side]
    shapes = [
        jax.ShapeDtypeStruct((heads, rows, HD), jnp.bfloat16),
        jax.ShapeDtypeStruct((heads, rows, 2 * HD), jnp.float32),
    ]
    keys = sum(block.shape[1] for block in blocks) // 2 + rows // 2
    return pl.pallas_call(
        functools.partial(most_body, len(stale), img_rows, len(arrived)),
        grid_spec=pltpu.PrefetchScalarGridSpec(
            num_scalar_prefetch=1,
            grid=(heads,),
            in_specs=[column_spec(qkv, part * heads) for part in range(3)]
            + [column_spec(block, 0) for block in blocks],
            out_specs=[head_spec(shape.shape) for shape in shapes],
            scratch_shapes=[pltpu.SMEM((1,), jnp.int32)],
        ),
        out_shape=shapes,
        compiler_params=params(),
        cost_estimate=attend_cost(rows, keys, heads),
        name="attend_most",
    )(info, qkv, qkv, qkv, *blocks)


def last_body(pair, img_rows, sides, _, *refs):
    info = whereabouts(pair, lax.axis_size("patch") // pair - 1, sides)
    q_ref, aug_ref, total_ref = refs[:3]
    arrived = refs[3 : 3 + sides * pair]
    out, total, shift, flag = refs[3 + sides * pair :]
    q_img, q_txt = split_rows(q_ref[...], img_rows)
    fresh_rows = q_img.shape[0]
    rows = total.shape[1]

    def queries_at(span):
        if span.stop <= fresh_rows:
            queries = q_img[span, :]
        else:
            queries = q_txt[span.start - fresh_rows : span.stop - fresh_rows, :]
        return jnp.concatenate([queries, aug_ref[0, span, :]], axis=1)

    def each_arrived(act):
        for side in range(sides):
            blocks = arrived[side * pair : (side + 1) * pair]

            @pl.when(info[1 + side] == 1)
            def _():
                key_rows = with_ones(jnp.concatenate([block[0] for block in blocks], 0))
                values = with_ones(jnp.concatenate([block[1] for block in blocks], 0))
                for first, last in ((0, fresh_rows), (fresh_rows, rows)):
                    for tile in tiles_of(last - first):
                        act(slice(first + tile.start, first + tile.stop), key_rows, values)

    def add(span, key_rows, values):
        total[0, span, :] += weighted(queries_at(span), key_rows, values)

    def raise_to(span, key_rows, _):
        above = jnp.max(dot(queries_at(span), key_rows, (1, 1)), axis=1, keepdims=True)
        shift[span, :] = jnp.maximum(shift[span, :], jnp.broadcast_to(above, shift[span, :].shape))

    def add_shifted(span, key_rows, values):
        scores = dot(queries_at(span), key_rows, (1, 1)) - shift[span, :1]
        total[0, span, :] += dot(jnp.exp2(scores * SCALE).astype(jnp.bfloat16), values, (1, 0))

    def attempt(turn):
        @pl.when(turn == 0)
        def _():
            total[...] = total_ref[...]
            each_arrived(add)

        @pl.when(turn == 1)
        def _():
            shift[...] = jnp.zeros_like(shift)
            each_arrived(raise_to)
            keep = jnp.exp2(shift[...] * -SCALE)
            total[0] = total_ref[0] * jnp.concatenate([keep, keep], axis=1)
            each_arrived(add_shifted)

    until_small(flag, total, attempt)
    attended = (total[0, :, :HD] / total[0, :, HD:]).astype(out.dtype)
    destinations = out.shape[0]
    out[:, :img_rows, :] = attended[:fresh_rows].reshape(destinations, img_rows, HD)
    out[:, img_rows:, :] = attended[fresh_rows:].reshape(destinations, -1, HD)


def attend_last(info, qkv, img_rows, state, arrived):
    heads = qkv.shape[2] // (3 * HD)
    rows = qkv.shape[0] * qkv.shape[1]
    blocks = [block for side in arrived for block in side]
    return pl.pallas_call(
        functools.partial(last_body, len(arrived[0]), img_rows, len(arrived)),
        grid_spec=pltpu.PrefetchScalarGridSpec(
            num_scalar_prefetch=1,
            grid=(heads,),
            in_specs=[column_spec(qkv, 0)]
            + [head_spec(part.shape) for part in state]
            + [column_spec(block, 0) for block in blocks],
            out_specs=pl.BlockSpec(qkv.shape[:2] + (HD,), lambda h, info: (0, 0, h)),
            scratch_shapes=[
                pltpu.VMEM((1, rows, 2 * HD), jnp.float32),
                pltpu.VMEM((rows, HD), jnp.float32),
                pltpu.SMEM((1,), jnp.int32),
            ],
        ),
        out_shape=jax.ShapeDtypeStruct(qkv.shape[:2] + (heads * HD,), qkv.dtype),
        compiler_params=params(),
        cost_estimate=attend_cost(rows, blocks[0].shape[1] * len(arrived[0]), heads),
        name="attend_last",
    )(info, qkv, *state, *blocks)


def project_body(order, x_ref, weight, residual, gate, out, held, total, sems):
    rows = out.shape[0]
    copies = [
        pltpu.make_async_copy(weight.at[place], held.at[place], sems.at[place])
        for place in order
    ]
    for copy in copies:
        copy.start()
    for source, (place, copy) in enumerate(zip(order, copies)):
        copy.wait()
        part = jnp.dot(x_ref[source, :rows, :], held[place], preferred_element_type=jnp.float32)
        if source == 0:
            total[...] = part
        else:
            total[...] += part
    out[...] = (residual[...].astype(jnp.float32) + gate[...] * total[...]).astype(out.dtype)


def project(x, order, weight, residual, gate):
    rows, model = residual.shape
    destinations, _, width = x.shape
    vmem = pl.BlockSpec(memory_space=pltpu.VMEM)
    return pl.pallas_call(
        functools.partial(project_body, order),
        in_specs=[vmem, pl.BlockSpec(memory_space=pl.ANY), vmem, vmem],
        out_specs=vmem,
        out_shape=jax.ShapeDtypeStruct((rows, model), residual.dtype),
        scratch_shapes=[
            pltpu.VMEM((destinations, width, model), weight.dtype),
            pltpu.VMEM((rows, model), jnp.float32),
            pltpu.SemaphoreType.DMA((destinations,)),
        ],
        compiler_params=pltpu.CompilerParams(vmem_limit_bytes=WIDE_LIMIT),
        cost_estimate=pl.CostEstimate(
            flops=2 * rows * model * model, bytes_accessed=2 * model * model, transcendentals=0
        ),
        name="project",
    )(x, weight.reshape(destinations, width, model), residual, gate.reshape(1, model))


def unpack_body(order, first, x_ref, out):
    width = x_ref.shape[2]
    for source, place in enumerate(order):
        out[:, place * width : (place + 1) * width] = x_ref[source, first:, :]


def unpack_text(x, order, first):
    model = x.shape[0] * x.shape[2]
    return pl.pallas_call(
        functools.partial(unpack_body, order, first),
        grid=(1,),
        in_specs=[pl.BlockSpec(x.shape, lambda n: (0, 0, 0))],
        out_specs=pl.BlockSpec((x.shape[1] - first, model), lambda n: (0, 0)),
        out_shape=jax.ShapeDtypeStruct((x.shape[1] - first, model), x.dtype),
        compiler_params=params(),
        name="unpack_text",
    )(x)


def per_device(img_qkv, txt_qkv, stale_kv, residual, gate_scale, proj_weight):
    patches, head_owners = lax.axis_size("patch"), lax.axis_size("head")
    patch = lax.axis_index("patch")
    owned_heads = stale_kv.shape[2] // HD
    pair = 2 if patches % 2 == 0 and owned_heads % 2 == 0 else 1
    planes = patches // pair
    plane, core = patch // pair, patch % pair
    width = stale_kv.shape[2] // pair
    img_rows = img_qkv.shape[0]
    text_rows = txt_qkv.shape[0] // pair
    destinations = pair * head_owners

    def column_block(d):
        return (d % head_owners) * pair + d // head_owners

    order = [column_block(d) for d in range(destinations)]
    groups = [[g * destinations + d for d in range(destinations)] for g in range(planes)]

    def exchange(x):
        return lax.all_to_all(
            x, ("patch", "head"), split_axis=0, concat_axis=0, axis_index_groups=groups, tiled=True
        )

    swap_pairs = [(p, p + 1 - 2 * (p % 2)) for p in range(patches)]
    stale = [lax.dynamic_slice_in_dim(stale_kv, core * width, width, 2)]
    if pair == 2:
        theirs = lax.dynamic_slice_in_dim(stale_kv, (1 - core) * width, width, 2)
        stale.append(lax.ppermute(theirs, "patch", swap_pairs))

    core_only = core.astype(jnp.int32).reshape(1)
    qkv = exchange(
        pack(core_only, img_qkv, txt_qkv, text_rows, destinations, column_block, width, stale[1:])
    )

    arrived = []
    from_left, from_right = stale, stale
    for step in range(1, planes):
        right_pairs = [(p, p + pair) for p in range((step - 1) * pair, patches - pair)]
        left_pairs = [(p + pair, p) for p in range(0, patches - step * pair)]
        from_left = [lax.ppermute(block, "patch", right_pairs) for block in from_left]
        from_right = [lax.ppermute(block, "patch", left_pairs) for block in from_right]
        arrived += [from_left, from_right]
    early = max(0, len(arrived) - 2)
    state = attend_most(core_only, qkv, img_rows, stale, arrived[:early])
    attended = attend_last(core_only, qkv, img_rows, state, arrived[early:])

    back = exchange(attended)
    text_out = unpack_text(back, order, img_rows)
    if pair == 2:
        other = lax.ppermute(text_out, "patch", swap_pairs)
        lower = core == 0
        text_out = jnp.concatenate(
            [jnp.where(lower, text_out, other), jnp.where(lower, other, text_out)], 0
        )
    image_out = project(back, order, proj_weight, residual, gate_scale)
    return (image_out, text_out)


def solution(mesh):
    return jax.shard_map(
        per_device,
        mesh=mesh,
        in_specs=(
            P(("patch", "head"), None),
            P("head", None),
            P(None, "patch", "head"),
            P(("patch", "head"), None),
            P(),
            P(),
        ),
        out_specs=(P(("patch", "head"), None), P("head", None)),
        check_vma=False,
    )
```

```python
import functools
import math

import jax
import jax.numpy as jnp
from jax import lax
from jax.experimental import pallas as pl
from jax.experimental.pallas import tpu as pltpu
from jax.sharding import PartitionSpec as P

HD = 128
SCALE = math.log2(math.e) / math.sqrt(HD)
VMEM_LIMIT = 24 * 1024 * 1024
WIDE_LIMIT = 48 * 1024 * 1024
TILE = 256
LARGE = 2.0**60


def params():
    return pltpu.CompilerParams(
        vmem_limit_bytes=VMEM_LIMIT, dimension_semantics=("arbitrary",)
    )


def pack_body(info, *refs):
    sources, packed = refs[:6], refs[-1]
    first = 0
    for group in (sources[:3], sources[3:]):
        rows, width = group[0].shape
        for part, source in enumerate(group):
            packed[0, first : first + rows, part * width : (part + 1) * width] = source[...]
        first += rows


def pack(core, img_qkv, txt_qkv, text_rows, destinations, column_block, width, after):
    img_rows = img_qkv.shape[0]
    blocks = img_qkv.shape[1] // 3 // width

    def source(rows, part, by_core):
        def place(d, info):
            return (info[0] if by_core else 0, part * blocks + column_block(d))

        return pl.BlockSpec((rows, width), place)

    return pl.pallas_call(
        pack_body,
        grid_spec=pltpu.PrefetchScalarGridSpec(
            num_scalar_prefetch=1,
            grid=(destinations,),
            in_specs=[source(img_rows, part, False) for part in range(3)]
            + [source(text_rows, part, True) for part in range(3)]
            + [pl.BlockSpec(memory_space=pl.ANY)] * len(after),
            out_specs=pl.BlockSpec(
                (1, img_rows + text_rows, 3 * width), lambda d, info: (d, 0, 0)
            ),
        ),
        out_shape=jax.ShapeDtypeStruct(
            (destinations, img_rows + text_rows, 3 * width), img_qkv.dtype
        ),
        compiler_params=params(),
        name="pack_heads",
    )(core, img_qkv, img_qkv, img_qkv, txt_qkv, txt_qkv, txt_qkv, *after)


def dot(first, second, contract):
    return lax.dot_general(
        first, second, ((contract[:1], contract[1:]), ((), ())), preferred_element_type=jnp.float32
    )


def with_ones(block):
    return jnp.concatenate([block, jnp.ones_like(block)], axis=1)


def reference_columns(row_max):
    reference = row_max.astype(jnp.bfloat16).astype(jnp.float32)
    return jnp.broadcast_to(reference * (-1.0 / HD), (row_max.shape[0], HD)).astype(jnp.bfloat16)


def weighted(queries, key_rows, values):
    weights = jnp.exp2(dot(queries, key_rows, (1, 1)) * SCALE).astype(jnp.bfloat16)
    return dot(weights, values, (1, 0))


def tiles_of(rows):
    tile = min(TILE, rows)
    return [slice(first, min(first + tile, rows)) for first in range(0, rows, tile)]


def split_rows(block, img_rows):
    return (
        block[:, :img_rows, :].reshape(-1, HD),
        block[:, img_rows:, :].reshape(-1, HD),
    )


def until_small(flag, total, attempt):
    flag[0] = 1

    @pl.loop(0, 2)
    def _(turn):
        @pl.when(flag[0] == 1)
        def _():
            attempt(turn)
            flag[0] = jnp.where(jnp.max(total[0, :, HD:]) > LARGE, 1, 0).astype(jnp.int32)


def whereabouts(pair, first_step, sides):
    patch, planes = lax.axis_index("patch"), lax.axis_size("patch") // pair
    plane = patch // pair
    flags = []
    for side in range(sides):
        step = first_step + side // 2
        there = plane >= step if side % 2 == 0 else plane + step < planes
        flags.append(there.astype(jnp.int32))
    return [patch % pair] + flags


def most_body(pair, img_rows, sides, _, *refs):
    info = whereabouts(pair, 1, sides)
    q_ref, k_ref, v_ref = refs[:3]
    stale = refs[3 : 3 + pair]
    arrived = refs[3 + pair : 3 + pair + sides * pair]
    aug, total, flag = refs[3 + pair + sides * pair :]
    core = info[0]
    k_img, k_txt = split_rows(k_ref[...], img_rows)
    v_img, v_txt = split_rows(v_ref[...], img_rows)
    q_img, q_txt = split_rows(q_ref[...], img_rows)
    fresh_rows = q_img.shape[0]
    group_rows = fresh_rows // pair
    rows = fresh_rows + q_txt.shape[0]

    def queries_at(span):
        if span.stop <= fresh_rows:
            return q_img[span, :]
        return q_txt[span.start - fresh_rows : span.stop - fresh_rows, :]

    def own_sets():
        sets = []
        for group in range(pair):
            span = slice(group * group_rows, (group + 1) * group_rows)
            key_rows, values = [k_txt, k_img[span, :]], [v_txt, v_img[span, :]]
            if pair == 2:
                mine = core == group
                key_rows.append(jnp.where(mine, stale[1][0], stale[0][0]))
                values.append(jnp.where(mine, stale[1][1], stale[0][1]))
            sets.append((span, key_rows, values))
        sets.append(
            (
                slice(fresh_rows, rows),
                [k_txt] + [block[0] for block in stale],
                [v_txt] + [block[1] for block in stale],
            )
        )
        for span, key_rows, values in sets:
            key_rows, values = jnp.concatenate(key_rows, 0), jnp.concatenate(values, 0)
            spans = [
                slice(span.start + t.start, span.start + t.stop)
                for t in tiles_of(span.stop - span.start)
            ]
            yield spans, key_rows, values

    def each_arrived(act):
        for side in range(sides):
            blocks = arrived[side * pair : (side + 1) * pair]

            @pl.when(info[1 + side] == 1)
            def _():
                key_rows = jnp.concatenate([block[0] for block in blocks], 0)
                values = jnp.concatenate([block[1] for block in blocks], 0)
                for first in range(0, rows, fresh_rows):
                    for tile in tiles_of(min(fresh_rows, rows - first)):
                        act(slice(first + tile.start, first + tile.stop), key_rows, values)

    def largest(span, key_rows):
        return jnp.max(dot(queries_at(span), key_rows, (1, 1)), axis=1, keepdims=True)

    def attempt(turn):
        @pl.when(turn == 0)
        def _():
            for spans, key_rows, _ in own_sets():
                for span in spans:
                    aug[0, span, :] = reference_columns(
                        largest(span, key_rows[: min(256, key_rows.shape[0]), :])
                    )

        @pl.when(turn == 1)
        def _():
            def raise_to(span, key_rows, _):
                total[0, span, :] = jnp.maximum(
                    total[0, span, :], jnp.broadcast_to(largest(span, key_rows), total[0, span, :].shape)
                )

            for spans, key_rows, _ in own_sets():
                for span in spans:
                    total[0, span, :] = jnp.broadcast_to(
                        largest(span, key_rows), total[0, span, :].shape
                    )
            each_arrived(raise_to)
            for spans, _, _ in own_sets():
                for span in spans:
                    aug[0, span, :] = reference_columns(total[0, span, :1])

        def queries_of(span):
            return jnp.concatenate([queries_at(span), aug[0, span, :]], axis=1)

        def add(span, key_rows, values):
            total[0, span, :] += weighted(queries_of(span), with_ones(key_rows), with_ones(values))

        for spans, key_rows, values in own_sets():
            key_rows, values = with_ones(key_rows), with_ones(values)
            for span in spans:
                total[0, span, :] = weighted(queries_of(span), key_rows, values)
        each_arrived(add)

    until_small(flag, total, attempt)


def column_spec(array, offset):
    return pl.BlockSpec(array.shape[:2] + (HD,), lambda h, info: (0, 0, offset + h))


def head_spec(shape):
    return pl.BlockSpec((1,) + shape[1:], lambda h, info: (h, 0, 0))


def attend_cost(queries, keys, heads):
    return pl.CostEstimate(
        flops=4 * queries * keys * heads * HD,
        bytes_accessed=4 * queries * heads * HD + 4 * keys * heads * HD,
        transcendentals=queries * keys * heads,
    )


def attend_most(info, qkv, img_rows, stale, arrived):
    heads = qkv.shape[2] // (3 * HD)
    rows = qkv.shape[0] * qkv.shape[1]
    blocks = list(stale) + [block for side in arrived for block in side]
    shapes = [
        jax.ShapeDtypeStruct((heads, rows, HD), jnp.bfloat16),
        jax.ShapeDtypeStruct((heads, rows, 2 * HD), jnp.float32),
    ]
    keys = sum(block.shape[1] for block in blocks) // 2 + rows // 2
    return pl.pallas_call(
        functools.partial(most_body, len(stale), img_rows, len(arrived)),
        grid_spec=pltpu.PrefetchScalarGridSpec(
            num_scalar_prefetch=1,
            grid=(heads,),
            in_specs=[column_spec(qkv, part * heads) for part in range(3)]
            + [column_spec(block, 0) for block in blocks],
            out_specs=[head_spec(shape.shape) for shape in shapes],
            scratch_shapes=[pltpu.SMEM((1,), jnp.int32)],
        ),
        out_shape=shapes,
        compiler_params=params(),
        cost_estimate=attend_cost(rows, keys, heads),
        name="attend_most",
    )(info, qkv, qkv, qkv, *blocks)


def last_body(pair, img_rows, sides, _, *refs):
    info = whereabouts(pair, lax.axis_size("patch") // pair - 1, sides)
    q_ref, aug_ref, total_ref = refs[:3]
    arrived = refs[3 : 3 + sides * pair]
    out, total, shift, flag = refs[3 + sides * pair :]
    q_img, q_txt = split_rows(q_ref[...], img_rows)
    fresh_rows = q_img.shape[0]
    rows = total.shape[1]

    def queries_at(span):
        if span.stop <= fresh_rows:
            queries = q_img[span, :]
        else:
            queries = q_txt[span.start - fresh_rows : span.stop - fresh_rows, :]
        return jnp.concatenate([queries, aug_ref[0, span, :]], axis=1)

    def each_arrived(act):
        for side in range(sides):
            blocks = arrived[side * pair : (side + 1) * pair]

            @pl.when(info[1 + side] == 1)
            def _():
                key_rows = with_ones(jnp.concatenate([block[0] for block in blocks], 0))
                values = with_ones(jnp.concatenate([block[1] for block in blocks], 0))
                for first, last in ((0, fresh_rows), (fresh_rows, rows)):
                    for tile in tiles_of(last - first):
                        act(slice(first + tile.start, first + tile.stop), key_rows, values)

    def add(span, key_rows, values):
        total[0, span, :] += weighted(queries_at(span), key_rows, values)

    def raise_to(span, key_rows, _):
        above = jnp.max(dot(queries_at(span), key_rows, (1, 1)), axis=1, keepdims=True)
        shift[span, :] = jnp.maximum(shift[span, :], jnp.broadcast_to(above, shift[span, :].shape))

    def add_shifted(span, key_rows, values):
        scores = dot(queries_at(span), key_rows, (1, 1)) - shift[span, :1]
        total[0, span, :] += dot(jnp.exp2(scores * SCALE).astype(jnp.bfloat16), values, (1, 0))

    def attempt(turn):
        @pl.when(turn == 0)
        def _():
            total[...] = total_ref[...]
            each_arrived(add)

        @pl.when(turn == 1)
        def _():
            shift[...] = jnp.zeros_like(shift)
            each_arrived(raise_to)
            keep = jnp.exp2(shift[...] * -SCALE)
            total[0] = total_ref[0] * jnp.concatenate([keep, keep], axis=1)
            each_arrived(add_shifted)

    until_small(flag, total, attempt)
    attended = (total[0, :, :HD] / total[0, :, HD:]).astype(out.dtype)
    destinations = out.shape[0]
    out[:, :img_rows, :] = attended[:fresh_rows].reshape(destinations, img_rows, HD)
    out[:, img_rows:, :] = attended[fresh_rows:].reshape(destinations, -1, HD)


def attend_last(info, qkv, img_rows, state, arrived):
    heads = qkv.shape[2] // (3 * HD)
    rows = qkv.shape[0] * qkv.shape[1]
    blocks = [block for side in arrived for block in side]
    return pl.pallas_call(
        functools.partial(last_body, len(arrived[0]), img_rows, len(arrived)),
        grid_spec=pltpu.PrefetchScalarGridSpec(
            num_scalar_prefetch=1,
            grid=(heads,),
            in_specs=[column_spec(qkv, 0)]
            + [head_spec(part.shape) for part in state]
            + [column_spec(block, 0) for block in blocks],
            out_specs=pl.BlockSpec(qkv.shape[:2] + (HD,), lambda h, info: (0, 0, h)),
            scratch_shapes=[
                pltpu.VMEM((1, rows, 2 * HD), jnp.float32),
                pltpu.VMEM((rows, HD), jnp.float32),
                pltpu.SMEM((1,), jnp.int32),
            ],
        ),
        out_shape=jax.ShapeDtypeStruct(qkv.shape[:2] + (heads * HD,), qkv.dtype),
        compiler_params=params(),
        cost_estimate=attend_cost(rows, blocks[0].shape[1] * len(arrived[0]), heads),
        name="attend_last",
    )(info, qkv, *state, *blocks)


def project_body(order, x_ref, weight, residual, gate, out, held, total, sems):
    rows = out.shape[0]
    copies = [
        pltpu.make_async_copy(weight.at[place], held.at[place], sems.at[place])
        for place in order
    ]
    for copy in copies:
        copy.start()
    for source, (place, copy) in enumerate(zip(order, copies)):
        copy.wait()
        part = jnp.dot(x_ref[source, :rows, :], held[place], preferred_element_type=jnp.float32)
        if source == 0:
            total[...] = part
        else:
            total[...] += part
    out[...] = (residual[...].astype(jnp.float32) + gate[...] * total[...]).astype(out.dtype)


def project(x, order, weight, residual, gate):
    rows, model = residual.shape
    destinations, _, width = x.shape
    vmem = pl.BlockSpec(memory_space=pltpu.VMEM)
    return pl.pallas_call(
        functools.partial(project_body, order),
        in_specs=[vmem, pl.BlockSpec(memory_space=pl.ANY), vmem, vmem],
        out_specs=vmem,
        out_shape=jax.ShapeDtypeStruct((rows, model), residual.dtype),
        scratch_shapes=[
            pltpu.VMEM((destinations, width, model), weight.dtype),
            pltpu.VMEM((rows, model), jnp.float32),
            pltpu.SemaphoreType.DMA((destinations,)),
        ],
        compiler_params=pltpu.CompilerParams(vmem_limit_bytes=WIDE_LIMIT),
        cost_estimate=pl.CostEstimate(
            flops=2 * rows * model * model, bytes_accessed=2 * model * model, transcendentals=0
        ),
        name="project",
    )(x, weight.reshape(destinations, width, model), residual, gate.reshape(1, model))


def unpack_body(order, first, x_ref, out):
    width = x_ref.shape[2]
    for source, place in enumerate(order):
        out[:, place * width : (place + 1) * width] = x_ref[source, first:, :]


def unpack_text(x, order, first):
    model = x.shape[0] * x.shape[2]
    return pl.pallas_call(
        functools.partial(unpack_body, order, first),
        grid=(1,),
        in_specs=[pl.BlockSpec(x.shape, lambda n: (0, 0, 0))],
        out_specs=pl.BlockSpec((x.shape[1] - first, model), lambda n: (0, 0)),
        out_shape=jax.ShapeDtypeStruct((x.shape[1] - first, model), x.dtype),
        compiler_params=params(),
        name="unpack_text",
    )(x)


def per_device(img_qkv, txt_qkv, stale_kv, residual, gate_scale, proj_weight):
    patches, head_owners = lax.axis_size("patch"), lax.axis_size("head")
    patch = lax.axis_index("patch")
    owned_heads = stale_kv.shape[2] // HD
    pair = 2 if patches % 2 == 0 and owned_heads % 2 == 0 else 1
    planes = patches // pair
    plane, core = patch // pair, patch % pair
    width = stale_kv.shape[2] // pair
    img_rows = img_qkv.shape[0]
    text_rows = txt_qkv.shape[0] // pair
    destinations = pair * head_owners

    def column_block(d):
        return (d % head_owners) * pair + d // head_owners

    order = [column_block(d) for d in range(destinations)]
    groups = [[g * destinations + d for d in range(destinations)] for g in range(planes)]

    def exchange(x):
        return lax.all_to_all(
            x, ("patch", "head"), split_axis=0, concat_axis=0, axis_index_groups=groups, tiled=True
        )

    swap_pairs = [(p, p + 1 - 2 * (p % 2)) for p in range(patches)]
    stale = [lax.dynamic_slice_in_dim(stale_kv, core * width, width, 2)]
    if pair == 2:
        theirs = lax.dynamic_slice_in_dim(stale_kv, (1 - core) * width, width, 2)
        stale.append(lax.ppermute(theirs, "patch", swap_pairs))

    core_only = core.astype(jnp.int32).reshape(1)
    qkv = exchange(
        pack(core_only, img_qkv, txt_qkv, text_rows, destinations, column_block, width, ())
    )

    arrived = []
    from_left, from_right = stale, stale
    for step in range(1, planes):
        right_pairs = [(p, p + pair) for p in range((step - 1) * pair, patches - pair)]
        left_pairs = [(p + pair, p) for p in range(0, patches - step * pair)]
        from_left = [lax.ppermute(block, "patch", right_pairs) for block in from_left]
        from_right = [lax.ppermute(block, "patch", left_pairs) for block in from_right]
        arrived += [from_left, from_right]
    early = max(0, len(arrived) - 2)
    state = attend_most(core_only, qkv, img_rows, stale, arrived[:early])
    attended = attend_last(core_only, qkv, img_rows, state, arrived[early:])

    back = exchange(attended)
    text_out = unpack_text(back, order, img_rows)
    if pair == 2:
        other = lax.ppermute(text_out, "patch", swap_pairs)
        lower = core == 0
        text_out = jnp.concatenate(
            [jnp.where(lower, text_out, other), jnp.where(lower, other, text_out)], 0
        )
    image_out = project(back, order, proj_weight, residual, gate_scale)
    return (image_out, text_out)


def solution(mesh):
    return jax.shard_map(
        per_device,
        mesh=mesh,
        in_specs=(
            P(("patch", "head"), None),
            P("head", None),
            P(None, "patch", "head"),
            P(("patch", "head"), None),
            P(),
            P(),
        ),
        out_specs=(P(("patch", "head"), None), P("head", None)),
        check_vma=False,
    )
```
